32 devices in a mesh: probe: 4 (over z), sx: 4 (over x, core), sy: 2 (over y).
Axes of the slice: x: 2, y: 2, z: 4, core: 2. Of those that a mesh axis runs over, the one named last changes fastest.
Arguments:
- probes: float32 [8, 128, 64, 256], P('probe', 'sx', 'sy'), may hold values from -6 to 6
- velocity: float32 [3, 128, 64, 256], P(None, 'sx', 'sy'), may hold values from -0.15 to 0.15
- diffusivity: float32 [128, 64, 256], P('sx', 'sy'), may hold values from 0.02 to 0.15
- obs_weight: float32 [128, 64, 256], P('sx', 'sy'), may hold values from 0.05 to 1
Outputs:
- basis_fields: float32 [8, 128, 64, 256], P('probe', 'sx', 'sy')
- projected_hessian: float32 [8, 8], replicated
The draws below stay inside these ranges and needn't reach their ends.
All inputs are finite; a program needn't handle non-finite values.
Results may differ from the reference program's by a relative error of at most 0.00013.
Values sent between devices are 32-bit elements; how exact they have to be, the bound alone decides.
No kernel may reach another device: no remote copies, remote signals or barrier semaphores. Data moves between devices by JAX's collectives and lax.ppermute only.
A program may use at most 128 MiB of HBM per device.

```python
import math
import jax
import jax.numpy as jnp
from jax import lax

CZ = 256
STEPS = 4
PROBES = 8
NX = 128
NY = 64
NCELLS = 2097152


def block_scale(rng, extent, pieces, least, high):
    level, own = 1.0, jax.random.fold_in(rng, 6)
    for axis_at, blocks in pieces:
        steps = jnp.exp(jax.random.uniform(jax.random.fold_in(own, axis_at), (blocks,), jnp.float32, least / len(pieces), high / len(pieces)))
        level = level * jnp.repeat(steps, extent[axis_at] // blocks).reshape([-1 if axis == axis_at else 1 for axis in range(len(extent))])
    return level


def normal_values(rng, dims, scale, most, split=(), held_as=jnp.bfloat16):
    values = jax.random.normal(rng, dims, jnp.float32) * scale
    if len(split) > 0:
        values = block_scale(rng, dims, split, -0.22, 0.18) * values
    return jnp.clip(values, min=-most, max=most).astype(held_as)


def setup_inputs(seed: int = 0) -> dict:
    key_list = jax.random.split(jax.random.key(seed), 5)
    probes = normal_values(key_list[0], (PROBES, NX, NY, CZ), 1.0, 6.0, ((0, 4), (1, 4), (2, 2)), jnp.float32)
    velocity = jnp.clip(jax.random.uniform(key_list[1], (3, NX, NY, CZ), jnp.float32, -0.15, 0.15) * block_scale(key_list[1], (3, NX, NY, CZ), ((1, 4), (2, 2)), -0.4, 0.0), -0.15, 0.15)
    diffusivity = jnp.clip(jnp.exp(math.log(0.15) - 2.014903 * jax.random.uniform(key_list[2], (NX, NY, CZ), jnp.float32) ** block_scale(key_list[2], (NX, NY, CZ), ((0, 4), (1, 2)), -0.2, 0.2)), 0.02, 0.15)
    obs_weight = jnp.clip(jnp.exp(math.log(1.0) - 2.9957323 * jax.random.uniform(key_list[3], (NX, NY, CZ), jnp.float32) ** block_scale(key_list[3], (NX, NY, CZ), ((0, 4), (1, 2)), -0.2, 0.2)), 0.05, 1.0)
    return {"probes": probes, "velocity": velocity, "diffusivity": diffusivity, "obs_weight": obs_weight}


def forward_step(state, coeffs):
    cc = coeffs[:, 1:-1, 1:-1, :]
    spread = cc[0]
    inner = state[:, 1:-1, 1:-1, :]
    padded = jnp.pad(inner, ((0, 0), (0, 0), (0, 0), (1, 1)))
    result = (1.0 - 6.0 * spread) * inner
    result = result + (spread - 0.5 * cc[1]) * state[:, 2:, 1:-1, :] + (spread + 0.5 * cc[1]) * state[:, :-2, 1:-1, :]
    result = result + (spread - 0.5 * cc[2]) * state[:, 1:-1, 2:, :] + (spread + 0.5 * cc[2]) * state[:, 1:-1, :-2, :]
    result = result + (spread - 0.5 * cc[3]) * padded[..., 2:] + (spread + 0.5 * cc[3]) * padded[..., :-2]
    return result

def adjoint_step(state, coeffs):
    spread = coeffs[0]
    plus_x = (spread - 0.5 * coeffs[1]) * state
    minus_x = (spread + 0.5 * coeffs[1]) * state
    plus_y = (spread - 0.5 * coeffs[2]) * state
    minus_y = (spread + 0.5 * coeffs[2]) * state
    cc = coeffs[:, 1:-1, 1:-1, :]
    inner = state[:, 1:-1, 1:-1, :]
    pad_plus = jnp.pad((cc[0] - 0.5 * cc[3]) * inner, ((0, 0), (0, 0), (0, 0), (1, 1)))
    pad_minus = jnp.pad((cc[0] + 0.5 * cc[3]) * inner, ((0, 0), (0, 0), (0, 0), (1, 1)))
    result = (1.0 - 6.0 * cc[0]) * inner
    result = result + plus_x[:, :-2, 1:-1, :] + minus_x[:, 2:, 1:-1, :]
    result = result + plus_y[:, 1:-1, :-2, :] + minus_y[:, 1:-1, 2:, :]
    result = result + pad_plus[..., :-2] + pad_minus[..., 2:]
    return result

def reference(probes, velocity, diffusivity, obs_weight):
    coeffs = jnp.concatenate([diffusivity[None], velocity], axis=0)
    coeffs = jnp.pad(coeffs, ((0, 0), (1, 1), (1, 1), (0, 0)))
    widths = ((0, 0), (1, 1), (1, 1), (0, 0))

    def hessian(field):
        state = field[None]
        for step in range(STEPS):
            state = forward_step(jnp.pad(state, widths), coeffs)
        state = obs_weight * state
        for step in range(STEPS):
            state = adjoint_step(jnp.pad(state, widths), coeffs)
        return state[0]
    images = lax.map(hessian, probes)
    flat = images.reshape(PROBES, -1)
    gram = jnp.dot(flat, flat.T, precision=lax.Precision.HIGHEST) / NCELLS
    lower = jnp.linalg.cholesky(gram)
    inverse = jax.scipy.linalg.solve_triangular(lower, jnp.eye(PROBES, dtype=jnp.float32), lower=True)
    basis = jnp.dot(inverse, flat, precision=lax.Precision.HIGHEST)
    basis_fields = basis.reshape(images.shape)
    second = lax.map(hessian, basis_fields).reshape(PROBES, -1)
    projected = jnp.dot(basis, second.T, precision=lax.Precision.HIGHEST) / NCELLS
    return (basis_fields, projected)
```

```python
import functools

import jax
import jax.numpy as jnp
from jax import lax
from jax.experimental import pallas as pl
from jax.experimental.pallas import tpu as pltpu
from jax.sharding import PartitionSpec as P

STEPS = 4
SUB = 8
LANES = 128
VMEM_LIMIT = 58 * 1024 * 1024


def vmem_call(body, outs, scratch, ins, flops, smem_first=True):
    specs = [pl.BlockSpec(memory_space=pltpu.VMEM)] * len(ins)
    if smem_first:
        specs[0] = pl.BlockSpec(memory_space=pltpu.SMEM)
    size = sum(4 * a.size for a in list(ins) + list(outs))
    return pl.pallas_call(
        body,
        out_shape=outs,
        in_specs=specs,
        out_specs=[pl.BlockSpec(memory_space=pltpu.VMEM)] * len(outs),
        scratch_shapes=scratch,
        compiler_params=pltpu.CompilerParams(vmem_limit_bytes=VMEM_LIMIT),
        cost_estimate=pl.CostEstimate(flops=flops, bytes_accessed=size, transcendentals=0),
    )(*ins)


def f32(*shape):
    return jax.ShapeDtypeStruct(shape, jnp.float32)


def strip_shapes(fields, x, y, z, both):
    packs = [f32(fields, x // 2, SUB, z), f32(fields, 2, SUB, z), f32(fields, 2, SUB, z)]
    return [f32(fields, STEPS, y, z)] * 2 + packs * (2 if both else 1)


def write_strips(tile, field, outs, side):
    x, y, z = outs[2].shape[1] * 2, outs[0].shape[2], outs[0].shape[3]
    for i in range(STEPS):
        outs[0][field, i] = tile(i, slice(0, y))
        outs[1][field, i] = tile(x - STEPS + i, slice(0, y))
    row = lax.broadcasted_iota(jnp.int32, (SUB, z), 0)
    both = len(outs) > 5

    def packed(i):
        first_lo, second_lo = tile(2 * i, slice(0, SUB)), tile(2 * i + 1, slice(0, SUB))
        first_hi, second_hi = tile(2 * i, slice(y - SUB, y)), tile(2 * i + 1, slice(y - SUB, y))
        lo = jnp.where(row < STEPS, first_lo, pltpu.roll(second_lo, STEPS, 0))
        hi = jnp.where(row < STEPS, pltpu.roll(first_hi, STEPS, 0), second_hi)
        return [lo, hi] if both else [jnp.where(side == 0, hi, lo)]

    def step(i, carry):
        for n, value in enumerate(packed(i)):
            outs[2 + 3 * n][field, i] = value
        return carry

    lax.fori_loop(0, x // 2, step, None)
    for n in range(2 if both else 1):
        for i in range(2):
            outs[3 + 3 * n][field, i] = outs[2 + 3 * n][field, i]
            outs[4 + 3 * n][field, i] = outs[2 + 3 * n][field, x // 2 - 2 + i]


def exchange(strips):
    nx, ny = lax.axis_size("sx"), lax.axis_size("sy")
    up = [(i, i + 1) for i in range(nx - 1)]
    down = [(j, i) for i, j in up]

    def moved(value, dx, dys):
        pairs = []
        for i in range(nx):
            for j in range(ny):
                for dy in dys(j):
                    if 0 <= i + dx < nx and 0 <= j + dy < ny:
                        pairs.append((i * ny + j, (i + dx) * ny + j + dy))
        return lax.ppermute(value, ("sx", "sy"), pairs)

    below = lax.ppermute(strips[1], "sx", up)
    above = lax.ppermute(strips[0], "sx", down)
    received = [below, above]
    if len(strips) == 5:
        flip = lambda j: (1 - 2 * j,)
        pack, corner_lo, corner_hi = strips[2:]
        received += [moved(pack, 0, flip), moved(corner_hi, 1, flip), moved(corner_lo, -1, flip)]
    else:
        for n, dy in ((0, -1), (1, 1)):
            pack, corner_lo, corner_hi = strips[2 + 3 * n : 5 + 3 * n]
            one = lambda j, dy=dy: (dy,)
            received += [moved(pack, 0, one), moved(corner_hi, 1, one), moved(corner_lo, -1, one)]
    return received


def assemble(dst, tile, field, received, side):
    x, y, z = received[2].shape[1] * 2, received[0].shape[2], received[0].shape[3]

    def copy(i, carry):
        dst(i, slice(0, y), tile(i))
        return carry

    lax.fori_loop(0, x, copy, None)
    for i in range(STEPS):
        dst(x + i, slice(0, y), received[1][field, i])
        dst(x + STEPS + i, slice(0, y), received[0][field, i])
    row = lax.broadcasted_iota(jnp.int32, (SUB, z), 0)
    both = len(received) > 5

    def put(at, packs):
        if both:
            hi, lo = packs
        else:
            hi = jnp.where(side == 0, packs[0], 0.0)
            lo = jnp.where(side == 0, 0.0, packs[0])
        dst(at, slice(y, y + SUB), jnp.where(row < STEPS, hi, pltpu.roll(lo, STEPS, 0)))
        dst(at + 1, slice(y, y + SUB), jnp.where(row < STEPS, pltpu.roll(hi, STEPS, 0), lo))

    groups = [received[2:5]] + ([received[5:8]] if both else [])

    def main(i, carry):
        put(2 * i, [g[0][field, i] for g in groups])
        return carry

    lax.fori_loop(0, x // 2, main, None)
    for i in range(2):
        put(x + 2 * i, [g[2][field, i] for g in groups])
        put(x + STEPS + 2 * i, [g[1][field, i] for g in groups])


def coefficient_rows(coef):
    _, wide, rows, z = coef.shape
    lane = lax.broadcasted_iota(jnp.int32, (rows, z), 1)

    def row(i, carry):
        spread = coef[0, i]
        for d in range(3):
            half = 0.5 * coef[1 + 2 * d, i]
            plus, minus = spread - half, spread + half
            if d == 2:
                plus = jnp.where(lane == z - 1, 0.0, plus)
                minus = jnp.where(lane == 0, 0.0, minus)
            coef[1 + 2 * d, i] = plus
            coef[2 + 2 * d, i] = minus
        coef[0, i] = 1.0 - 6.0 * spread
        return carry

    lax.fori_loop(0, wide, row, None)


def sweep(coef, src, step, adjoint, tile_rows, write):
    fields, wide, rows, z = src.shape
    x = wide - 2 * STEPS
    reach = STEPS - 1 - step
    chunks, cols = rows // SUB, z // LANES
    done = tile_rows // SUB if step == STEPS - 1 else chunks
    sub = lax.broadcasted_iota(jnp.int32, (SUB, LANES), 0)
    lane = lax.broadcasted_iota(jnp.int32, (SUB, LANES), 1)
    first_row, last_row = sub == 0, sub == SUB - 1
    first_lane, last_lane = lane == 0, lane == LANES - 1

    def piece(ref, lead, xi, c, j):
        return ref[lead, xi, SUB * c : SUB * (c + 1), LANES * j : LANES * (j + 1)]

    def body(i, carry):
        wrap = lambda a: jnp.where(a < 0, a + wide, a)
        here, back, ahead = wrap(i), wrap(i - 1), wrap(i + 1)
        value, up, down = {}, {}, {}

        def state(p, c, j):
            if (p, c, j) not in value:
                value[p, c, j] = piece(src, p, here, c, j)
            return value[p, c, j]

        def shifted(p, c, j):
            key = (p, c % chunks, j)
            if key not in up:
                u = state(*key)
                if adjoint:
                    up[key] = pltpu.roll(piece(coef, 4, here, key[1], j) * u, SUB - 1, 0)
                    down[key] = pltpu.roll(piece(coef, 3, here, key[1], j) * u, 1, 0)
                else:
                    up[key] = pltpu.roll(u, SUB - 1, 0)
                    down[key] = pltpu.roll(u, 1, 0)
            return up[key], down[key]

        for c in range(done):
            for p in range(fields):
                us = [state(p, c, j) for j in range(cols)]
                if adjoint:
                    plus = [pltpu.roll(piece(coef, 6, here, c, j) * us[j], LANES - 1, 1) for j in range(cols)]
                    minus = [pltpu.roll(piece(coef, 5, here, c, j) * us[j], 1, 1) for j in range(cols)]
                else:
                    plus = [pltpu.roll(us[j], LANES - 1, 1) for j in range(cols)]
                    minus = [pltpu.roll(us[j], 1, 1) for j in range(cols)]
                for j in range(cols):
                    yp = jnp.where(last_row, shifted(p, c + 1, j)[0], shifted(p, c, j)[0])
                    ym = jnp.where(first_row, shifted(p, c - 1, j)[1], shifted(p, c, j)[1])
                    zp = jnp.where(last_lane, plus[(j + 1) % cols], plus[j])
                    zm = jnp.where(first_lane, minus[j - 1], minus[j])
                    xp, xm = piece(src, p, ahead, c, j), piece(src, p, back, c, j)
                    if adjoint:
                        xs = piece(coef, 2, ahead, c, j) * xp + piece(coef, 1, back, c, j) * xm
                        ys, zs = yp + ym, zp + zm
                    else:
                        xs = piece(coef, 1, here, c, j) * xp + piece(coef, 2, here, c, j) * xm
                        ys = piece(coef, 3, here, c, j) * yp + piece(coef, 4, here, c, j) * ym
                        zs = piece(coef, 5, here, c, j) * zp + piece(coef, 6, here, c, j) * zm
                    write(p, here, c, j, (piece(coef, 0, here, c, j) * us[j] + xs) + (ys + zs))
        return carry

    lax.fori_loop(-reach, x + reach, body, None)


def run_steps(coef, state, out, adjoint, weight=None):
    tile_rows = out.shape[2]
    for step in range(STEPS):
        src, dst = state.at[step % 2], state.at[(step + 1) % 2]

        def write(p, i, c, j, value, dst=dst, last=step == STEPS - 1):
            at = (pl.ds(SUB * c, SUB), pl.ds(LANES * j, LANES))
            if last:
                out[p, i, *at] = value if weight is None else weight[i, *at] * value
            else:
                dst[p, i, *at] = value

        sweep(coef, src, step, adjoint, tile_rows, write)


def pack_kernel(scalars, probes, velocity, diffusivity, *outs):
    side = scalars[0]
    write_strips(lambda i, r: diffusivity[i, r], 0, outs, side)
    for d in range(3):
        write_strips(lambda i, r: velocity[d, i, r], 1 + d, outs, side)
    for p in range(probes.shape[0]):
        write_strips(lambda i, r: probes[p, i, r], 4 + p, outs, side)


def first_kernel(count, scalars, probes, velocity, diffusivity, weight, *refs):
    side = scalars[0]
    received, (coef, out), strips, state = refs[:count], refs[count : count + 2], refs[count + 2 : -1], refs[-1]

    def slot(s):
        def store(i, rows, value):
            coef[s, i, rows] = value
        return store

    assemble(slot(0), lambda i: diffusivity[i], 0, received, side)
    for d in range(3):
        assemble(slot(1 + 2 * d), lambda i: velocity[d, i], 1 + d, received, side)
    coefficient_rows(coef)
    fill_state(state, probes, 4, received, side)
    run_steps(coef, state, out, False, weight)
    for p in range(out.shape[0]):
        write_strips(lambda i, r: out[p, i, r], p, strips, side)


def fill_state(state, tile, offset, received, side):
    for p in range(tile.shape[0]):
        def store(i, rows, value):
            state[0, p, i, rows] = value

        assemble(store, lambda i: tile[p, i], offset + p, received, side)


def next_kernel(count, adjoint, scalars, coef, tile, weight, *refs):
    side = scalars[0]
    received, out, strips, state = refs[:count], refs[count], refs[count + 1 : -1], refs[-1]
    fill_state(state, tile, 0, received, side)
    run_steps(coef, state, out, adjoint, None if adjoint else weight)
    if strips:
        for p in range(out.shape[0]):
            write_strips(lambda i, r: out[p, i, r], p, strips, side)


def dots_kernel(own_group, scalars, images, second, others, out):
    group, x, y, z = images.shape
    chunks, cols = y // SUB, z // LANES
    pairs = [(a, b) for a in range(group) for b in range(group) if not own_group or b <= a]

    def body(i, sums):
        sums = list(sums)
        for c in range(chunks):
            for j in range(cols):
                at = (pl.ds(SUB * c, SUB), pl.ds(LANES * j, LANES))
                other = [others[b, i, *at] for b in range(group)]
                mine = [images[a, i, *at] for a in range(group)]
                then = [second[a, i, *at] for a in range(group)]
                for n, (a, b) in enumerate(pairs):
                    sums[2 * n] = sums[2 * n] + mine[a] * other[b]
                    sums[2 * n + 1] = sums[2 * n + 1] + then[a] * other[b]
        return tuple(sums)

    zero = jnp.zeros((SUB, LANES), jnp.float32)
    sums = lax.fori_loop(0, x, body, (zero,) * (2 * len(pairs)))
    row0, col0 = scalars[1] * group, scalars[2] * group
    count = out.shape[0]
    row = lax.broadcasted_iota(jnp.int32, out.shape, 0)
    lane = lax.broadcasted_iota(jnp.int32, out.shape, 1)
    total = jnp.zeros(out.shape, jnp.float32)
    for n, (a, b) in enumerate(pairs):
        for k in range(2):
            value = jnp.sum(jnp.sum(sums[2 * n + k], axis=0, keepdims=True), axis=1, keepdims=True)
            here = (row == row0 + a) & (lane == col0 + b + k * count) & (scalars[2] >= 0)
            total = total + jnp.where(here, value, 0.0)
    out[...] = total


def basis_kernel(inverse, *refs):
    images, out = refs[:-1], refs[-1]
    group, x, y, z = out.shape
    chunks, cols = y // SUB, z // LANES

    def body(i, carry):
        for c in range(chunks):
            for j in range(cols):
                at = (pl.ds(SUB * c, SUB), pl.ds(LANES * j, LANES))
                sums = [None] * group
                for s, image in enumerate(images):
                    for b in range(group):
                        value = image[b, i, *at]
                        for a in range(group):
                            term = inverse[a, s * group + b] * value
                            sums[a] = term if sums[a] is None else sums[a] + term
                for a in range(group):
                    out[a, i, *at] = sums[a]
        return carry

    lax.fori_loop(0, x, body, None)


def all_sum(value):
    for axis in ("sx", "sy", "probe"):
        devices = lax.axis_size(axis)
        if devices & (devices - 1):
            value = lax.psum(value, axis)
            continue
        bit = 1
        while bit < devices:
            value = value + lax.ppermute(value, axis, [(i, i ^ bit) for i in range(devices)])
            bit *= 2
    return value


def shards(probes, velocity, diffusivity, obs_weight):
    group, x, y, z = probes.shape
    groups = lax.axis_size("probe")
    count = group * groups
    ncells = x * y * z * lax.axis_size("sx") * lax.axis_size("sy")
    both = lax.axis_size("sy") != 2
    side, mine = lax.axis_index("sy"), lax.axis_index("probe")
    cells = group * x * y * z

    def scalars(other):
        return jnp.stack([side, mine, mine - other]).astype(jnp.int32)

    where = scalars(0)
    wide = (x + 2 * STEPS, y + 2 * STEPS, z)
    state = [pltpu.VMEM((2, group) + wide, jnp.float32)]
    tile = f32(group, x, y, z)
    strips2 = strip_shapes(group, x, y, z, both)

    strips = vmem_call(pack_kernel, strip_shapes(4 + group, x, y, z, both), [], [where, probes, velocity, diffusivity], cells)
    received = exchange(strips)
    coef, halfway, *strips = vmem_call(
        functools.partial(first_kernel, len(received)),
        [f32(7, *wide), tile] + strips2,
        state,
        [where, probes, velocity, diffusivity, obs_weight] + received,
        100 * cells,
    )

    def model(field, strips, adjoint, last=False):
        received = exchange(strips)
        return vmem_call(
            functools.partial(next_kernel, len(received), adjoint),
            [tile] + ([] if last else strips2),
            state,
            [where, coef, field, obs_weight] + received,
            70 * cells,
        )

    images, *strips = model(halfway, strips, True)

    right = [(i, i + 1) for i in range(groups - 1)]
    passed = [images]
    for _ in range(groups - 1):
        passed.append(lax.ppermute(passed[-1], "probe", right))

    halfway, *strips = model(images, strips, False)
    (second,) = model(halfway, strips, True, True)

    partial = None
    for n, others in enumerate(passed):
        (part,) = vmem_call(
            functools.partial(dots_kernel, n == 0),
            [f32(count, LANES)],
            [],
            [scalars(n), images, second, others],
            4 * cells,
        )
        partial = part if partial is None else partial + part
    total = all_sum(partial) / ncells
    strict = jnp.tril(jnp.ones((count, count), jnp.float32), -1)
    gram, ritz = total[:, :count], total[:, count : 2 * count]
    gram = gram + (gram * strict).T
    ritz = ritz + (ritz * strict).T
    lower = jnp.linalg.cholesky(gram)
    inverse = jax.scipy.linalg.solve_triangular(lower, jnp.eye(count, dtype=jnp.float32), lower=True)
    highest = lax.Precision.HIGHEST
    projected = jnp.dot(jnp.dot(inverse, ritz, precision=highest), inverse.T, precision=highest)

    rows = lax.dynamic_slice_in_dim(inverse, mine * group, group, 0)
    parts = []
    for n in range(groups):
        part = lax.dynamic_slice_in_dim(rows, jnp.maximum(mine - n, 0) * group, group, 1)
        parts.append(jnp.where(mine >= n, part, 0.0))
    (basis,) = vmem_call(basis_kernel, [tile], [], [jnp.concatenate(parts, 1)] + passed, 2 * count * cells)
    return (basis, projected)


def solution(mesh):
    return jax.shard_map(
        shards,
        mesh=mesh,
        in_specs=(
            P("probe", "sx", "sy", None),
            P(None, "sx", "sy", None),
            P("sx", "sy", None),
            P("sx", "sy", None),
        ),
        out_specs=(P("probe", "sx", "sy", None), P()),
        check_vma=False,
    )
```

```python
import functools

import jax
import jax.numpy as jnp
from jax import lax
from jax.experimental import pallas as pl
from jax.experimental.pallas import tpu as pltpu
from jax.sharding import PartitionSpec as P

STEPS = 4
SUB = 8
LANES = 128
VMEM_LIMIT = 58 * 1024 * 1024
FLOPS_PER_MICRO = 1.15e9
BYTES_PER_MICRO = 3.6e6


def kernel_call(body, outs, scratch, ins, micros, anywhere=(), outs_anywhere=()):
    spec = lambda n, names: pl.BlockSpec(memory_space=pl.ANY if n in names else pltpu.VMEM)
    specs = [spec(n, anywhere) for n in range(len(ins))]
    specs[0] = pl.BlockSpec(memory_space=pltpu.SMEM)
    return pl.pallas_call(
        body,
        out_shape=outs,
        in_specs=specs,
        out_specs=[spec(n, outs_anywhere) for n in range(len(outs))],
        scratch_shapes=scratch,
        compiler_params=pltpu.CompilerParams(vmem_limit_bytes=VMEM_LIMIT),
        cost_estimate=pl.CostEstimate(
            flops=int(micros * FLOPS_PER_MICRO),
            bytes_accessed=int(micros * BYTES_PER_MICRO),
            transcendentals=0,
        ),
    )(*ins)


def f32(*shape):
    return jax.ShapeDtypeStruct(shape, jnp.float32)


def strip_shapes(fields, x, y, z, both):
    packs = [f32(fields, x // 2, SUB, z), f32(fields, 2, SUB, z), f32(fields, 2, SUB, z)]
    return [f32(fields, STEPS, y, z)] * 2 + packs * (2 if both else 1)


def pack_starts(packs, y, side):
    if packs == 2:
        return [(0, False), (y - SUB, True)]
    return [(pl.multiple_of(jnp.where(side == 0, y - SUB, 0), SUB), side == 0)]


def packed_pair(row, first, second, last):
    hi = lambda: jnp.where(row < STEPS, pltpu.roll(first, STEPS, 0), second)
    lo = lambda: jnp.where(row < STEPS, first, pltpu.roll(second, STEPS, 0))
    if isinstance(last, bool):
        return hi() if last else lo()
    return jnp.where(last, hi(), lo())


def write_packs(field, n, rows, last, outs):
    pack, corner_lo, corner_hi = outs[2 + 3 * n : 5 + 3 * n]
    half, z = pack.shape[1], pack.shape[3]
    row = lax.broadcasted_iota(jnp.int32, (SUB, z), 0)

    def step(i, carry):
        pack[field, i] = packed_pair(row, rows(2 * i), rows(2 * i + 1), last)
        return carry

    lax.fori_loop(0, half, step, None, unroll=4)
    for i in range(2):
        corner_lo[field, i] = pack[field, i]
        corner_hi[field, i] = pack[field, half - 2 + i]


def write_strips(tile, outs, side):
    fields, x, y, _ = tile.shape
    for p in range(fields):
        for i in range(STEPS):
            outs[0][p, i] = tile[p, i]
            outs[1][p, i] = tile[p, x - STEPS + i]
        for n, (start, last) in enumerate(pack_starts((len(outs) - 2) // 3, y, side)):
            write_packs(p, n, lambda i: tile[p, i, pl.ds(start, SUB)], last, outs)


def exchange(strips):
    nx, ny = lax.axis_size("sx"), lax.axis_size("sy")
    up = [(i, i + 1) for i in range(nx - 1)]
    down = [(j, i) for i, j in up]

    def moved(value, dx, dys):
        pairs = []
        for i in range(nx):
            for j in range(ny):
                for dy in dys(j):
                    if 0 <= i + dx < nx and 0 <= j + dy < ny:
                        pairs.append((i * ny + j, (i + dx) * ny + j + dy))
        return lax.ppermute(value, ("sx", "sy"), pairs)

    below = lax.ppermute(strips[1], "sx", up)
    above = lax.ppermute(strips[0], "sx", down)
    received = [below, above]
    if len(strips) == 5:
        flip = lambda j: (1 - 2 * j,)
        pack, corner_lo, corner_hi = strips[2:]
        received += [moved(pack, 0, flip), moved(corner_hi, 1, flip), moved(corner_lo, -1, flip)]
    else:
        for n, dy in ((0, -1), (1, 1)):
            pack, corner_lo, corner_hi = strips[2 + 3 * n : 5 + 3 * n]
            one = lambda j, dy=dy: (dy,)
            received += [moved(pack, 0, one), moved(corner_hi, 1, one), moved(corner_lo, -1, one)]
    return received


class Copies:
    def __init__(self, sems):
        self.sems, self.open, self.used = sems, [], 0

    def start(self, src, dst):
        copy = pltpu.make_async_copy(src, dst, self.sems.at[self.used])
        self.used += 1
        copy.start()
        self.open.append(copy)
        return copy

    def wait(self):
        for copy in self.open:
            copy.wait()
        self.open = []


def start_widening(copies, dst, tile, field, received):
    x, y = tile.shape[0], tile.shape[1]
    copies.start(tile, dst.at[pl.ds(0, x), pl.ds(0, y)])
    copies.start(received[1].at[field], dst.at[pl.ds(x, STEPS), pl.ds(0, y)])
    copies.start(received[0].at[field], dst.at[pl.ds(x + STEPS, STEPS), pl.ds(0, y)])


def widen_rows(dst, field, received, side):
    half, z = received[2].shape[1], received[2].shape[3]
    x, y = 2 * half, dst.shape[1] - SUB
    row = lax.broadcasted_iota(jnp.int32, (SUB, z), 0)
    both = len(received) > 5

    def put(at, packs):
        if both:
            hi, lo = packs
        else:
            hi = jnp.where(side == 0, packs[0], 0.0)
            lo = jnp.where(side == 0, 0.0, packs[0])
        dst[at, y : y + SUB] = jnp.where(row < STEPS, hi, pltpu.roll(lo, STEPS, 0))
        dst[at + 1, y : y + SUB] = jnp.where(row < STEPS, pltpu.roll(hi, STEPS, 0), lo)

    groups = [received[2:5]] + ([received[5:8]] if both else [])

    def main(i, carry):
        put(2 * i, [g[0][field, i] for g in groups])
        return carry

    lax.fori_loop(0, half, main, None, unroll=4)
    for i in range(2):
        put(x + 2 * i, [g[2][field, i] for g in groups])
        put(x + STEPS + 2 * i, [g[1][field, i] for g in groups])


def coefficient_rows(coef):
    _, wide, rows, z = coef.shape
    lane = lax.broadcasted_iota(jnp.int32, (SUB, z), 1)

    def row(i, carry):
        for c in range(rows // SUB):
            at = pl.ds(SUB * c, SUB)
            spread = coef[0, i, at]
            values = [1.0 - 6.0 * spread]
            for d in range(3):
                half = 0.5 * coef[1 + 2 * d, i, at]
                plus, minus = spread - half, spread + half
                if d == 2:
                    plus = jnp.where(lane == z - 1, 0.0, plus)
                    minus = jnp.where(lane == 0, 0.0, minus)
                values += [plus, minus]
            for s, value in enumerate(values):
                coef[s, i, at] = value
        return carry

    lax.fori_loop(0, wide, row, None)


def sweep(coef, src, first, stop, adjoint, done, write):
    fields, wide, rows, z = src.shape
    chunks, cols = rows // SUB, z // LANES
    sub = lax.broadcasted_iota(jnp.int32, (SUB, LANES), 0)
    lane = lax.broadcasted_iota(jnp.int32, (SUB, LANES), 1)
    first_row, last_row = sub == 0, sub == SUB - 1
    first_lane, last_lane = lane == 0, lane == LANES - 1

    def piece(ref, lead, xi, c, j):
        return ref[lead, xi, SUB * c : SUB * (c + 1), LANES * j : LANES * (j + 1)]

    def body(i, carry):
        wrap = lambda a: jnp.where(a < 0, a + wide, a)
        here, back, ahead = wrap(i), wrap(i - 1), wrap(i + 1)
        value, up, down = {}, {}, {}

        def state(p, c, j):
            if (p, c, j) not in value:
                value[p, c, j] = piece(src, p, here, c, j)
            return value[p, c, j]

        def turned(kept, slot, shift, p, c, j):
            key = (p, c % chunks, j)
            if key not in kept:
                u = state(*key)
                if adjoint:
                    u = piece(coef, slot, here, key[1], j) * u
                kept[key] = pltpu.roll(u, shift, 0)
            return kept[key]

        for c in range(done):
            results = []
            plus, minus = {}, {}
            for j in range(cols):
                for p in range(fields):
                    u = state(p, c, j)
                    a, b = (piece(coef, 6, here, c, j) * u, piece(coef, 5, here, c, j) * u) if adjoint else (u, u)
                    plus[p, j], minus[p, j] = pltpu.roll(a, LANES - 1, 1), pltpu.roll(b, 1, 1)
            for j in range(cols):
                middle = piece(coef, 0, here, c, j)
                if adjoint:
                    cxp, cxm = piece(coef, 2, ahead, c, j), piece(coef, 1, back, c, j)
                else:
                    cxp, cxm = piece(coef, 1, here, c, j), piece(coef, 2, here, c, j)
                    cyp, cym = piece(coef, 3, here, c, j), piece(coef, 4, here, c, j)
                    czp, czm = piece(coef, 5, here, c, j), piece(coef, 6, here, c, j)
                for p in range(fields):
                    yp = jnp.where(last_row, turned(up, 4, SUB - 1, p, c + 1, j), turned(up, 4, SUB - 1, p, c, j))
                    ym = jnp.where(first_row, turned(down, 3, 1, p, c - 1, j), turned(down, 3, 1, p, c, j))
                    zp = jnp.where(last_lane, plus[p, (j + 1) % cols], plus[p, j])
                    zm = jnp.where(first_lane, minus[p, (j - 1) % cols], minus[p, j])
                    xs = cxp * piece(src, p, ahead, c, j) + cxm * piece(src, p, back, c, j)
                    ys, zs = (yp + ym, zp + zm) if adjoint else (cyp * yp + cym * ym, czp * zp + czm * zm)
                    results.append((p, here, c, j, (middle * state(p, c, j) + xs) + (ys + zs)))
            for result in results:
                write(*result)
        return carry

    lax.fori_loop(first, stop, body, None)


def run_steps(coef, states, out, adjoint, weight=None, parts=None):
    x, tile_rows = out.shape[1], out.shape[2]
    for step in range(STEPS):
        src, dst = states[step % 2], states[(step + 1) % 2]
        last = step == STEPS - 1

        def write(p, i, c, j, value):
            at = (pl.ds(SUB * c, SUB), pl.ds(LANES * j, LANES))
            if last:
                out[p, i, *at] = value if weight is None else weight[i, *at] * value
            else:
                dst[p, i, *at] = value

        done = (tile_rows if last else src.shape[2]) // SUB
        reach = STEPS - 1 - step
        bounds = [-reach, x + reach]
        if step == 0 and parts is not None:
            bounds[1:1] = [SUB * (n + 1) - 1 for n in range(len(parts) - 1)]
        for n in range(len(bounds) - 1):
            if step == 0 and parts is not None:
                parts[n]()
            sweep(coef, src, bounds[n], bounds[n + 1], adjoint, done, write)


def pack_kernel(fields_in, scalars, *refs):
    sources, outs, (buffers, sems) = refs[:fields_in], refs[fields_in:-2], refs[-2:]
    side = scalars[0]
    tiles = [ref.at[n] for ref in sources for n in range(ref.shape[0])]
    x, y, _ = tiles[0].shape
    starts = pack_starts((len(outs) - 2) // 3, y, side)
    copies = Copies(sems)
    for f, tile in enumerate(tiles):
        for n, (start, _) in enumerate(starts):
            copies.start(tile.at[:, pl.ds(start, SUB)], buffers.at[n, f])
    loads, copies.open = copies.open, []
    for f, tile in enumerate(tiles):
        copies.start(tile.at[pl.ds(0, STEPS)], outs[0].at[f])
        copies.start(tile.at[pl.ds(x - STEPS, STEPS)], outs[1].at[f])
    for f in range(len(tiles)):
        for n, (_, last) in enumerate(starts):
            loads[f * len(starts) + n].wait()
            write_packs(f, n, lambda i: buffers[n, f, i], last, outs)
    copies.wait()


def first_kernel(count, scalars, diffusivity, velocity, probes, weight, *refs):
    side = scalars[0]
    received, coef_out, out = refs[:count], refs[count], refs[count + 1]
    strips, (coef, state, other, sems) = refs[count + 2 : -4], refs[-4:]
    copies = Copies(sems)
    tiles = [diffusivity.at[0]] + [velocity.at[d] for d in range(3)]
    slots = [coef.at[s] for s in (0, 1, 3, 5)]
    for p in range(probes.shape[0]):
        tiles.append(probes.at[p])
        slots.append(state.at[p])
    for f, (tile, slot) in enumerate(zip(tiles, slots)):
        start_widening(copies, slot, tile, f, received)
    for f, slot in enumerate(slots):
        widen_rows(slot, f, received, side)
    copies.wait()
    coefficient_rows(coef)
    copies.start(coef, coef_out)
    run_steps(coef, (state, other), out, False, weight)
    write_strips(out, strips, side)
    copies.wait()


def next_kernel(count, adjoint, scalars, coef_in, tile, *refs):
    side = scalars[0]
    weight = None if adjoint else refs[0]
    refs = refs if adjoint else refs[1:]
    received, out = refs[:count], refs[count]
    strips, (coef, state, other, sems) = refs[count + 1 : -4], refs[-4:]
    fields, x = tile.shape[0], tile.shape[1]
    copies = Copies(sems)
    for p in range(fields):
        start_widening(copies, state.at[p], tile.at[p], p, received)
    ends = Copies(sems.at[pl.ds(3 * fields, x // SUB + 1)])
    rows = [(x, 2 * STEPS)] + [(n, SUB) for n in range(0, x, SUB)]
    waits = []
    for at, size in rows:
        part = (slice(None), pl.ds(at, size))
        waits.append(ends.start(coef_in.at[part], coef.at[part]).wait)
    for p in range(fields):
        widen_rows(state.at[p], p, received, side)
    copies.wait()
    waits[0]()
    run_steps(coef, (state, other), out, adjoint, weight, waits[1:])
    if strips:
        write_strips(out, strips, side)


def dots_kernel(own_group, scalars, images, second, others, out):
    group, x, y, z = images.shape
    chunks, cols = y // SUB, z // LANES
    pairs = [(a, b) for a in range(group) for b in range(group) if not own_group or b <= a]

    def body(i, sums):
        sums = list(sums)
        for c in range(chunks):
            for j in range(cols):
                at = (pl.ds(SUB * c, SUB), pl.ds(LANES * j, LANES))
                other = [others[b, i, *at] for b in range(group)]
                mine = [images[a, i, *at] for a in range(group)]
                then = [second[a, i, *at] for a in range(group)]
                for n, (a, b) in enumerate(pairs):
                    sums[2 * n] = sums[2 * n] + mine[a] * other[b]
                    sums[2 * n + 1] = sums[2 * n + 1] + then[a] * other[b]
        return tuple(sums)

    zero = jnp.zeros((SUB, LANES), jnp.float32)
    sums = lax.fori_loop(0, x, body, (zero,) * (2 * len(pairs)))
    row0, col0 = scalars[1] * group, scalars[2] * group
    count = out.shape[0]
    row = lax.broadcasted_iota(jnp.int32, out.shape, 0)
    lane = lax.broadcasted_iota(jnp.int32, out.shape, 1)
    total = jnp.zeros(out.shape, jnp.float32)
    for n, (a, b) in enumerate(pairs):
        for k in range(2):
            value = jnp.sum(jnp.sum(sums[2 * n + k], axis=0, keepdims=True), axis=1, keepdims=True)
            here = (row == row0 + a) & (lane == col0 + b + k * count) & (scalars[2] >= 0)
            total = total + jnp.where(here, value, 0.0)
    out[...] = total


def basis_kernel(inverse, *refs):
    images, out = refs[:-1], refs[-1]
    group, x, y, z = out.shape
    chunks, cols = y // SUB, z // LANES

    def body(i, carry):
        for c in range(chunks):
            for j in range(cols):
                at = (pl.ds(SUB * c, SUB), pl.ds(LANES * j, LANES))
                sums = [None] * group
                for s, image in enumerate(images):
                    for b in range(group):
                        value = image[b, i, *at]
                        for a in range(group):
                            term = inverse[a, s * group + b] * value
                            sums[a] = term if sums[a] is None else sums[a] + term
                for a in range(group):
                    out[a, i, *at] = sums[a]
        return carry

    lax.fori_loop(0, x, body, None)


def all_sum(value):
    for axis in ("sx", "sy", "probe"):
        devices = lax.axis_size(axis)
        if devices & (devices - 1):
            value = lax.psum(value, axis)
            continue
        bit = 1
        while bit < devices:
            value = value + lax.ppermute(value, axis, [(i, i ^ bit) for i in range(devices)])
            bit *= 2
    return value


def shards(probes, velocity, diffusivity, obs_weight):
    group, x, y, z = probes.shape
    groups = lax.axis_size("probe")
    count = group * groups
    ncells = x * y * z * lax.axis_size("sx") * lax.axis_size("sy")
    both = lax.axis_size("sy") != 2
    side, mine = lax.axis_index("sy"), lax.axis_index("probe")

    def scalars(other):
        return jnp.stack([side, mine, mine - other]).astype(jnp.int32)

    where = scalars(0)
    wide = (x + 2 * STEPS, y + 2 * STEPS, z)
    tile = f32(group, x, y, z)
    strips2 = strip_shapes(group, x, y, z, both)
    fields = [diffusivity[None], velocity, probes]
    total = 4 + group

    def scratch(copies):
        return [
            pltpu.VMEM((7,) + wide, jnp.float32),
            pltpu.VMEM((group,) + wide, jnp.float32),
            pltpu.VMEM((group,) + wide, jnp.float32),
            pltpu.SemaphoreType.DMA((copies,)),
        ]

    packs = 2 if both else 1
    strips = kernel_call(
        functools.partial(pack_kernel, len(fields)),
        strip_shapes(total, x, y, z, both),
        [pltpu.VMEM((packs, total, x, SUB, z), jnp.float32), pltpu.SemaphoreType.DMA((total * (packs + 2),))],
        [where] + fields,
        3.0,
        anywhere=(1, 2, 3),
        outs_anywhere=(0, 1),
    )
    received = exchange(strips)
    coef, halfway, *strips = kernel_call(
        functools.partial(first_kernel, len(received)),
        [f32(7, *wide), tile] + strips2,
        scratch(3 * total + 1),
        [where] + fields + [obs_weight] + received,
        14.0,
        anywhere=(1, 2, 3, 5, 6),
        outs_anywhere=(0,),
    )

    def model(field, strips, adjoint, last=False):
        received = exchange(strips)
        ins = [where, coef, field] + ([] if adjoint else [obs_weight])
        return kernel_call(
            functools.partial(next_kernel, len(received), adjoint),
            [tile] + ([] if last else strips2),
            scratch(3 * group + x // SUB + 1),
            ins + received,
            12.0,
            anywhere=(1, 2, len(ins), len(ins) + 1),
        )

    images, *strips = model(halfway, strips, True)

    right = [(i, i + 1) for i in range(groups - 1)]
    passed = [images]
    for _ in range(groups - 1):
        passed.append(lax.ppermute(passed[-1], "probe", right))

    halfway, *strips = model(images, strips, False)
    (second,) = model(halfway, strips, True, True)

    partial = None
    for n, others in enumerate(passed):
        (part,) = kernel_call(
            functools.partial(dots_kernel, n == 0),
            [f32(count, LANES)],
            [],
            [scalars(n), images, second, others],
            4.0,
        )
        partial = part if partial is None else partial + part
    inner = all_sum(partial) / ncells
    strict = jnp.tril(jnp.ones((count, count), jnp.float32), -1)
    gram, ritz = inner[:, :count], inner[:, count : 2 * count]
    gram = gram + (gram * strict).T
    ritz = ritz + (ritz * strict).T
    lower = jnp.linalg.cholesky(gram)
    inverse = jax.scipy.linalg.solve_triangular(lower, jnp.eye(count, dtype=jnp.float32), lower=True)
    highest = lax.Precision.HIGHEST
    projected = jnp.dot(jnp.dot(inverse, ritz, precision=highest), inverse.T, precision=highest)

    rows = lax.dynamic_slice_in_dim(inverse, mine * group, group, 0)
    parts = []
    for n in range(groups):
        part = lax.dynamic_slice_in_dim(rows, jnp.maximum(mine - n, 0) * group, group, 1)
        parts.append(jnp.where(mine >= n, part, 0.0))
    (basis,) = kernel_call(basis_kernel, [tile], [], [jnp.concatenate(parts, 1)] + passed, 6.0)
    return (basis, projected)


def solution(mesh):
    return jax.shard_map(
        shards,
        mesh=mesh,
        in_specs=(
            P("probe", "sx", "sy", None),
            P(None, "sx", "sy", None),
            P("sx", "sy", None),
            P("sx", "sy", None),
        ),
        out_specs=(P("probe", "sx", "sy", None), P()),
        check_vma=False,
    )
```

```python
import functools

import jax
import jax.numpy as jnp
from jax import lax
from jax.experimental import pallas as pl
from jax.experimental.pallas import tpu as pltpu
from jax.sharding import PartitionSpec as P

STEPS = 4
SUB = 8
LANES = 128
ROWS = 2
VMEM_LIMIT = 58 * 1024 * 1024
FLOPS_PER_MICRO = 1.15e9
BYTES_PER_MICRO = 3.6e6


def kernel_call(body, outs, scratch, ins, micros, anywhere=(), outs_anywhere=()):
    spec = lambda n, names: pl.BlockSpec(memory_space=pl.ANY if n in names else pltpu.VMEM)
    specs = [spec(n, anywhere) for n in range(len(ins))]
    specs[0] = pl.BlockSpec(memory_space=pltpu.SMEM)
    return pl.pallas_call(
        body,
        out_shape=outs,
        in_specs=specs,
        out_specs=[spec(n, outs_anywhere) for n in range(len(outs))],
        scratch_shapes=scratch,
        compiler_params=pltpu.CompilerParams(vmem_limit_bytes=VMEM_LIMIT),
        cost_estimate=pl.CostEstimate(
            flops=int(micros * FLOPS_PER_MICRO),
            bytes_accessed=int(micros * BYTES_PER_MICRO),
            transcendentals=0,
        ),
    )(*ins)


def f32(*shape):
    return jax.ShapeDtypeStruct(shape, jnp.float32)


def strip_shapes(fields, x, y, z, both):
    packs = [f32(fields, x // 2, SUB, z), f32(fields, 2, SUB, z), f32(fields, 2, SUB, z)]
    return [f32(fields, STEPS, y, z)] * 2 + packs * (2 if both else 1)


def pack_starts(packs, y, side):
    if packs == 2:
        return [(0, False), (y - SUB, True)]
    return [(pl.multiple_of(jnp.where(side == 0, y - SUB, 0), SUB), side == 0)]


def packed_pair(row, first, second, last):
    hi = lambda: jnp.where(row < STEPS, pltpu.roll(first, STEPS, 0), second)
    lo = lambda: jnp.where(row < STEPS, first, pltpu.roll(second, STEPS, 0))
    if isinstance(last, bool):
        return hi() if last else lo()
    return jnp.where(last, hi(), lo())


def write_packs(field, n, rows, last, outs):
    pack, corner_lo, corner_hi = outs[2 + 3 * n : 5 + 3 * n]
    half, z = pack.shape[1], pack.shape[3]
    row = lax.broadcasted_iota(jnp.int32, (SUB, z), 0)

    def step(i, carry):
        pack[field, i] = packed_pair(row, rows(2 * i), rows(2 * i + 1), last)
        return carry

    lax.fori_loop(0, half, step, None, unroll=4)
    for i in range(2):
        corner_lo[field, i] = pack[field, i]
        corner_hi[field, i] = pack[field, half - 2 + i]


def write_strips(tile, outs, side):
    fields, x, y, _ = tile.shape
    for p in range(fields):
        for i in range(STEPS):
            outs[0][p, i] = tile[p, i]
            outs[1][p, i] = tile[p, x - STEPS + i]
        for n, (start, last) in enumerate(pack_starts((len(outs) - 2) // 3, y, side)):
            write_packs(p, n, lambda i: tile[p, i, pl.ds(start, SUB)], last, outs)


def exchange(strips):
    nx, ny = lax.axis_size("sx"), lax.axis_size("sy")
    up = [(i, i + 1) for i in range(nx - 1)]
    down = [(j, i) for i, j in up]

    def moved(value, dx, dys):
        pairs = []
        for i in range(nx):
            for j in range(ny):
                for dy in dys(j):
                    if 0 <= i + dx < nx and 0 <= j + dy < ny:
                        pairs.append((i * ny + j, (i + dx) * ny + j + dy))
        return lax.ppermute(value, ("sx", "sy"), pairs)

    below = lax.ppermute(strips[1], "sx", up)
    above = lax.ppermute(strips[0], "sx", down)
    received = [below, above]
    if len(strips) == 5:
        flip = lambda j: (1 - 2 * j,)
        pack, corner_lo, corner_hi = strips[2:]
        received += [moved(pack, 0, flip), moved(corner_hi, 1, flip), moved(corner_lo, -1, flip)]
    else:
        for n, dy in ((0, -1), (1, 1)):
            pack, corner_lo, corner_hi = strips[2 + 3 * n : 5 + 3 * n]
            one = lambda j, dy=dy: (dy,)
            received += [moved(pack, 0, one), moved(corner_hi, 1, one), moved(corner_lo, -1, one)]
    return received


class Copies:
    def __init__(self, sems):
        self.sems, self.open, self.used = sems, [], 0

    def start(self, src, dst):
        copy = pltpu.make_async_copy(src, dst, self.sems.at[self.used])
        self.used += 1
        copy.start()
        self.open.append(copy)
        return copy

    def wait(self):
        for copy in self.open:
            copy.wait()
        self.open = []


def start_widening(copies, dst, tile, field, received):
    x, y = tile.shape[0], tile.shape[1]
    copies.start(tile, dst.at[pl.ds(0, x), pl.ds(0, y)])
    copies.start(received[1].at[field], dst.at[pl.ds(x, STEPS), pl.ds(0, y)])
    copies.start(received[0].at[field], dst.at[pl.ds(x + STEPS, STEPS), pl.ds(0, y)])


def widen_rows(dst, field, received, side):
    half, z = received[2].shape[1], received[2].shape[3]
    x, y = 2 * half, dst.shape[1] - SUB
    row = lax.broadcasted_iota(jnp.int32, (SUB, z), 0)
    both = len(received) > 5

    def put(at, packs):
        if both:
            hi, lo = packs
        else:
            hi = jnp.where(side == 0, packs[0], 0.0)
            lo = jnp.where(side == 0, 0.0, packs[0])
        dst[at, y : y + SUB] = jnp.where(row < STEPS, hi, pltpu.roll(lo, STEPS, 0))
        dst[at + 1, y : y + SUB] = jnp.where(row < STEPS, pltpu.roll(hi, STEPS, 0), lo)

    groups = [received[2:5]] + ([received[5:8]] if both else [])

    def main(i, carry):
        put(2 * i, [g[0][field, i] for g in groups])
        return carry

    lax.fori_loop(0, half, main, None, unroll=4)
    for i in range(2):
        put(x + 2 * i, [g[2][field, i] for g in groups])
        put(x + STEPS + 2 * i, [g[1][field, i] for g in groups])


def coefficient_rows(coef):
    _, wide, rows, z = coef.shape
    lane = lax.broadcasted_iota(jnp.int32, (SUB, z), 1)

    def row(i, carry):
        for c in range(rows // SUB):
            at = pl.ds(SUB * c, SUB)
            spread = coef[0, i, at]
            values = [1.0 - 6.0 * spread]
            for d in range(3):
                half = 0.5 * coef[1 + 2 * d, i, at]
                plus, minus = spread - half, spread + half
                if d == 2:
                    plus = jnp.where(lane == z - 1, 0.0, plus)
                    minus = jnp.where(lane == 0, 0.0, minus)
                values += [plus, minus]
            for s, value in enumerate(values):
                coef[s, i, at] = value
        return carry

    lax.fori_loop(0, wide, row, None)


def sweep(coef, src, first, stop, adjoint, done, write):
    fields, wide, rows, z = src.shape
    chunks, cols = rows // SUB, z // LANES
    sub = lax.broadcasted_iota(jnp.int32, (SUB, LANES), 0)
    lane = lax.broadcasted_iota(jnp.int32, (SUB, LANES), 1)
    first_row, last_row = sub == 0, sub == SUB - 1
    first_lane, last_lane = lane == 0, lane == LANES - 1

    def piece(ref, lead, xi, c, j):
        return ref[lead, xi, SUB * c : SUB * (c + 1), LANES * j : LANES * (j + 1)]

    def body(pair, carry):
        wrap = lambda a: jnp.where(a < 0, a + wide, a)
        base = first + ROWS * pair
        at = [wrap(base + d) for d in range(-1, ROWS + 1)]
        kept = {}

        def load(ref, lead, r, c, j):
            key = (ref is coef, lead, r, c % chunks, j)
            if key not in kept:
                kept[key] = piece(ref, lead, at[r + 1], c % chunks, j)
            return kept[key]

        def scaled(slot, p, r, c, j):
            u = load(src, p, r, c, j)
            return load(coef, slot, r, c, j) * u if adjoint else u

        def turned(slot, shift, p, r, c, j):
            key = ("turned", slot, p, r, c % chunks, j)
            if key not in kept:
                kept[key] = pltpu.roll(scaled(slot, p, r, c, j), shift, 0)
            return kept[key]

        for c in range(done):
            results = []
            for r in range(ROWS):
                plus, minus = {}, {}
                for j in range(cols):
                    for p in range(fields):
                        plus[p, j] = pltpu.roll(scaled(6, p, r, c, j), LANES - 1, 1)
                        minus[p, j] = pltpu.roll(scaled(5, p, r, c, j), 1, 1)
                for j in range(cols):
                    for p in range(fields):
                        u, xp, xm = (load(src, p, r + d, c, j) for d in (0, 1, -1))
                        yp = jnp.where(last_row, turned(4, SUB - 1, p, r, c + 1, j), turned(4, SUB - 1, p, r, c, j))
                        ym = jnp.where(first_row, turned(3, 1, p, r, c - 1, j), turned(3, 1, p, r, c, j))
                        zp = jnp.where(last_lane, plus[p, (j + 1) % cols], plus[p, j])
                        zm = jnp.where(first_lane, minus[p, (j - 1) % cols], minus[p, j])
                        if adjoint:
                            xs = load(coef, 2, r + 1, c, j) * xp + load(coef, 1, r - 1, c, j) * xm
                            ys, zs = yp + ym, zp + zm
                        else:
                            xs = load(coef, 1, r, c, j) * xp + load(coef, 2, r, c, j) * xm
                            ys = load(coef, 3, r, c, j) * yp + load(coef, 4, r, c, j) * ym
                            zs = load(coef, 5, r, c, j) * zp + load(coef, 6, r, c, j) * zm
                        value = (load(coef, 0, r, c, j) * u + xs) + (ys + zs)
                        results.append((p, at[r + 1], c, j, value))
            for result in results:
                write(*result)
        return carry

    lax.fori_loop(0, (stop - first) // ROWS, body, None)


def run_steps(coef, states, out, adjoint, weight=None, parts=None):
    x, tile_rows = out.shape[1], out.shape[2]
    for step in range(STEPS):
        src, dst = states[step % 2], states[(step + 1) % 2]
        last = step == STEPS - 1

        def write(p, i, c, j, value):
            at = (pl.ds(SUB * c, SUB), pl.ds(LANES * j, LANES))
            if last:
                out[p, i, *at] = value if weight is None else weight[i, *at] * value
            else:
                dst[p, i, *at] = value

        done = (tile_rows if last else src.shape[2]) // SUB
        reach = STEPS - 1 - step
        bounds = [-reach, x + reach]
        if step == 0 and parts is not None:
            bounds[1:1] = [SUB * (n + 1) - 1 for n in range(len(parts) - 1)]
        for n in range(len(bounds) - 1):
            if step == 0 and parts is not None:
                parts[n]()
            sweep(coef, src, bounds[n], bounds[n + 1], adjoint, done, write)


def pack_kernel(fields_in, scalars, *refs):
    sources, outs, (buffers, sems) = refs[:fields_in], refs[fields_in:-2], refs[-2:]
    side = scalars[0]
    tiles = [ref.at[n] for ref in sources for n in range(ref.shape[0])]
    x, y, _ = tiles[0].shape
    starts = pack_starts((len(outs) - 2) // 3, y, side)
    copies = Copies(sems)
    for f, tile in enumerate(tiles):
        for n, (start, _) in enumerate(starts):
            copies.start(tile.at[:, pl.ds(start, SUB)], buffers.at[n, f])
    loads, copies.open = copies.open, []
    for f, tile in enumerate(tiles):
        copies.start(tile.at[pl.ds(0, STEPS)], outs[0].at[f])
        copies.start(tile.at[pl.ds(x - STEPS, STEPS)], outs[1].at[f])
    for f in range(len(tiles)):
        for n, (_, last) in enumerate(starts):
            loads[f * len(starts) + n].wait()
            write_packs(f, n, lambda i: buffers[n, f, i], last, outs)
    copies.wait()


def first_kernel(count, scalars, diffusivity, velocity, probes, weight, *refs):
    side = scalars[0]
    received, coef_out, out = refs[:count], refs[count], refs[count + 1]
    strips, (coef, state, other, sems) = refs[count + 2 : -4], refs[-4:]
    copies = Copies(sems)
    tiles = [diffusivity.at[0]] + [velocity.at[d] for d in range(3)]
    slots = [coef.at[s] for s in (0, 1, 3, 5)]
    for p in range(probes.shape[0]):
        tiles.append(probes.at[p])
        slots.append(state.at[p])
    for f, (tile, slot) in enumerate(zip(tiles, slots)):
        start_widening(copies, slot, tile, f, received)
    for f, slot in enumerate(slots):
        widen_rows(slot, f, received, side)
    copies.wait()
    coefficient_rows(coef)
    copies.start(coef, coef_out)
    run_steps(coef, (state, other), out, False, weight)
    write_strips(out, strips, side)
    copies.wait()


def next_kernel(count, adjoint, scalars, coef_in, tile, *refs):
    side = scalars[0]
    weight = None if adjoint else refs[0]
    refs = refs if adjoint else refs[1:]
    received, out = refs[:count], refs[count]
    strips, (coef, state, other, sems) = refs[count + 1 : -4], refs[-4:]
    fields, x = tile.shape[0], tile.shape[1]
    copies = Copies(sems)
    for p in range(fields):
        start_widening(copies, state.at[p], tile.at[p], p, received)
    ends = Copies(sems.at[pl.ds(3 * fields, x // SUB + 1)])
    rows = [(x, 2 * STEPS)] + [(n, SUB) for n in range(0, x, SUB)]
    waits = []
    for at, size in rows:
        part = (slice(None), pl.ds(at, size))
        waits.append(ends.start(coef_in.at[part], coef.at[part]).wait)
    for p in range(fields):
        widen_rows(state.at[p], p, received, side)
    copies.wait()
    waits[0]()
    run_steps(coef, (state, other), out, adjoint, weight, waits[1:])
    if strips:
        write_strips(out, strips, side)


def dots_kernel(own_group, scalars, images, second, others, out):
    group, x, y, z = images.shape
    chunks, cols = y // SUB, z // LANES
    pairs = [(a, b) for a in range(group) for b in range(group) if not own_group or b <= a]

    def body(i, sums):
        sums = list(sums)
        for c in range(chunks):
            for j in range(cols):
                at = (pl.ds(SUB * c, SUB), pl.ds(LANES * j, LANES))
                other = [others[b, i, *at] for b in range(group)]
                mine = [images[a, i, *at] for a in range(group)]
                then = [second[a, i, *at] for a in range(group)]
                for n, (a, b) in enumerate(pairs):
                    sums[2 * n] = sums[2 * n] + mine[a] * other[b]
                    sums[2 * n + 1] = sums[2 * n + 1] + then[a] * other[b]
        return tuple(sums)

    zero = jnp.zeros((SUB, LANES), jnp.float32)
    sums = lax.fori_loop(0, x, body, (zero,) * (2 * len(pairs)))
    row0, col0 = scalars[1] * group, scalars[2] * group
    count = out.shape[0]
    row = lax.broadcasted_iota(jnp.int32, out.shape, 0)
    lane = lax.broadcasted_iota(jnp.int32, out.shape, 1)
    total = jnp.zeros(out.shape, jnp.float32)
    for n, (a, b) in enumerate(pairs):
        for k in range(2):
            value = jnp.sum(jnp.sum(sums[2 * n + k], axis=0, keepdims=True), axis=1, keepdims=True)
            here = (row == row0 + a) & (lane == col0 + b + k * count) & (scalars[2] >= 0)
            total = total + jnp.where(here, value, 0.0)
    out[...] = total


def basis_kernel(inverse, *refs):
    images, out = refs[:-1], refs[-1]
    group, x, y, z = out.shape
    chunks, cols = y // SUB, z // LANES

    def body(i, carry):
        for c in range(chunks):
            for j in range(cols):
                at = (pl.ds(SUB * c, SUB), pl.ds(LANES * j, LANES))
                sums = [None] * group
                for s, image in enumerate(images):
                    for b in range(group):
                        value = image[b, i, *at]
                        for a in range(group):
                            term = inverse[a, s * group + b] * value
                            sums[a] = term if sums[a] is None else sums[a] + term
                for a in range(group):
                    out[a, i, *at] = sums[a]
        return carry

    lax.fori_loop(0, x, body, None)


def all_sum(value):
    for axis in ("sx", "sy", "probe"):
        devices = lax.axis_size(axis)
        if devices & (devices - 1):
            value = lax.psum(value, axis)
            continue
        bit = 1
        while bit < devices:
            value = value + lax.ppermute(value, axis, [(i, i ^ bit) for i in range(devices)])
            bit *= 2
    return value


def shards(probes, velocity, diffusivity, obs_weight):
    group, x, y, z = probes.shape
    groups = lax.axis_size("probe")
    count = group * groups
    ncells = x * y * z * lax.axis_size("sx") * lax.axis_size("sy")
    both = lax.axis_size("sy") != 2
    side, mine = lax.axis_index("sy"), lax.axis_index("probe")

    def scalars(other):
        return jnp.stack([side, mine, mine - other]).astype(jnp.int32)

    where = scalars(0)
    wide = (x + 2 * STEPS, y + 2 * STEPS, z)
    tile = f32(group, x, y, z)
    strips2 = strip_shapes(group, x, y, z, both)
    fields = [diffusivity[None], velocity, probes]
    total = 4 + group

    def scratch(copies):
        return [
            pltpu.VMEM((7,) + wide, jnp.float32),
            pltpu.VMEM((group,) + wide, jnp.float32),
            pltpu.VMEM((group,) + wide, jnp.float32),
            pltpu.SemaphoreType.DMA((copies,)),
        ]

    packs = 2 if both else 1
    strips = kernel_call(
        functools.partial(pack_kernel, len(fields)),
        strip_shapes(total, x, y, z, both),
        [pltpu.VMEM((packs, total, x, SUB, z), jnp.float32), pltpu.SemaphoreType.DMA((total * (packs + 2),))],
        [where] + fields,
        3.0,
        anywhere=(1, 2, 3),
    )
    received = exchange(strips)
    coef, halfway, *strips = kernel_call(
        functools.partial(first_kernel, len(received)),
        [f32(7, *wide), tile] + strips2,
        scratch(3 * total + 1),
        [where] + fields + [obs_weight] + received,
        14.0,
        anywhere=(1, 2, 3, 5, 6),
        outs_anywhere=(0,),
    )

    def model(field, strips, adjoint, last=False):
        received = exchange(strips)
        ins = [where, coef, field] + ([] if adjoint else [obs_weight])
        return kernel_call(
            functools.partial(next_kernel, len(received), adjoint),
            [tile] + ([] if last else strips2),
            scratch(3 * group + x // SUB + 1),
            ins + received,
            12.0,
            anywhere=(1, 2, len(ins), len(ins) + 1),
        )

    images, *strips = model(halfway, strips, True)

    right = [(i, i + 1) for i in range(groups - 1)]
    passed = [images]
    for _ in range(groups - 1):
        passed.append(lax.ppermute(passed[-1], "probe", right))

    halfway, *strips = model(images, strips, False)
    (second,) = model(halfway, strips, True, True)

    partial = None
    for n, others in enumerate(passed):
        (part,) = kernel_call(
            functools.partial(dots_kernel, n == 0),
            [f32(count, LANES)],
            [],
            [scalars(n), images, second, others],
            4.0,
        )
        partial = part if partial is None else partial + part
    inner = all_sum(partial) / ncells
    strict = jnp.tril(jnp.ones((count, count), jnp.float32), -1)
    gram, ritz = inner[:, :count], inner[:, count : 2 * count]
    gram = gram + (gram * strict).T
    ritz = ritz + (ritz * strict).T
    lower = jnp.linalg.cholesky(gram)
    inverse = jax.scipy.linalg.solve_triangular(lower, jnp.eye(count, dtype=jnp.float32), lower=True)
    highest = lax.Precision.HIGHEST
    projected = jnp.dot(jnp.dot(inverse, ritz, precision=highest), inverse.T, precision=highest)

    rows = lax.dynamic_slice_in_dim(inverse, mine * group, group, 0)
    parts = []
    for n in range(groups):
        part = lax.dynamic_slice_in_dim(rows, jnp.maximum(mine - n, 0) * group, group, 1)
        parts.append(jnp.where(mine >= n, part, 0.0))
    (basis,) = kernel_call(basis_kernel, [tile], [], [jnp.concatenate(parts, 1)] + passed, 6.0)
    return (basis, projected)


def solution(mesh):
    return jax.shard_map(
        shards,
        mesh=mesh,
        in_specs=(
            P("probe", "sx", "sy", None),
            P(None, "sx", "sy", None),
            P("sx", "sy", None),
            P("sx", "sy", None),
        ),
        out_specs=(P("probe", "sx", "sy", None), P()),
        check_vma=False,
    )
```

```python
import functools

import jax
import jax.numpy as jnp
from jax import lax
from jax.experimental import pallas as pl
from jax.experimental.pallas import tpu as pltpu
from jax.sharding import PartitionSpec as P

STEPS = 4
SUB = 8
LANES = 128
ROWS = 2
VMEM_LIMIT = 58 * 1024 * 1024
FLOPS_PER_MICRO = 1.15e9
BYTES_PER_MICRO = 3.6e6


def kernel_call(body, outs, scratch, ins, micros, anywhere=(), outs_anywhere=()):
    spec = lambda n, names: pl.BlockSpec(memory_space=pl.ANY if n in names else pltpu.VMEM)
    specs = [spec(n, anywhere) for n in range(len(ins))]
    specs[0] = pl.BlockSpec(memory_space=pltpu.SMEM)
    return pl.pallas_call(
        body,
        out_shape=outs,
        in_specs=specs,
        out_specs=[spec(n, outs_anywhere) for n in range(len(outs))],
        scratch_shapes=scratch,
        compiler_params=pltpu.CompilerParams(vmem_limit_bytes=VMEM_LIMIT),
        cost_estimate=pl.CostEstimate(
            flops=int(micros * FLOPS_PER_MICRO),
            bytes_accessed=int(micros * BYTES_PER_MICRO),
            transcendentals=0,
        ),
    )(*ins)


def f32(*shape):
    return jax.ShapeDtypeStruct(shape, jnp.float32)


def strip_shapes(fields, x, y, z, both):
    packs = [f32(fields, x // 2, SUB, z), f32(fields, 2, SUB, z), f32(fields, 2, SUB, z)]
    return [f32(fields, STEPS, y, z)] * 2 + packs * (2 if both else 1)


def pack_starts(packs, y, side):
    if packs == 2:
        return [(0, False), (y - SUB, True)]
    return [(pl.multiple_of(jnp.where(side == 0, y - SUB, 0), SUB), side == 0)]


def packed_pair(row, first, second, last):
    hi = lambda: jnp.where(row < STEPS, pltpu.roll(first, STEPS, 0), second)
    lo = lambda: jnp.where(row < STEPS, first, pltpu.roll(second, STEPS, 0))
    if isinstance(last, bool):
        return hi() if last else lo()
    return jnp.where(last, hi(), lo())


def write_packs(field, n, rows, last, outs):
    pack, corner_lo, corner_hi = outs[2 + 3 * n : 5 + 3 * n]
    half, z = pack.shape[1], pack.shape[3]
    row = lax.broadcasted_iota(jnp.int32, (SUB, z), 0)

    def step(i, carry):
        pack[field, i] = packed_pair(row, rows(2 * i), rows(2 * i + 1), last)
        return carry

    lax.fori_loop(0, half, step, None, unroll=4)
    for i in range(2):
        corner_lo[field, i] = pack[field, i]
        corner_hi[field, i] = pack[field, half - 2 + i]


def write_strips(tile, outs, side):
    fields, x, y, _ = tile.shape
    for p in range(fields):
        for i in range(STEPS):
            outs[0][p, i] = tile[p, i]
            outs[1][p, i] = tile[p, x - STEPS + i]
        for n, (start, last) in enumerate(pack_starts((len(outs) - 2) // 3, y, side)):
            write_packs(p, n, lambda i: tile[p, i, pl.ds(start, SUB)], last, outs)


def exchange(strips):
    nx, ny = lax.axis_size("sx"), lax.axis_size("sy")
    up = [(i, i + 1) for i in range(nx - 1)]
    down = [(j, i) for i, j in up]

    def moved(value, dx, dys):
        pairs = []
        for i in range(nx):
            for j in range(ny):
                for dy in dys(j):
                    if 0 <= i + dx < nx and 0 <= j + dy < ny:
                        pairs.append((i * ny + j, (i + dx) * ny + j + dy))
        return lax.ppermute(value, ("sx", "sy"), pairs)

    below = lax.ppermute(strips[1], "sx", up)
    above = lax.ppermute(strips[0], "sx", down)
    received = [below, above]
    if len(strips) == 5:
        flip = lambda j: (1 - 2 * j,)
        pack, corner_lo, corner_hi = strips[2:]
        received += [moved(pack, 0, flip), moved(corner_hi, 1, flip), moved(corner_lo, -1, flip)]
    else:
        for n, dy in ((0, -1), (1, 1)):
            pack, corner_lo, corner_hi = strips[2 + 3 * n : 5 + 3 * n]
            one = lambda j, dy=dy: (dy,)
            received += [moved(pack, 0, one), moved(corner_hi, 1, one), moved(corner_lo, -1, one)]
    return received


class Copies:
    def __init__(self, sems):
        self.sems, self.open, self.used = sems, [], 0

    def start(self, src, dst):
        copy = pltpu.make_async_copy(src, dst, self.sems.at[self.used])
        self.used += 1
        copy.start()
        self.open.append(copy)
        return copy

    def wait(self):
        for copy in self.open:
            copy.wait()
        self.open = []


def start_widening(copies, dst, tile, field, received):
    x, y = tile.shape[0], tile.shape[1]
    copies.start(tile, dst.at[pl.ds(0, x), pl.ds(0, y)])
    copies.start(received[1].at[field], dst.at[pl.ds(x, STEPS), pl.ds(0, y)])
    copies.start(received[0].at[field], dst.at[pl.ds(x + STEPS, STEPS), pl.ds(0, y)])


def widen_rows(dst, field, received, side):
    half, z = received[2].shape[1], received[2].shape[3]
    x, y = 2 * half, dst.shape[1] - SUB
    row = lax.broadcasted_iota(jnp.int32, (SUB, z), 0)
    both = len(received) > 5

    def put(at, packs):
        if both:
            hi, lo = packs
        else:
            hi = jnp.where(side == 0, packs[0], 0.0)
            lo = jnp.where(side == 0, 0.0, packs[0])
        dst[at, y : y + SUB] = jnp.where(row < STEPS, hi, pltpu.roll(lo, STEPS, 0))
        dst[at + 1, y : y + SUB] = jnp.where(row < STEPS, pltpu.roll(hi, STEPS, 0), lo)

    groups = [received[2:5]] + ([received[5:8]] if both else [])

    def main(i, carry):
        put(2 * i, [g[0][field, i] for g in groups])
        return carry

    lax.fori_loop(0, half, main, None, unroll=4)
    for i in range(2):
        put(x + 2 * i, [g[2][field, i] for g in groups])
        put(x + STEPS + 2 * i, [g[1][field, i] for g in groups])


def coefficient_rows(coef):
    _, wide, rows, z = coef.shape
    lane = lax.broadcasted_iota(jnp.int32, (SUB, z), 1)

    def row(i, carry):
        for c in range(rows // SUB):
            at = pl.ds(SUB * c, SUB)
            spread = coef[0, i, at]
            values = [1.0 - 6.0 * spread]
            for d in range(3):
                half = 0.5 * coef[1 + 2 * d, i, at]
                plus, minus = spread - half, spread + half
                if d == 2:
                    plus = jnp.where(lane == z - 1, 0.0, plus)
                    minus = jnp.where(lane == 0, 0.0, minus)
                values += [plus, minus]
            for s, value in enumerate(values):
                coef[s, i, at] = value
        return carry

    lax.fori_loop(0, wide, row, None)


def sweep(coef, src, first, stop, adjoint, done, write):
    fields, wide, rows, z = src.shape
    chunks, cols = rows // SUB, z // LANES
    sub = lax.broadcasted_iota(jnp.int32, (SUB, LANES), 0)
    lane = lax.broadcasted_iota(jnp.int32, (SUB, LANES), 1)
    first_row, last_row = sub == 0, sub == SUB - 1
    first_lane, last_lane = lane == 0, lane == LANES - 1

    def piece(ref, lead, xi, c, j):
        return ref[lead, xi, SUB * c : SUB * (c + 1), LANES * j : LANES * (j + 1)]

    def body(pair, carry):
        wrap = lambda a: jnp.where(a < 0, a + wide, a)
        base = first + ROWS * pair
        at = [wrap(base + d) for d in range(-1, ROWS + 1)]
        kept = {}

        def load(ref, lead, r, c, j):
            key = (ref is coef, lead, r, c % chunks, j)
            if key not in kept:
                kept[key] = piece(ref, lead, at[r + 1], c % chunks, j)
            return kept[key]

        def scaled(slot, p, r, c, j):
            u = load(src, p, r, c, j)
            return load(coef, slot, r, c, j) * u if adjoint else u

        def turned(slot, shift, p, r, c, j):
            key = ("turned", slot, p, r, c % chunks, j)
            if key not in kept:
                kept[key] = pltpu.roll(scaled(slot, p, r, c, j), shift, 0)
            return kept[key]

        for c in range(done):
            results = []
            for r in range(ROWS):
                plus, minus = {}, {}
                for j in range(cols):
                    for p in range(fields):
                        plus[p, j] = pltpu.roll(scaled(6, p, r, c, j), LANES - 1, 1)
                        minus[p, j] = pltpu.roll(scaled(5, p, r, c, j), 1, 1)
                for j in range(cols):
                    for p in range(fields):
                        u, xp, xm = (load(src, p, r + d, c, j) for d in (0, 1, -1))
                        yp = jnp.where(last_row, turned(4, SUB - 1, p, r, c + 1, j), turned(4, SUB - 1, p, r, c, j))
                        ym = jnp.where(first_row, turned(3, 1, p, r, c - 1, j), turned(3, 1, p, r, c, j))
                        zp = jnp.where(last_lane, plus[p, (j + 1) % cols], plus[p, j])
                        zm = jnp.where(first_lane, minus[p, (j - 1) % cols], minus[p, j])
                        if adjoint:
                            xs = load(coef, 2, r + 1, c, j) * xp + load(coef, 1, r - 1, c, j) * xm
                            ys, zs = yp + ym, zp + zm
                        else:
                            xs = load(coef, 1, r, c, j) * xp + load(coef, 2, r, c, j) * xm
                            ys = load(coef, 3, r, c, j) * yp + load(coef, 4, r, c, j) * ym
                            zs = load(coef, 5, r, c, j) * zp + load(coef, 6, r, c, j) * zm
                        value = (load(coef, 0, r, c, j) * u + xs) + (ys + zs)
                        results.append((p, at[r + 1], c, j, value))
            for result in results:
                write(*result)
        return carry

    lax.fori_loop(0, (stop - first) // ROWS, body, None)


def run_steps(coef, states, out, adjoint, weight=None, parts=None):
    x, tile_rows = out.shape[1], out.shape[2]
    for step in range(STEPS):
        src, dst = states[step % 2], states[(step + 1) % 2]
        last = step == STEPS - 1

        def write(p, i, c, j, value):
            at = (pl.ds(SUB * c, SUB), pl.ds(LANES * j, LANES))
            if last:
                out[p, i, *at] = value if weight is None else weight[i, *at] * value
            else:
                dst[p, i, *at] = value

        done = (tile_rows if last else src.shape[2]) // SUB
        reach = STEPS - 1 - step
        bounds = [-reach, x + reach]
        if step == 0 and parts is not None:
            bounds[1:1] = [SUB * (n + 1) - 1 for n in range(len(parts) - 1)]
        for n in range(len(bounds) - 1):
            if step == 0 and parts is not None:
                parts[n]()
            sweep(coef, src, bounds[n], bounds[n + 1], adjoint, done, write)


def pack_kernel(fields_in, scalars, *refs):
    sources, outs, (buffers, sems) = refs[:fields_in], refs[fields_in:-2], refs[-2:]
    side = scalars[0]
    tiles = [ref.at[n] for ref in sources for n in range(ref.shape[0])]
    x, y, _ = tiles[0].shape
    starts = pack_starts((len(outs) - 2) // 3, y, side)
    copies = Copies(sems)
    for f, tile in enumerate(tiles):
        for n, (start, _) in enumerate(starts):
            copies.start(tile.at[:, pl.ds(start, SUB)], buffers.at[n, f])
    loads, copies.open = copies.open, []
    for f, tile in enumerate(tiles):
        copies.start(tile.at[pl.ds(0, STEPS)], outs[0].at[f])
        copies.start(tile.at[pl.ds(x - STEPS, STEPS)], outs[1].at[f])
    for f in range(len(tiles)):
        for n, (_, last) in enumerate(starts):
            loads[f * len(starts) + n].wait()
            write_packs(f, n, lambda i: buffers[n, f, i], last, outs)
    copies.wait()


def first_kernel(count, scalars, diffusivity, velocity, probes, weight, *refs):
    side = scalars[0]
    received, coef_out, out = refs[:count], refs[count], refs[count + 1]
    strips, (coef, state, other, sems) = refs[count + 2 : -4], refs[-4:]
    copies = Copies(sems)
    tiles = [diffusivity.at[0]] + [velocity.at[d] for d in range(3)]
    slots = [coef.at[s] for s in (0, 1, 3, 5)]
    for p in range(probes.shape[0]):
        tiles.append(probes.at[p])
        slots.append(state.at[p])
    for f, (tile, slot) in enumerate(zip(tiles, slots)):
        start_widening(copies, slot, tile, f, received)
    for f, slot in enumerate(slots):
        widen_rows(slot, f, received, side)
    copies.wait()
    coefficient_rows(coef)
    copies.start(coef, coef_out)
    run_steps(coef, (state, other), out, False, weight)
    write_strips(out, strips, side)
    copies.wait()


def next_kernel(count, adjoint, scalars, coef_in, tile, *refs):
    side = scalars[0]
    weight = None if adjoint else refs[0]
    refs = refs if adjoint else refs[1:]
    received, out = refs[:count], refs[count]
    strips, (coef, state, other, sems) = refs[count + 1 : -4], refs[-4:]
    fields, x = tile.shape[0], tile.shape[1]
    copies = Copies(sems)
    for p in range(fields):
        start_widening(copies, state.at[p], tile.at[p], p, received)
    ends = Copies(sems.at[pl.ds(3 * fields, x // SUB + 1)])
    rows = [(x, 2 * STEPS)] + [(n, SUB) for n in range(0, x, SUB)]
    waits = []
    for at, size in rows:
        part = (slice(None), pl.ds(at, size))
        waits.append(ends.start(coef_in.at[part], coef.at[part]).wait)
    for p in range(fields):
        widen_rows(state.at[p], p, received, side)
    copies.wait()
    waits[0]()
    run_steps(coef, (state, other), out, adjoint, weight, waits[1:])
    if strips:
        write_strips(out, strips, side)


def dots_kernel(own_group, scalars, images, second, others, out):
    group, x, y, z = images.shape
    chunks, cols = y // SUB, z // LANES
    pairs = [(a, b) for a in range(group) for b in range(group) if not own_group or b <= a]

    def body(i, sums):
        sums = list(sums)
        for c in range(chunks):
            for j in range(cols):
                at = (pl.ds(SUB * c, SUB), pl.ds(LANES * j, LANES))
                other = [others[b, i, *at] for b in range(group)]
                mine = [images[a, i, *at] for a in range(group)]
                then = [second[a, i, *at] for a in range(group)]
                for n, (a, b) in enumerate(pairs):
                    sums[2 * n] = sums[2 * n] + mine[a] * other[b]
                    sums[2 * n + 1] = sums[2 * n + 1] + then[a] * other[b]
        return tuple(sums)

    zero = jnp.zeros((SUB, LANES), jnp.float32)
    sums = lax.fori_loop(0, x, body, (zero,) * (2 * len(pairs)))
    row0, col0 = scalars[1] * group, scalars[2] * group
    count = out.shape[0]
    row = lax.broadcasted_iota(jnp.int32, out.shape, 0)
    lane = lax.broadcasted_iota(jnp.int32, out.shape, 1)
    total = jnp.zeros(out.shape, jnp.float32)
    for n, (a, b) in enumerate(pairs):
        for k in range(2):
            value = jnp.sum(jnp.sum(sums[2 * n + k], axis=0, keepdims=True), axis=1, keepdims=True)
            here = (row == row0 + a) & (lane == col0 + b + k * count) & (scalars[2] >= 0)
            total = total + jnp.where(here, value, 0.0)
    out[...] = total


def basis_kernel(inverse, *refs):
    images, out = refs[:-1], refs[-1]
    group, x, y, z = out.shape
    chunks, cols = y // SUB, z // LANES

    def body(i, carry):
        for c in range(chunks):
            for j in range(cols):
                at = (pl.ds(SUB * c, SUB), pl.ds(LANES * j, LANES))
                sums = [None] * group
                for s, image in enumerate(images):
                    for b in range(group):
                        value = image[b, i, *at]
                        for a in range(group):
                            term = inverse[a, s * group + b] * value
                            sums[a] = term if sums[a] is None else sums[a] + term
                for a in range(group):
                    out[a, i, *at] = sums[a]
        return carry

    lax.fori_loop(0, x, body, None)


def all_sum(value):
    for axis in ("sx", "sy", "probe"):
        devices = lax.axis_size(axis)
        if devices & (devices - 1):
            value = lax.psum(value, axis)
            continue
        move = lambda bits: lax.ppermute(value, axis, [(i, i ^ bits) for i in range(devices)])
        bit = 1
        while bit < devices:
            if 4 * bit <= devices:
                value = (value + move(bit)) + (move(2 * bit) + move(3 * bit))
                bit *= 4
            else:
                value = value + move(bit)
                bit *= 2
    return value


def shards(probes, velocity, diffusivity, obs_weight):
    group, x, y, z = probes.shape
    groups = lax.axis_size("probe")
    count = group * groups
    ncells = x * y * z * lax.axis_size("sx") * lax.axis_size("sy")
    both = lax.axis_size("sy") != 2
    side, mine = lax.axis_index("sy"), lax.axis_index("probe")

    def scalars(other):
        return jnp.stack([side, mine, mine - other]).astype(jnp.int32)

    where = scalars(0)
    wide = (x + 2 * STEPS, y + 2 * STEPS, z)
    tile = f32(group, x, y, z)
    strips2 = strip_shapes(group, x, y, z, both)
    fields = [diffusivity[None], velocity, probes]
    total = 4 + group

    def scratch(copies):
        return [
            pltpu.VMEM((7,) + wide, jnp.float32),
            pltpu.VMEM((group,) + wide, jnp.float32),
            pltpu.VMEM((group,) + wide, jnp.float32),
            pltpu.SemaphoreType.DMA((copies,)),
        ]

    packs = 2 if both else 1

    def pack(sources):
        number = sum(a.shape[0] for a in sources)
        return kernel_call(
            functools.partial(pack_kernel, len(sources)),
            strip_shapes(number, x, y, z, both),
            [pltpu.VMEM((packs, number, x, SUB, z), jnp.float32), pltpu.SemaphoreType.DMA((number * (packs + 2),))],
            [where] + sources,
            3.0,
            anywhere=range(1, len(sources) + 1),
        )

    def right(value, hops):
        return lax.ppermute(value, "probe", [(i, i + hops) for i in range(groups - hops)])

    next_probes = right(probes, 1)
    strips = pack(fields)
    received = exchange(strips)
    coef, halfway, *strips = kernel_call(
        functools.partial(first_kernel, len(received)),
        [f32(7, *wide), tile] + strips2,
        scratch(3 * total + 1),
        [where] + fields + [obs_weight] + received,
        14.0,
        anywhere=(1, 2, 3, 5, 6),
        outs_anywhere=(0,),
    )

    def model(field, strips, adjoint, last=False):
        received = exchange(strips)
        ins = [where, coef, field] + ([] if adjoint else [obs_weight])
        return kernel_call(
            functools.partial(next_kernel, len(received), adjoint),
            [tile] + ([] if last else strips2),
            scratch(3 * group + x // SUB + 1),
            ins + received,
            12.0,
            anywhere=(1, 2, len(ins), len(ins) + 1),
        )

    images, *strips = model(halfway, strips, True)
    far = [right(images, hops) for hops in range(3, groups)]

    half_next, *strips_next = model(next_probes, pack([next_probes]), False)
    halfway, *strips = model(images, strips, False)
    (images_next,) = model(half_next, strips_next, True, True)
    images_next, far = lax.optimization_barrier((images_next, far))
    passed = [images, images_next, right(images_next, 1)] + far
    (second,) = model(halfway, strips, True, True)

    partial = None
    for n, others in enumerate(passed):
        (part,) = kernel_call(
            functools.partial(dots_kernel, n == 0),
            [f32(count, LANES)],
            [],
            [scalars(n), images, second, others],
            4.0,
        )
        partial = part if partial is None else partial + part
    inner = all_sum(partial) / ncells
    strict = jnp.tril(jnp.ones((count, count), jnp.float32), -1)
    gram, ritz = inner[:, :count], inner[:, count : 2 * count]
    gram = gram + (gram * strict).T
    ritz = ritz + (ritz * strict).T
    lower = jnp.linalg.cholesky(gram)
    inverse = jax.scipy.linalg.solve_triangular(lower, jnp.eye(count, dtype=jnp.float32), lower=True)
    highest = lax.Precision.HIGHEST
    projected = jnp.dot(jnp.dot(inverse, ritz, precision=highest), inverse.T, precision=highest)

    rows = lax.dynamic_slice_in_dim(inverse, mine * group, group, 0)
    parts = []
    for n in range(groups):
        part = lax.dynamic_slice_in_dim(rows, jnp.maximum(mine - n, 0) * group, group, 1)
        parts.append(jnp.where(mine >= n, part, 0.0))
    (basis,) = kernel_call(basis_kernel, [tile], [], [jnp.concatenate(parts, 1)] + passed, 6.0)
    return (basis, projected)


def solution(mesh):
    return jax.shard_map(
        shards,
        mesh=mesh,
        in_specs=(
            P("probe", "sx", "sy", None),
            P(None, "sx", "sy", None),
            P("sx", "sy", None),
            P("sx", "sy", None),
        ),
        out_specs=(P("probe", "sx", "sy", None), P()),
        check_vma=False,
    )
```

```python
import functools

import jax
import jax.numpy as jnp
from jax import lax
from jax.experimental import pallas as pl
from jax.experimental.pallas import tpu as pltpu
from jax.sharding import PartitionSpec as P

STEPS = 4
SUB = 8
LANES = 128
ROWS = 2
BLOCK = 4
VMEM_LIMIT = 58 * 1024 * 1024
FLOPS_PER_MICRO = 1.15e9
BYTES_PER_MICRO = 3.6e6


def kernel_call(body, outs, scratch, ins, micros, anywhere=(), outs_anywhere=()):
    spec = lambda n, names: pl.BlockSpec(memory_space=pl.ANY if n in names else pltpu.VMEM)
    specs = [spec(n, anywhere) for n in range(len(ins))]
    specs[0] = pl.BlockSpec(memory_space=pltpu.SMEM)
    return pl.pallas_call(
        body,
        out_shape=outs,
        in_specs=specs,
        out_specs=[spec(n, outs_anywhere) for n in range(len(outs))],
        scratch_shapes=scratch,
        compiler_params=pltpu.CompilerParams(vmem_limit_bytes=VMEM_LIMIT),
        cost_estimate=pl.CostEstimate(
            flops=int(micros * FLOPS_PER_MICRO),
            bytes_accessed=int(micros * BYTES_PER_MICRO),
            transcendentals=0,
        ),
    )(*ins)


def f32(*shape):
    return jax.ShapeDtypeStruct(shape, jnp.float32)


def strip_shapes(fields, x, y, z, both):
    packs = [f32(fields, x // 2, SUB, z), f32(fields, 2, SUB, z), f32(fields, 2, SUB, z)]
    return [f32(fields, STEPS, y, z)] * 2 + packs * (2 if both else 1)


def pack_starts(packs, y, side):
    if packs == 2:
        return [(0, False), (y - SUB, True)]
    return [(pl.multiple_of(jnp.where(side == 0, y - SUB, 0), SUB), side == 0)]


def packed_pair(row, first, second, last):
    hi = lambda: jnp.where(row < STEPS, pltpu.roll(first, STEPS, 0), second)
    lo = lambda: jnp.where(row < STEPS, first, pltpu.roll(second, STEPS, 0))
    if isinstance(last, bool):
        return hi() if last else lo()
    return jnp.where(last, hi(), lo())


def write_packs(field, n, rows, last, outs):
    pack, corner_lo, corner_hi = outs[2 + 3 * n : 5 + 3 * n]
    half, z = pack.shape[1], pack.shape[3]
    row = lax.broadcasted_iota(jnp.int32, (SUB, z), 0)

    def step(i, carry):
        pack[field, i] = packed_pair(row, rows(2 * i), rows(2 * i + 1), last)
        return carry

    lax.fori_loop(0, half, step, None, unroll=4)
    for i in range(2):
        corner_lo[field, i] = pack[field, i]
        corner_hi[field, i] = pack[field, half - 2 + i]


def write_strips(tile, outs, side):
    fields, x, y, _ = tile.shape
    for p in range(fields):
        for i in range(STEPS):
            outs[0][p, i] = tile[p, i]
            outs[1][p, i] = tile[p, x - STEPS + i]
        for n, (start, last) in enumerate(pack_starts((len(outs) - 2) // 3, y, side)):
            write_packs(p, n, lambda i: tile[p, i, pl.ds(start, SUB)], last, outs)


def exchange(strips):
    nx, ny = lax.axis_size("sx"), lax.axis_size("sy")
    up = [(i, i + 1) for i in range(nx - 1)]
    down = [(j, i) for i, j in up]

    def moved(value, dx, dys):
        pairs = []
        for i in range(nx):
            for j in range(ny):
                for dy in dys(j):
                    if 0 <= i + dx < nx and 0 <= j + dy < ny:
                        pairs.append((i * ny + j, (i + dx) * ny + j + dy))
        return lax.ppermute(value, ("sx", "sy"), pairs)

    below = lax.ppermute(strips[1], "sx", up)
    above = lax.ppermute(strips[0], "sx", down)
    received = [below, above]
    if len(strips) == 5:
        flip = lambda j: (1 - 2 * j,)
        pack, corner_lo, corner_hi = strips[2:]
        received += [moved(pack, 0, flip), moved(corner_hi, 1, flip), moved(corner_lo, -1, flip)]
    else:
        for n, dy in ((0, -1), (1, 1)):
            pack, corner_lo, corner_hi = strips[2 + 3 * n : 5 + 3 * n]
            one = lambda j, dy=dy: (dy,)
            received += [moved(pack, 0, one), moved(corner_hi, 1, one), moved(corner_lo, -1, one)]
    return received


class Copies:
    def __init__(self, sems):
        self.sems, self.open, self.used = sems, [], 0

    def start(self, src, dst):
        copy = pltpu.make_async_copy(src, dst, self.sems.at[self.used])
        self.used += 1
        copy.start()
        self.open.append(copy)
        return copy

    def wait(self):
        for copy in self.open:
            copy.wait()
        self.open = []


def start_widening(copies, dst, tile, field, received):
    x, y = tile.shape[0], tile.shape[1]
    copies.start(tile, dst.at[pl.ds(0, x), pl.ds(0, y)])
    copies.start(received[1].at[field], dst.at[pl.ds(x, STEPS), pl.ds(0, y)])
    copies.start(received[0].at[field], dst.at[pl.ds(x + STEPS, STEPS), pl.ds(0, y)])


def widen_rows(dst, field, received, side):
    half, z = received[2].shape[1], received[2].shape[3]
    x, y = 2 * half, dst.shape[1] - SUB
    row = lax.broadcasted_iota(jnp.int32, (SUB, z), 0)
    both = len(received) > 5

    def put(at, packs):
        if both:
            hi, lo = packs
        else:
            hi = jnp.where(side == 0, packs[0], 0.0)
            lo = jnp.where(side == 0, 0.0, packs[0])
        dst[at, y : y + SUB] = jnp.where(row < STEPS, hi, pltpu.roll(lo, STEPS, 0))
        dst[at + 1, y : y + SUB] = jnp.where(row < STEPS, pltpu.roll(hi, STEPS, 0), lo)

    groups = [received[2:5]] + ([received[5:8]] if both else [])

    def main(i, carry):
        put(2 * i, [g[0][field, i] for g in groups])
        return carry

    lax.fori_loop(0, half, main, None, unroll=4)
    for i in range(2):
        put(x + 2 * i, [g[2][field, i] for g in groups])
        put(x + STEPS + 2 * i, [g[1][field, i] for g in groups])


def coefficient_rows(coef):
    _, wide, rows, z = coef.shape
    lane = lax.broadcasted_iota(jnp.int32, (SUB, z), 1)

    def row(i, carry):
        for c in range(rows // SUB):
            at = pl.ds(SUB * c, SUB)
            spread = coef[0, i, at]
            values = [1.0 - 6.0 * spread]
            for d in range(3):
                half = 0.5 * coef[1 + 2 * d, i, at]
                plus, minus = spread - half, spread + half
                if d == 2:
                    plus = jnp.where(lane == z - 1, 0.0, plus)
                    minus = jnp.where(lane == 0, 0.0, minus)
                values += [plus, minus]
            for s, value in enumerate(values):
                coef[s, i, at] = value
        return carry

    lax.fori_loop(0, wide, row, None)


def sweep(coef, src, first, stop, adjoint, done, write):
    fields, wide, rows, z = src.shape
    chunks, cols = rows // SUB, z // LANES
    sub = lax.broadcasted_iota(jnp.int32, (SUB, LANES), 0)
    lane = lax.broadcasted_iota(jnp.int32, (SUB, LANES), 1)
    first_row, last_row = sub == 0, sub == SUB - 1
    first_lane, last_lane = lane == 0, lane == LANES - 1

    def piece(ref, lead, xi, c, j):
        return ref[lead, xi, SUB * c : SUB * (c + 1), LANES * j : LANES * (j + 1)]

    def body(pair, carry):
        wrap = lambda a: jnp.where(a < 0, a + wide, a)
        base = first + ROWS * pair
        at = [wrap(base + d) for d in range(-1, ROWS + 1)]
        kept = {}

        def load(ref, lead, r, c, j):
            key = (ref is coef, lead, r, c % chunks, j)
            if key not in kept:
                kept[key] = piece(ref, lead, at[r + 1], c % chunks, j)
            return kept[key]

        def scaled(slot, p, r, c, j):
            u = load(src, p, r, c, j)
            return load(coef, slot, r, c, j) * u if adjoint else u

        def turned(slot, shift, p, r, c, j):
            key = ("turned", slot, p, r, c % chunks, j)
            if key not in kept:
                kept[key] = pltpu.roll(scaled(slot, p, r, c, j), shift, 0)
            return kept[key]

        for c in range(done):
            results = []
            for r in range(ROWS):
                plus, minus = {}, {}
                for j in range(cols):
                    for p in range(fields):
                        plus[p, j] = pltpu.roll(scaled(6, p, r, c, j), LANES - 1, 1)
                        minus[p, j] = pltpu.roll(scaled(5, p, r, c, j), 1, 1)
                for j in range(cols):
                    for p in range(fields):
                        u, xp, xm = (load(src, p, r + d, c, j) for d in (0, 1, -1))
                        yp = jnp.where(last_row, turned(4, SUB - 1, p, r, c + 1, j), turned(4, SUB - 1, p, r, c, j))
                        ym = jnp.where(first_row, turned(3, 1, p, r, c - 1, j), turned(3, 1, p, r, c, j))
                        zp = jnp.where(last_lane, plus[p, (j + 1) % cols], plus[p, j])
                        zm = jnp.where(first_lane, minus[p, (j - 1) % cols], minus[p, j])
                        if adjoint:
                            xs = load(coef, 2, r + 1, c, j) * xp + load(coef, 1, r - 1, c, j) * xm
                            ys, zs = yp + ym, zp + zm
                        else:
                            xs = load(coef, 1, r, c, j) * xp + load(coef, 2, r, c, j) * xm
                            ys = load(coef, 3, r, c, j) * yp + load(coef, 4, r, c, j) * ym
                            zs = load(coef, 5, r, c, j) * zp + load(coef, 6, r, c, j) * zm
                        value = (load(coef, 0, r, c, j) * u + xs) + (ys + zs)
                        results.append((p, at[r + 1], c, j, value))
            for result in results:
                write(*result)
        return carry

    lax.fori_loop(0, (stop - first) // ROWS, body, None)


def run_steps(coef, states, out, adjoint, weight=None, parts=None):
    x, tile_rows = out.shape[1], out.shape[2]
    for step in range(STEPS):
        src, dst = states[step % 2], states[(step + 1) % 2]
        last = step == STEPS - 1

        def write(p, i, c, j, value):
            at = (pl.ds(SUB * c, SUB), pl.ds(LANES * j, LANES))
            if last:
                out[p, i, *at] = value if weight is None else weight[i, *at] * value
            else:
                dst[p, i, *at] = value

        done = (tile_rows if last else src.shape[2]) // SUB
        reach = STEPS - 1 - step
        bounds = [-reach, x + reach]
        if step == 0 and parts is not None:
            bounds[1:1] = [SUB * (n + 1) - 1 for n in range(len(parts) - 1)]
        for n in range(len(bounds) - 1):
            if step == 0 and parts is not None:
                parts[n]()
            sweep(coef, src, bounds[n], bounds[n + 1], adjoint, done, write)


def pack_kernel(fields_in, scalars, *refs):
    sources, outs, (buffers, sems) = refs[:fields_in], refs[fields_in:-2], refs[-2:]
    side = scalars[0]
    tiles = [ref.at[n] for ref in sources for n in range(ref.shape[0])]
    x, y, _ = tiles[0].shape
    starts = pack_starts((len(outs) - 2) // 3, y, side)
    copies = Copies(sems)
    for f, tile in enumerate(tiles):
        for n, (start, _) in enumerate(starts):
            copies.start(tile.at[:, pl.ds(start, SUB)], buffers.at[n, f])
    loads, copies.open = copies.open, []
    for f, tile in enumerate(tiles):
        copies.start(tile.at[pl.ds(0, STEPS)], outs[0].at[f])
        copies.start(tile.at[pl.ds(x - STEPS, STEPS)], outs[1].at[f])
    for f in range(len(tiles)):
        for n, (_, last) in enumerate(starts):
            loads[f * len(starts) + n].wait()
            write_packs(f, n, lambda i: buffers[n, f, i], last, outs)
    copies.wait()


def first_kernel(count, scalars, diffusivity, velocity, probes, weight, *refs):
    side = scalars[0]
    received, coef_out, out = refs[:count], refs[count], refs[count + 1]
    strips, (coef, state, other, sems) = refs[count + 2 : -4], refs[-4:]
    copies = Copies(sems)
    tiles = [diffusivity.at[0]] + [velocity.at[d] for d in range(3)]
    slots = [coef.at[s] for s in (0, 1, 3, 5)]
    for p in range(probes.shape[0]):
        tiles.append(probes.at[p])
        slots.append(state.at[p])
    for f, (tile, slot) in enumerate(zip(tiles, slots)):
        start_widening(copies, slot, tile, f, received)
    for f, slot in enumerate(slots):
        widen_rows(slot, f, received, side)
    copies.wait()
    coefficient_rows(coef)
    copies.start(coef, coef_out)
    run_steps(coef, (state, other), out, False, weight)
    write_strips(out, strips, side)
    copies.wait()


def next_kernel(count, adjoint, scalars, coef_in, tile, *refs):
    side = scalars[0]
    weight = None if adjoint else refs[0]
    refs = refs if adjoint else refs[1:]
    received, out = refs[:count], refs[count]
    strips, (coef, state, other, sems) = refs[count + 1 : -4], refs[-4:]
    fields, x = tile.shape[0], tile.shape[1]
    copies = Copies(sems)
    for p in range(fields):
        start_widening(copies, state.at[p], tile.at[p], p, received)
    ends = Copies(sems.at[pl.ds(3 * fields, x // SUB + 1)])
    rows = [(x, 2 * STEPS)] + [(n, SUB) for n in range(0, x, SUB)]
    waits = []
    for at, size in rows:
        part = (slice(None), pl.ds(at, size))
        waits.append(ends.start(coef_in.at[part], coef.at[part]).wait)
    for p in range(fields):
        widen_rows(state.at[p], p, received, side)
    copies.wait()
    waits[0]()
    run_steps(coef, (state, other), out, adjoint, weight, waits[1:])
    if strips:
        write_strips(out, strips, side)


def blocked_call(body, out_shape, out_block, scratch, scalars, ins, micros):
    group, x, y, z = ins[0].shape
    block = pl.BlockSpec((group, BLOCK, y, z), lambda i: (0, i, 0, 0))
    out = block if out_block else pl.BlockSpec(out_shape.shape, lambda i: (0, 0))
    return pl.pallas_call(
        body,
        grid=(x // BLOCK,),
        out_shape=out_shape,
        in_specs=[pl.BlockSpec(memory_space=pltpu.SMEM)] + [block] * len(ins),
        out_specs=out,
        scratch_shapes=scratch,
        compiler_params=pltpu.CompilerParams(vmem_limit_bytes=VMEM_LIMIT),
        cost_estimate=pl.CostEstimate(
            flops=int(micros * FLOPS_PER_MICRO),
            bytes_accessed=int(micros * BYTES_PER_MICRO),
            transcendentals=0,
        ),
    )(scalars, *ins)


def dots_pairs(group, slots):
    return [(s, a, b) for s in range(slots) for a in range(group) for b in range(group) if s or b <= a]


def dots_kernel(scalars, second, *refs):
    passed, (out, held) = refs[:-2], refs[-2:]
    group, rows, y, z = second.shape
    chunks, cols = y // SUB, z // LANES
    pairs = dots_pairs(group, len(passed))
    at_step = pl.program_id(0)

    @pl.when(at_step == 0)
    def _():
        held[...] = jnp.zeros(held.shape, jnp.float32)

    def body(i, sums):
        sums = list(sums)
        for c in range(chunks):
            for j in range(cols):
                at = (pl.ds(SUB * c, SUB), pl.ds(LANES * j, LANES))
                mine = [passed[0][a, i, *at] for a in range(group)]
                then = [second[a, i, *at] for a in range(group)]
                other = {(s, b): passed[s][b, i, *at] for s in range(1, len(passed)) for b in range(group)}
                for n, (s, a, b) in enumerate(pairs):
                    value = other[s, b] if s else mine[b]
                    sums[2 * n] = sums[2 * n] + mine[a] * value
                    sums[2 * n + 1] = sums[2 * n + 1] + then[a] * value
        return tuple(sums)

    sums = lax.fori_loop(0, rows, body, tuple(held[n] for n in range(2 * len(pairs))))
    for n, value in enumerate(sums):
        held[n] = value

    @pl.when(at_step == pl.num_programs(0) - 1)
    def _():
        me = scalars[1]
        count = out.shape[0]
        row = lax.broadcasted_iota(jnp.int32, out.shape, 0)
        lane = lax.broadcasted_iota(jnp.int32, out.shape, 1)
        total = jnp.zeros(out.shape, jnp.float32)
        for n, (s, a, b) in enumerate(pairs):
            for k in range(2):
                value = jnp.sum(jnp.sum(sums[2 * n + k], axis=0, keepdims=True), axis=1, keepdims=True)
                column = (me - s) * group + b + k * count
                here = (row == me * group + a) & (lane == column) & (me >= s)
                total = total + jnp.where(here, value, 0.0)
        out[...] = total


def basis_kernel(inverse, *refs):
    images, out = refs[:-1], refs[-1]
    group, rows, y, z = out.shape
    factors = [[inverse[a, n] for n in range(group * len(images))] for a in range(group)]

    def body(i, carry):
        for c in range(y // SUB):
            for j in range(z // LANES):
                at = (pl.ds(SUB * c, SUB), pl.ds(LANES * j, LANES))
                values = [image[b, i, *at] for image in images for b in range(group)]
                for a in range(group):
                    terms = [factor * value for factor, value in zip(factors[a], values)]
                    while len(terms) > 1:
                        terms = [sum(terms[n : n + 2][1:], terms[n]) for n in range(0, len(terms), 2)]
                    out[a, i, *at] = terms[0]
        return carry

    lax.fori_loop(0, rows, body, None)


def all_sum(value):
    for axis in ("sx", "sy", "probe"):
        devices = lax.axis_size(axis)
        if devices & (devices - 1):
            value = lax.psum(value, axis)
            continue
        move = lambda bits: lax.ppermute(value, axis, [(i, i ^ bits) for i in range(devices)])
        bit = 1
        while bit < devices:
            if 4 * bit <= devices:
                value = (value + move(bit)) + (move(2 * bit) + move(3 * bit))
                bit *= 4
            else:
                value = value + move(bit)
                bit *= 2
    return value


def shards(probes, velocity, diffusivity, obs_weight):
    group, x, y, z = probes.shape
    groups = lax.axis_size("probe")
    count = group * groups
    ncells = x * y * z * lax.axis_size("sx") * lax.axis_size("sy")
    both = lax.axis_size("sy") != 2
    side, mine = lax.axis_index("sy"), lax.axis_index("probe")

    where = jnp.stack([side, mine]).astype(jnp.int32)
    wide = (x + 2 * STEPS, y + 2 * STEPS, z)
    tile = f32(group, x, y, z)
    strips2 = strip_shapes(group, x, y, z, both)
    fields = [diffusivity[None], velocity, probes]
    total = 4 + group

    def scratch(copies):
        return [
            pltpu.VMEM((7,) + wide, jnp.float32),
            pltpu.VMEM((group,) + wide, jnp.float32),
            pltpu.VMEM((group,) + wide, jnp.float32),
            pltpu.SemaphoreType.DMA((copies,)),
        ]

    packs = 2 if both else 1

    def pack(sources):
        number = sum(a.shape[0] for a in sources)
        return kernel_call(
            functools.partial(pack_kernel, len(sources)),
            strip_shapes(number, x, y, z, both),
            [pltpu.VMEM((packs, number, x, SUB, z), jnp.float32), pltpu.SemaphoreType.DMA((number * (packs + 2),))],
            [where] + sources,
            3.0,
            anywhere=range(1, len(sources) + 1),
        )

    def right(value, hops):
        return lax.ppermute(value, "probe", [(i, i + hops) for i in range(groups - hops)])

    next_probes = right(probes, 1)
    strips = pack(fields)
    received = exchange(strips)
    coef, halfway, *strips = kernel_call(
        functools.partial(first_kernel, len(received)),
        [f32(7, *wide), tile] + strips2,
        scratch(3 * total + 1),
        [where] + fields + [obs_weight] + received,
        14.0,
        anywhere=(1, 2, 3, 5, 6),
        outs_anywhere=(0,),
    )

    def model(field, received, adjoint, last=False):
        ins = [where, coef, field] + ([] if adjoint else [obs_weight])
        return kernel_call(
            functools.partial(next_kernel, len(received), adjoint),
            [tile] + ([] if last else strips2),
            scratch(3 * group + x // SUB + 1),
            ins + received,
            12.0,
            anywhere=(1, 2, len(ins), len(ins) + 1),
        )

    images, *strips = model(halfway, exchange(strips), True)
    far = [right(images, hops) for hops in range(3, groups)]

    half_next, *strips_next = model(next_probes, exchange(pack([next_probes])), False)
    strips, half_next = lax.optimization_barrier((strips, half_next))
    (images_next,) = model(half_next, exchange(strips_next), True, True)
    ready, (shifting, far) = images_next, lax.optimization_barrier((images_next, far))
    passed = [images, images_next, right(shifting, 1)] + far

    received, _ = lax.optimization_barrier((exchange(strips), ready))
    halfway, *strips = model(images, received, False)
    (second,) = model(halfway, exchange(strips), True, True)

    slots = len(passed)
    partial = blocked_call(
        dots_kernel,
        f32(count, LANES),
        False,
        [pltpu.VMEM((2 * len(dots_pairs(group, slots)), SUB, LANES), jnp.float32)],
        where,
        [second] + passed,
        5.0,
    )
    inner = all_sum(partial) / ncells
    strict = jnp.tril(jnp.ones((count, count), jnp.float32), -1)
    gram, ritz = inner[:, :count], inner[:, count : 2 * count]
    gram = gram + (gram * strict).T
    ritz = ritz + (ritz * strict).T
    lower = jnp.linalg.cholesky(gram)
    inverse = jax.scipy.linalg.solve_triangular(lower, jnp.eye(count, dtype=jnp.float32), lower=True)
    highest = lax.Precision.HIGHEST
    projected = jnp.dot(jnp.dot(inverse, ritz, precision=highest), inverse.T, precision=highest)

    rows = lax.dynamic_slice_in_dim(inverse, mine * group, group, 0)
    parts = []
    for n in range(groups):
        part = lax.dynamic_slice_in_dim(rows, jnp.maximum(mine - n, 0) * group, group, 1)
        parts.append(jnp.where(mine >= n, part, 0.0))
    basis = blocked_call(basis_kernel, tile, True, [], jnp.concatenate(parts, 1), passed, 4.0)
    return (basis, projected)


def solution(mesh):
    return jax.shard_map(
        shards,
        mesh=mesh,
        in_specs=(
            P("probe", "sx", "sy", None),
            P(None, "sx", "sy", None),
            P("sx", "sy", None),
            P("sx", "sy", None),
        ),
        out_specs=(P("probe", "sx", "sy", None), P()),
        check_vma=False,
    )
```

```python
import functools

import jax
import jax.numpy as jnp
from jax import lax
from jax.experimental import pallas as pl
from jax.experimental.pallas import tpu as pltpu
from jax.sharding import PartitionSpec as P

STEPS = 4
SUB = 8
LANES = 128
ROWS = 2
BLOCK = 4
MIB = 1024 * 1024
FLOPS_PER_MICRO = 1.15e9
BYTES_PER_MICRO = 3.6e6


def kernel_call(body, outs, scratch, ins, micros, mib, anywhere=(), outs_anywhere=()):
    spec = lambda n, names: pl.BlockSpec(memory_space=pl.ANY if n in names else pltpu.VMEM)
    specs = [spec(n, anywhere) for n in range(len(ins))]
    specs[0] = pl.BlockSpec(memory_space=pltpu.SMEM)
    return pl.pallas_call(
        body,
        out_shape=outs,
        in_specs=specs,
        out_specs=[spec(n, outs_anywhere) for n in range(len(outs))],
        scratch_shapes=scratch,
        compiler_params=pltpu.CompilerParams(vmem_limit_bytes=mib * MIB),
        cost_estimate=pl.CostEstimate(
            flops=int(micros * FLOPS_PER_MICRO),
            bytes_accessed=int(micros * BYTES_PER_MICRO),
            transcendentals=0,
        ),
    )(*ins)


def f32(*shape):
    return jax.ShapeDtypeStruct(shape, jnp.float32)


def strip_shapes(fields, x, y, z, both):
    packs = [f32(fields, x // 2, SUB, z), f32(fields, 2, SUB, z), f32(fields, 2, SUB, z)]
    return [f32(fields, STEPS, y, z)] * 2 + packs * (2 if both else 1)


def pack_starts(packs, y, side):
    if packs == 2:
        return [(0, False), (y - SUB, True)]
    return [(pl.multiple_of(jnp.where(side == 0, y - SUB, 0), SUB), side == 0)]


def packed_pair(row, first, second, last):
    hi = lambda: jnp.where(row < STEPS, pltpu.roll(first, STEPS, 0), second)
    lo = lambda: jnp.where(row < STEPS, first, pltpu.roll(second, STEPS, 0))
    if isinstance(last, bool):
        return hi() if last else lo()
    return jnp.where(last, hi(), lo())


def write_packs(field, n, rows, last, outs):
    pack, corner_lo, corner_hi = outs[2 + 3 * n : 5 + 3 * n]
    half, z = pack.shape[1], pack.shape[3]
    row = lax.broadcasted_iota(jnp.int32, (SUB, z), 0)

    def step(i, carry):
        pack[field, i] = packed_pair(row, rows(2 * i), rows(2 * i + 1), last)
        return carry

    lax.fori_loop(0, half, step, None, unroll=4)
    for i in range(2):
        corner_lo[field, i] = pack[field, i]
        corner_hi[field, i] = pack[field, half - 2 + i]


def write_strips(tile, outs, side):
    fields, x, y, _ = tile.shape
    for p in range(fields):
        for i in range(STEPS):
            outs[0][p, i] = tile[p, i]
            outs[1][p, i] = tile[p, x - STEPS + i]
        for n, (start, last) in enumerate(pack_starts((len(outs) - 2) // 3, y, side)):
            write_packs(p, n, lambda i: tile[p, i, pl.ds(start, SUB)], last, outs)


def exchange(strips):
    nx, ny = lax.axis_size("sx"), lax.axis_size("sy")
    up = [(i, i + 1) for i in range(nx - 1)]
    down = [(j, i) for i, j in up]

    def moved(value, dx, dys):
        pairs = []
        for i in range(nx):
            for j in range(ny):
                for dy in dys(j):
                    if 0 <= i + dx < nx and 0 <= j + dy < ny:
                        pairs.append((i * ny + j, (i + dx) * ny + j + dy))
        return lax.ppermute(value, ("sx", "sy"), pairs)

    below = lax.ppermute(strips[1], "sx", up)
    above = lax.ppermute(strips[0], "sx", down)
    received = [below, above]
    if len(strips) == 5:
        flip = lambda j: (1 - 2 * j,)
        pack, corner_lo, corner_hi = strips[2:]
        received += [moved(pack, 0, flip), moved(corner_hi, 1, flip), moved(corner_lo, -1, flip)]
    else:
        for n, dy in ((0, -1), (1, 1)):
            pack, corner_lo, corner_hi = strips[2 + 3 * n : 5 + 3 * n]
            one = lambda j, dy=dy: (dy,)
            received += [moved(pack, 0, one), moved(corner_hi, 1, one), moved(corner_lo, -1, one)]
    return received


class Copies:
    def __init__(self, sems):
        self.sems, self.open, self.used = sems, [], 0

    def start(self, src, dst):
        copy = pltpu.make_async_copy(src, dst, self.sems.at[self.used])
        self.used += 1
        copy.start()
        self.open.append(copy)
        return copy

    def wait(self):
        for copy in self.open:
            copy.wait()
        self.open = []


def start_widening(copies, dst, tile, field, received):
    x, y = tile.shape[0], tile.shape[1]
    copies.start(tile, dst.at[pl.ds(0, x), pl.ds(0, y)])
    copies.start(received[1].at[field], dst.at[pl.ds(x, STEPS), pl.ds(0, y)])
    copies.start(received[0].at[field], dst.at[pl.ds(x + STEPS, STEPS), pl.ds(0, y)])


def widen_rows(dst, field, received, side):
    half, z = received[2].shape[1], received[2].shape[3]
    x, y = 2 * half, dst.shape[1] - SUB
    row = lax.broadcasted_iota(jnp.int32, (SUB, z), 0)
    both = len(received) > 5

    def put(at, packs):
        if both:
            hi, lo = packs
        else:
            hi = jnp.where(side == 0, packs[0], 0.0)
            lo = jnp.where(side == 0, 0.0, packs[0])
        dst[at, y : y + SUB] = jnp.where(row < STEPS, hi, pltpu.roll(lo, STEPS, 0))
        dst[at + 1, y : y + SUB] = jnp.where(row < STEPS, pltpu.roll(hi, STEPS, 0), lo)

    groups = [received[2:5]] + ([received[5:8]] if both else [])

    def main(i, carry):
        put(2 * i, [g[0][field, i] for g in groups])
        return carry

    lax.fori_loop(0, half, main, None, unroll=4)
    for i in range(2):
        put(x + 2 * i, [g[2][field, i] for g in groups])
        put(x + STEPS + 2 * i, [g[1][field, i] for g in groups])


def coefficient_rows(coef):
    _, wide, rows, z = coef.shape
    lane = lax.broadcasted_iota(jnp.int32, (SUB, z), 1)

    def row(i, carry):
        for c in range(rows // SUB):
            at = pl.ds(SUB * c, SUB)
            spread = coef[0, i, at]
            values = [1.0 - 6.0 * spread]
            for d in range(3):
                half = 0.5 * coef[1 + 2 * d, i, at]
                plus, minus = spread - half, spread + half
                if d == 2:
                    plus = jnp.where(lane == z - 1, 0.0, plus)
                    minus = jnp.where(lane == 0, 0.0, minus)
                values += [plus, minus]
            for s, value in enumerate(values):
                coef[s, i, at] = value
        return carry

    lax.fori_loop(0, wide, row, None)


def sweep(coef, src, first, stop, adjoint, done, write):
    fields, wide, rows, z = src.shape
    chunks, cols = rows // SUB, z // LANES
    sub = lax.broadcasted_iota(jnp.int32, (SUB, LANES), 0)
    lane = lax.broadcasted_iota(jnp.int32, (SUB, LANES), 1)
    first_row, last_row = sub == 0, sub == SUB - 1
    first_lane, last_lane = lane == 0, lane == LANES - 1

    def piece(ref, lead, xi, c, j):
        return ref[lead, xi, SUB * c : SUB * (c + 1), LANES * j : LANES * (j + 1)]

    def body(pair, carry):
        wrap = lambda a: jnp.where(a < 0, a + wide, a)
        base = first + ROWS * pair
        at = [wrap(base + d) for d in range(-1, ROWS + 1)]
        kept = {}

        def load(ref, lead, r, c, j):
            key = (ref is coef, lead, r, c % chunks, j)
            if key not in kept:
                kept[key] = piece(ref, lead, at[r + 1], c % chunks, j)
            return kept[key]

        def scaled(slot, p, r, c, j):
            u = load(src, p, r, c, j)
            return load(coef, slot, r, c, j) * u if adjoint else u

        def turned(slot, shift, p, r, c, j):
            key = ("turned", slot, p, r, c % chunks, j)
            if key not in kept:
                kept[key] = pltpu.roll(scaled(slot, p, r, c, j), shift, 0)
            return kept[key]

        for c in range(done):
            results = []
            for r in range(ROWS):
                plus, minus = {}, {}
                for j in range(cols):
                    for p in range(fields):
                        plus[p, j] = pltpu.roll(scaled(6, p, r, c, j), LANES - 1, 1)
                        minus[p, j] = pltpu.roll(scaled(5, p, r, c, j), 1, 1)
                for j in range(cols):
                    for p in range(fields):
                        u, xp, xm = (load(src, p, r + d, c, j) for d in (0, 1, -1))
                        yp = jnp.where(last_row, turned(4, SUB - 1, p, r, c + 1, j), turned(4, SUB - 1, p, r, c, j))
                        ym = jnp.where(first_row, turned(3, 1, p, r, c - 1, j), turned(3, 1, p, r, c, j))
                        zp = jnp.where(last_lane, plus[p, (j + 1) % cols], plus[p, j])
                        zm = jnp.where(first_lane, minus[p, (j - 1) % cols], minus[p, j])
                        if adjoint:
                            xs = load(coef, 2, r + 1, c, j) * xp + load(coef, 1, r - 1, c, j) * xm
                            ys, zs = yp + ym, zp + zm
                        else:
                            xs = load(coef, 1, r, c, j) * xp + load(coef, 2, r, c, j) * xm
                            ys = load(coef, 3, r, c, j) * yp + load(coef, 4, r, c, j) * ym
                            zs = load(coef, 5, r, c, j) * zp + load(coef, 6, r, c, j) * zm
                        value = (load(coef, 0, r, c, j) * u + xs) + (ys + zs)
                        results.append((p, at[r + 1], c, j, value))
            for result in results:
                write(*result)
        return carry

    lax.fori_loop(0, (stop - first) // ROWS, body, None)


def run_steps(coef, states, out, adjoint, weight=None):
    x, tile_rows = out.shape[1], out.shape[2]
    for step in range(STEPS):
        src, dst = states[step % 2], states[(step + 1) % 2]
        last = step == STEPS - 1

        def write(p, i, c, j, value):
            at = (pl.ds(SUB * c, SUB), pl.ds(LANES * j, LANES))
            if last:
                out[p, i, *at] = value if weight is None else weight[i, *at] * value
            else:
                dst[p, i, *at] = value

        done = (tile_rows if last else src.shape[2]) // SUB
        reach = STEPS - 1 - step
        sweep(coef, src, -reach, x + reach, adjoint, done, write)


def pack_kernel(fields_in, scalars, *refs):
    sources, outs, (buffers, sems) = refs[:fields_in], refs[fields_in:-2], refs[-2:]
    side = scalars[0]
    tiles = [ref.at[n] for ref in sources for n in range(ref.shape[0])]
    x, y, _ = tiles[0].shape
    starts = pack_starts((len(outs) - 2) // 3, y, side)
    copies = Copies(sems)
    for f, tile in enumerate(tiles):
        for n, (start, _) in enumerate(starts):
            copies.start(tile.at[:, pl.ds(start, SUB)], buffers.at[n, f])
    loads, copies.open = copies.open, []
    for f, tile in enumerate(tiles):
        copies.start(tile.at[pl.ds(0, STEPS)], outs[0].at[f])
        copies.start(tile.at[pl.ds(x - STEPS, STEPS)], outs[1].at[f])
    for f in range(len(tiles)):
        for n, (_, last) in enumerate(starts):
            loads[f * len(starts) + n].wait()
            write_packs(f, n, lambda i: buffers[n, f, i], last, outs)
    copies.wait()


def first_kernel(count, scalars, diffusivity, velocity, probes, weight, *refs):
    side = scalars[0]
    received, coef, out = refs[:count], refs[count], refs[count + 1]
    strips, (state, other, sems) = refs[count + 2 : -3], refs[-3:]
    copies = Copies(sems)
    tiles = [diffusivity.at[0]] + [velocity.at[d] for d in range(3)]
    slots = [coef.at[s] for s in (0, 1, 3, 5)]
    for p in range(probes.shape[0]):
        tiles.append(probes.at[p])
        slots.append(state.at[p])
    for f, (tile, slot) in enumerate(zip(tiles, slots)):
        start_widening(copies, slot, tile, f, received)
    for f, slot in enumerate(slots):
        widen_rows(slot, f, received, side)
    copies.wait()
    coefficient_rows(coef)
    run_steps(coef, (state, other), out, False, weight)
    write_strips(out, strips, side)


def next_kernel(count, adjoint, scalars, coef, tile, *refs):
    side = scalars[0]
    weight = None if adjoint else refs[0]
    refs = refs if adjoint else refs[1:]
    received, out = refs[:count], refs[count]
    strips, (state, other, sems) = refs[count + 1 : -3], refs[-3:]
    fields = tile.shape[0]
    copies = Copies(sems)
    for p in range(fields):
        start_widening(copies, state.at[p], tile.at[p], p, received)
    for p in range(fields):
        widen_rows(state.at[p], p, received, side)
    copies.wait()
    run_steps(coef, (state, other), out, adjoint, weight)
    if strips:
        write_strips(out, strips, side)


def blocked_call(body, out_shape, out_block, scratch, scalars, ins, micros):
    group, x, y, z = ins[0].shape
    block = pl.BlockSpec((group, BLOCK, y, z), lambda i: (0, i, 0, 0))
    out = block if out_block else pl.BlockSpec(out_shape.shape, lambda i: (0, 0))
    return pl.pallas_call(
        body,
        grid=(x // BLOCK,),
        out_shape=out_shape,
        in_specs=[pl.BlockSpec(memory_space=pltpu.SMEM)] + [block] * len(ins),
        out_specs=out,
        scratch_shapes=scratch,
        compiler_params=pltpu.CompilerParams(vmem_limit_bytes=12 * MIB),
        cost_estimate=pl.CostEstimate(
            flops=int(micros * FLOPS_PER_MICRO),
            bytes_accessed=int(micros * BYTES_PER_MICRO),
            transcendentals=0,
        ),
    )(scalars, *ins)


def dots_pairs(group, slots):
    return [(s, a, b) for s in range(slots) for a in range(group) for b in range(group) if s or b <= a]


def dots_kernel(scalars, second, *refs):
    passed, (out, held) = refs[:-2], refs[-2:]
    group, rows, y, z = second.shape
    chunks, cols = y // SUB, z // LANES
    pairs = dots_pairs(group, len(passed))
    at_step = pl.program_id(0)

    @pl.when(at_step == 0)
    def _():
        held[...] = jnp.zeros(held.shape, jnp.float32)

    def body(i, sums):
        sums = list(sums)
        for c in range(chunks):
            for j in range(cols):
                at = (pl.ds(SUB * c, SUB), pl.ds(LANES * j, LANES))
                mine = [passed[0][a, i, *at] for a in range(group)]
                then = [second[a, i, *at] for a in range(group)]
                other = {(s, b): passed[s][b, i, *at] for s in range(1, len(passed)) for b in range(group)}
                for n, (s, a, b) in enumerate(pairs):
                    value = other[s, b] if s else mine[b]
                    sums[2 * n] = sums[2 * n] + mine[a] * value
                    sums[2 * n + 1] = sums[2 * n + 1] + then[a] * value
        return tuple(sums)

    sums = lax.fori_loop(0, rows, body, tuple(held[n] for n in range(2 * len(pairs))))
    for n, value in enumerate(sums):
        held[n] = value

    @pl.when(at_step == pl.num_programs(0) - 1)
    def _():
        me = scalars[1]
        count = out.shape[0]
        row = lax.broadcasted_iota(jnp.int32, out.shape, 0)
        lane = lax.broadcasted_iota(jnp.int32, out.shape, 1)
        total = jnp.zeros(out.shape, jnp.float32)
        for n, (s, a, b) in enumerate(pairs):
            for k in range(2):
                value = jnp.sum(jnp.sum(sums[2 * n + k], axis=0, keepdims=True), axis=1, keepdims=True)
                column = (me - s) * group + b + k * count
                here = (row == me * group + a) & (lane == column) & (me >= s)
                total = total + jnp.where(here, value, 0.0)
        out[...] = total


def basis_kernel(inverse, *refs):
    images, out = refs[:-1], refs[-1]
    group, rows, y, z = out.shape
    factors = [[inverse[a, n] for n in range(group * len(images))] for a in range(group)]

    def body(i, carry):
        for c in range(y // SUB):
            for j in range(z // LANES):
                at = (pl.ds(SUB * c, SUB), pl.ds(LANES * j, LANES))
                values = [image[b, i, *at] for image in images for b in range(group)]
                for a in range(group):
                    terms = [factor * value for factor, value in zip(factors[a], values)]
                    while len(terms) > 1:
                        terms = [sum(terms[n : n + 2][1:], terms[n]) for n in range(0, len(terms), 2)]
                    out[a, i, *at] = terms[0]
        return carry

    lax.fori_loop(0, rows, body, None)


def all_sum(value):
    for axis in ("sx", "sy", "probe"):
        devices = lax.axis_size(axis)
        if devices & (devices - 1):
            value = lax.psum(value, axis)
            continue
        move = lambda bits: lax.ppermute(value, axis, [(i, i ^ bits) for i in range(devices)])
        bit = 1
        while bit < devices:
            if 4 * bit <= devices:
                value = (value + move(bit)) + (move(2 * bit) + move(3 * bit))
                bit *= 4
            else:
                value = value + move(bit)
                bit *= 2
    return value


def shards(probes, velocity, diffusivity, obs_weight):
    group, x, y, z = probes.shape
    groups = lax.axis_size("probe")
    count = group * groups
    ncells = x * y * z * lax.axis_size("sx") * lax.axis_size("sy")
    both = lax.axis_size("sy") != 2
    side, mine = lax.axis_index("sy"), lax.axis_index("probe")

    where = jnp.stack([side, mine]).astype(jnp.int32)
    wide = (x + 2 * STEPS, y + 2 * STEPS, z)
    tile = f32(group, x, y, z)
    strips2 = strip_shapes(group, x, y, z, both)
    fields = [diffusivity[None], velocity, probes]
    total = 4 + group

    def scratch(copies):
        return [
            pltpu.VMEM((group,) + wide, jnp.float32),
            pltpu.VMEM((group,) + wide, jnp.float32),
            pltpu.SemaphoreType.DMA((copies,)),
        ]

    packs = 2 if both else 1

    def pack(sources):
        number = sum(a.shape[0] for a in sources)
        return kernel_call(
            functools.partial(pack_kernel, len(sources)),
            strip_shapes(number, x, y, z, both),
            [pltpu.VMEM((packs, number, x, SUB, z), jnp.float32), pltpu.SemaphoreType.DMA((number * (packs + 2),))],
            [where] + sources,
            3.0,
            12,
            anywhere=range(1, len(sources) + 1),
        )

    def right(value, hops):
        return lax.ppermute(value, "probe", [(i, i + hops) for i in range(groups - hops)])

    next_probes = right(probes, 1)
    strips = pack(fields)
    received = exchange(strips)
    coef, halfway, *strips = kernel_call(
        functools.partial(first_kernel, len(received)),
        [f32(7, *wide), tile] + strips2,
        scratch(3 * total),
        [where] + fields + [obs_weight] + received,
        14.0,
        14,
        anywhere=(1, 2, 3, 5, 6),
    )

    def model(field, received, adjoint, last=False):
        ins = [where, coef, field] + ([] if adjoint else [obs_weight])
        return kernel_call(
            functools.partial(next_kernel, len(received), adjoint),
            [tile] + ([] if last else strips2),
            scratch(3 * group),
            ins + received,
            12.0,
            14,
            anywhere=(2, len(ins), len(ins) + 1),
        )

    images, *strips = model(halfway, exchange(strips), True)
    far = [right(images, hops) for hops in range(3, groups)]

    half_next, *strips_next = model(next_probes, exchange(pack([next_probes])), False)
    strips, half_next = lax.optimization_barrier((strips, half_next))
    (images_next,) = model(half_next, exchange(strips_next), True, True)
    ready, (shifting, far) = images_next, lax.optimization_barrier((images_next, far))
    passed = [images, images_next, right(shifting, 1)] + far

    received, _ = lax.optimization_barrier((exchange(strips), ready))
    halfway, *strips = model(images, received, False)
    (second,) = model(halfway, exchange(strips), True, True)

    slots = len(passed)
    partial = blocked_call(
        dots_kernel,
        f32(count, LANES),
        False,
        [pltpu.VMEM((2 * len(dots_pairs(group, slots)), SUB, LANES), jnp.float32)],
        where,
        [second] + passed,
        5.0,
    )
    inner = all_sum(partial) / ncells
    strict = jnp.tril(jnp.ones((count, count), jnp.float32), -1)
    gram, ritz = inner[:, :count], inner[:, count : 2 * count]
    gram = gram + (gram * strict).T
    ritz = ritz + (ritz * strict).T
    lower = jnp.linalg.cholesky(gram)
    inverse = jax.scipy.linalg.solve_triangular(lower, jnp.eye(count, dtype=jnp.float32), lower=True)
    highest = lax.Precision.HIGHEST
    projected = jnp.dot(jnp.dot(inverse, ritz, precision=highest), inverse.T, precision=highest)

    rows = lax.dynamic_slice_in_dim(inverse, mine * group, group, 0)
    parts = []
    for n in range(groups):
        part = lax.dynamic_slice_in_dim(rows, jnp.maximum(mine - n, 0) * group, group, 1)
        parts.append(jnp.where(mine >= n, part, 0.0))
    basis = blocked_call(basis_kernel, tile, True, [], jnp.concatenate(parts, 1), passed, 4.0)
    return (basis, projected)


def solution(mesh):
    return jax.shard_map(
        shards,
        mesh=mesh,
        in_specs=(
            P("probe", "sx", "sy", None),
            P(None, "sx", "sy", None),
            P("sx", "sy", None),
            P("sx", "sy", None),
        ),
        out_specs=(P("probe", "sx", "sy", None), P()),
        check_vma=False,
    )
```

```python
import functools

import jax
import jax.numpy as jnp
from jax import lax
from jax.experimental import pallas as pl
from jax.experimental.pallas import tpu as pltpu
from jax.sharding import PartitionSpec as P

STEPS = 4
SUB = 8
LANES = 128
ROWS = 2
MIB = 1024 * 1024
FLOPS_PER_MICRO = 1.15e9
BYTES_PER_MICRO = 3.6e6


def kernel_call(body, outs, scratch, ins, micros, mib, anywhere=(), outs_anywhere=(), space=pl.ANY, scalars=True):
    spec = lambda n, names: pl.BlockSpec(memory_space=space if n in names else pltpu.VMEM)
    specs = [spec(n, anywhere) for n in range(len(ins))]
    if scalars:
        specs[0] = pl.BlockSpec(memory_space=pltpu.SMEM)
    return pl.pallas_call(
        body,
        out_shape=outs,
        in_specs=specs,
        out_specs=[spec(n, outs_anywhere) for n in range(len(outs))],
        scratch_shapes=scratch,
        compiler_params=pltpu.CompilerParams(vmem_limit_bytes=mib * MIB),
        cost_estimate=pl.CostEstimate(
            flops=int(micros * FLOPS_PER_MICRO),
            bytes_accessed=int(micros * BYTES_PER_MICRO),
            transcendentals=0,
        ),
    )(*ins)


def f32(*shape):
    return jax.ShapeDtypeStruct(shape, jnp.float32)


def strip_shapes(fields, x, y, z, both, joined=False):
    packs = [f32(fields, x // 2, SUB, z)] + [f32(fields, 2, SUB, z)] * (0 if joined else 2)
    return [f32(fields, STEPS, y, z)] * 2 + packs * (2 if both else 1)


def pack_starts(packs, y, side):
    if packs == 2:
        return [(0, False), (y - SUB, True)]
    return [(pl.multiple_of(jnp.where(side == 0, y - SUB, 0), SUB), side == 0)]


def packed_pair(row, first, second, last):
    hi = lambda: jnp.where(row < STEPS, pltpu.roll(first, STEPS, 0), second)
    lo = lambda: jnp.where(row < STEPS, first, pltpu.roll(second, STEPS, 0))
    if isinstance(last, bool):
        return hi() if last else lo()
    return jnp.where(last, hi(), lo())


def write_packs(field, n, rows, last, outs):
    pack, *corners = outs[2 + 3 * n : 5 + 3 * n]
    half, z = pack.shape[1], pack.shape[3]
    row = lax.broadcasted_iota(jnp.int32, (SUB, z), 0)

    def step(i, carry):
        pack[field, i] = packed_pair(row, rows(2 * i), rows(2 * i + 1), last)
        return carry

    lax.fori_loop(0, half, step, None, unroll=4)
    for corner, start in zip(corners, (0, half - 2)):
        for i in range(2):
            corner[field, i] = pack[field, start + i]


def write_strips(tile, outs, side):
    fields, x, y, _ = tile.shape
    for p in range(fields):
        for i in range(STEPS):
            outs[0][p, i] = tile[p, i]
            outs[1][p, i] = tile[p, x - STEPS + i]
        for n, (start, last) in enumerate(pack_starts(max((len(outs) - 2) // 3, 1), y, side)):
            write_packs(p, n, lambda i: tile[p, i, pl.ds(start, SUB)], last, outs)


def join_kernel(xlo, xhi, pack, lo, hi):
    fields, steps, y, _ = xlo.shape
    chunks, half = y // SUB, pack.shape[1]
    for f in range(fields):
        for strip, out, start in ((xlo, lo, 0), (xhi, hi, half - 2)):
            for i in range(steps):
                for c in range(chunks):
                    out[f, i * chunks + c] = strip[f, i, SUB * c : SUB * (c + 1)]
            for i in range(2):
                out[f, steps * chunks + i] = pack[f, start + i]


def join(xlo, xhi, pack):
    fields, steps, y, z = xlo.shape
    out = f32(fields, steps * y // SUB + 2, SUB, z)
    return kernel_call(join_kernel, [out, out], [], [xlo, xhi, pack], 1.0, 8, scalars=False)


def exchange(strips):
    nx, ny = lax.axis_size("sx"), lax.axis_size("sy")
    up = [(i, i + 1) for i in range(nx - 1)]
    down = [(j, i) for i, j in up]

    def moved(value, dx, dys):
        pairs = []
        for i in range(nx):
            for j in range(ny):
                for dy in dys(j):
                    if 0 <= i + dx < nx and 0 <= j + dy < ny:
                        pairs.append((i * ny + j, (i + dx) * ny + j + dy))
        return lax.ppermute(value, ("sx", "sy"), pairs)

    if len(strips) == 3:
        pack = moved(strips[2], 0, lambda j: (1 - 2 * j,))
        lo, hi = join(strips[0], strips[1], pack)
        return [lax.ppermute(hi, "sx", up), lax.ppermute(lo, "sx", down), pack]
    below = lax.ppermute(strips[1], "sx", up)
    above = lax.ppermute(strips[0], "sx", down)
    received = [below, above]
    if len(strips) == 5:
        flip = lambda j: (1 - 2 * j,)
        pack, corner_lo, corner_hi = strips[2:]
        received += [moved(pack, 0, flip), moved(corner_hi, 1, flip), moved(corner_lo, -1, flip)]
    else:
        for n, dy in ((0, -1), (1, 1)):
            pack, corner_lo, corner_hi = strips[2 + 3 * n : 5 + 3 * n]
            one = lambda j, dy=dy: (dy,)
            received += [moved(pack, 0, one), moved(corner_hi, 1, one), moved(corner_lo, -1, one)]
    return received


class Copies:
    def __init__(self, sems):
        self.sems, self.open, self.used = sems, [], 0

    def start(self, src, dst):
        copy = pltpu.make_async_copy(src, dst, self.sems.at[self.used])
        self.used += 1
        copy.start()
        self.open.append(copy)
        return copy

    def wait(self):
        for copy in self.open:
            copy.wait()
        self.open = []


def start_widening(copies, dst, tile, field, received):
    x, y = tile.shape[0], tile.shape[1]
    copies.start(tile, dst.at[pl.ds(0, x), pl.ds(0, y)])
    if len(received) == 3:
        return
    copies.start(received[1].at[field], dst.at[pl.ds(x, STEPS), pl.ds(0, y)])
    copies.start(received[0].at[field], dst.at[pl.ds(x + STEPS, STEPS), pl.ds(0, y)])


def widen_rows(dst, field, received, side):
    half, z = received[2].shape[1], received[2].shape[3]
    x, y = 2 * half, dst.shape[1] - SUB
    row = lax.broadcasted_iota(jnp.int32, (SUB, z), 0)
    both = len(received) > 5

    def put(at, packs):
        if both:
            hi, lo = packs
        else:
            hi = jnp.where(side == 0, packs[0], 0.0)
            lo = jnp.where(side == 0, 0.0, packs[0])
        dst[at, y : y + SUB] = jnp.where(row < STEPS, hi, pltpu.roll(lo, STEPS, 0))
        dst[at + 1, y : y + SUB] = jnp.where(row < STEPS, pltpu.roll(hi, STEPS, 0), lo)

    groups = [received[2:5]] + ([received[5:8]] if both else [])
    first = 0
    if len(received) == 3:
        below, above, pack = received
        groups = [[pack, below, above]]
        first = STEPS * y // SUB
        for strip, at in ((above, x), (below, x + STEPS)):
            for i in range(STEPS):
                for c in range(y // SUB):
                    dst[at + i, SUB * c : SUB * (c + 1)] = strip[field, i * (y // SUB) + c]

    def main(i, carry):
        put(2 * i, [g[0][field, i] for g in groups])
        return carry

    lax.fori_loop(0, half, main, None, unroll=4)
    for i in range(2):
        put(x + 2 * i, [g[2][field, first + i] for g in groups])
        put(x + STEPS + 2 * i, [g[1][field, first + i] for g in groups])


def coefficient_rows(coef):
    _, wide, rows, z = coef.shape
    lane = lax.broadcasted_iota(jnp.int32, (SUB, z), 1)

    def row(i, carry):
        for c in range(rows // SUB):
            at = pl.ds(SUB * c, SUB)
            spread = coef[0, i, at]
            values = [1.0 - 6.0 * spread]
            for d in range(3):
                half = 0.5 * coef[1 + 2 * d, i, at]
                plus, minus = spread - half, spread + half
                if d == 2:
                    plus = jnp.where(lane == z - 1, 0.0, plus)
                    minus = jnp.where(lane == 0, 0.0, minus)
                values += [plus, minus]
            for s, value in enumerate(values):
                coef[s, i, at] = value
        return carry

    lax.fori_loop(0, wide, row, None)


def sweep(coef, src, first, stop, adjoint, done, write):
    fields, wide, rows, z = src.shape
    chunks, cols = rows // SUB, z // LANES
    sub = lax.broadcasted_iota(jnp.int32, (SUB, LANES), 0)
    lane = lax.broadcasted_iota(jnp.int32, (SUB, LANES), 1)
    first_row, last_row = sub == 0, sub == SUB - 1
    first_lane, last_lane = lane == 0, lane == LANES - 1

    def piece(ref, lead, xi, c, j):
        return ref[lead, xi, SUB * c : SUB * (c + 1), LANES * j : LANES * (j + 1)]

    def body(pair, carry):
        wrap = lambda a: jnp.where(a < 0, a + wide, a)
        base = first + ROWS * pair
        at = [wrap(base + d) for d in range(-1, ROWS + 1)]
        kept = {}

        def load(ref, lead, r, c, j):
            key = (ref is coef, lead, r, c % chunks, j)
            if key not in kept:
                kept[key] = piece(ref, lead, at[r + 1], c % chunks, j)
            return kept[key]

        def scaled(slot, p, r, c, j):
            u = load(src, p, r, c, j)
            return load(coef, slot, r, c, j) * u if adjoint else u

        def turned(slot, shift, p, r, c, j):
            key = ("turned", slot, p, r, c % chunks, j)
            if key not in kept:
                kept[key] = pltpu.roll(scaled(slot, p, r, c, j), shift, 0)
            return kept[key]

        for c in range(done):
            results = []
            for r in range(ROWS):
                plus, minus = {}, {}
                for j in range(cols):
                    for p in range(fields):
                        plus[p, j] = pltpu.roll(scaled(6, p, r, c, j), LANES - 1, 1)
                        minus[p, j] = pltpu.roll(scaled(5, p, r, c, j), 1, 1)
                for j in range(cols):
                    for p in range(fields):
                        u, xp, xm = (load(src, p, r + d, c, j) for d in (0, 1, -1))
                        yp = jnp.where(last_row, turned(4, SUB - 1, p, r, c + 1, j), turned(4, SUB - 1, p, r, c, j))
                        ym = jnp.where(first_row, turned(3, 1, p, r, c - 1, j), turned(3, 1, p, r, c, j))
                        zp = jnp.where(last_lane, plus[p, (j + 1) % cols], plus[p, j])
                        zm = jnp.where(first_lane, minus[p, (j - 1) % cols], minus[p, j])
                        if adjoint:
                            xs = load(coef, 2, r + 1, c, j) * xp + load(coef, 1, r - 1, c, j) * xm
                            ys, zs = yp + ym, zp + zm
                        else:
                            xs = load(coef, 1, r, c, j) * xp + load(coef, 2, r, c, j) * xm
                            ys = load(coef, 3, r, c, j) * yp + load(coef, 4, r, c, j) * ym
                            zs = load(coef, 5, r, c, j) * zp + load(coef, 6, r, c, j) * zm
                        value = (load(coef, 0, r, c, j) * u + xs) + (ys + zs)
                        results.append((p, at[r + 1], c, j, value))
            for result in results:
                write(*result)
        return carry

    lax.fori_loop(0, (stop - first) // ROWS, body, None)


def run_steps(coef, states, out, adjoint, weight=None):
    x, tile_rows = out.shape[1], out.shape[2]
    for step in range(STEPS):
        src, dst = states[step % 2], states[(step + 1) % 2]
        last = step == STEPS - 1

        def write(p, i, c, j, value):
            at = (pl.ds(SUB * c, SUB), pl.ds(LANES * j, LANES))
            if last:
                out[p, i, *at] = value if weight is None else weight[i, *at] * value
            else:
                dst[p, i, *at] = value

        done = (tile_rows if last else src.shape[2]) // SUB
        reach = STEPS - 1 - step
        sweep(coef, src, -reach, x + reach, adjoint, done, write)


def pack_kernel(fields_in, scalars, *refs):
    sources, outs, (buffers, sems) = refs[:fields_in], refs[fields_in:-2], refs[-2:]
    side = scalars[0]
    tiles = [ref.at[n] for ref in sources for n in range(ref.shape[0])]
    x, y, _ = tiles[0].shape
    starts = pack_starts(max((len(outs) - 2) // 3, 1), y, side)
    copies = Copies(sems)
    for f, tile in enumerate(tiles):
        for n, (start, _) in enumerate(starts):
            copies.start(tile.at[:, pl.ds(start, SUB)], buffers.at[n, f])
    loads, copies.open = copies.open, []
    for f, tile in enumerate(tiles):
        copies.start(tile.at[pl.ds(0, STEPS)], outs[0].at[f])
        copies.start(tile.at[pl.ds(x - STEPS, STEPS)], outs[1].at[f])
    for f in range(len(tiles)):
        for n, (_, last) in enumerate(starts):
            loads[f * len(starts) + n].wait()
            write_packs(f, n, lambda i: buffers[n, f, i], last, outs)
    copies.wait()


def first_kernel(count, scalars, diffusivity, velocity, probes, weight, *refs):
    side = scalars[0]
    received, coef, out = refs[:count], refs[count], refs[count + 1]
    strips, (state, other, sems) = refs[count + 2 : -3], refs[-3:]
    copies = Copies(sems)
    tiles = [diffusivity.at[0]] + [velocity.at[d] for d in range(3)]
    slots = [coef.at[s] for s in (0, 1, 3, 5)]
    for p in range(probes.shape[0]):
        tiles.append(probes.at[p])
        slots.append(state.at[p])
    for f, (tile, slot) in enumerate(zip(tiles, slots)):
        start_widening(copies, slot, tile, f, received)
    for f, slot in enumerate(slots):
        widen_rows(slot, f, received, side)
    copies.wait()
    coefficient_rows(coef)
    run_steps(coef, (state, other), out, False, weight)
    write_strips(out, strips, side)


def next_kernel(count, adjoint, scalars, coef, tile, *refs):
    side = scalars[0]
    weight = None if adjoint else refs[0]
    refs = refs if adjoint else refs[1:]
    received, out = refs[:count], refs[count]
    strips, (state, other, sems) = refs[count + 1 : -3], refs[-3:]
    fields = tile.shape[0]
    copies = Copies(sems)
    for p in range(fields):
        start_widening(copies, state.at[p], tile.at[p], p, received)
    for p in range(fields):
        widen_rows(state.at[p], p, received, side)
    copies.wait()
    run_steps(coef, (state, other), out, adjoint, weight)
    if strips:
        write_strips(out, strips, side)


def dots_pairs(group, slots):
    return [(s, a, b) for s in range(slots) for a in range(group) for b in range(group) if s or b <= a]


def dots_kernel(scalars, second, *refs):
    passed, out = refs[:-1], refs[-1]
    group, rows, y, z = second.shape
    chunks, cols = y // SUB, z // LANES
    pairs = dots_pairs(group, len(passed))

    def body(i, sums):
        sums = list(sums)
        for c in range(chunks):
            for j in range(cols):
                at = (pl.ds(SUB * c, SUB), pl.ds(LANES * j, LANES))
                mine = [passed[0][a, i, *at] for a in range(group)]
                then = [second[a, i, *at] for a in range(group)]
                other = {(s, b): passed[s][b, i, *at] for s in range(1, len(passed)) for b in range(group)}
                for n, (s, a, b) in enumerate(pairs):
                    value = other[s, b] if s else mine[b]
                    sums[2 * n] = sums[2 * n] + mine[a] * value
                    sums[2 * n + 1] = sums[2 * n + 1] + then[a] * value
        return tuple(sums)

    zero = jnp.zeros((SUB, LANES), jnp.float32)
    sums = lax.fori_loop(0, rows, body, (zero,) * (2 * len(pairs)))
    me = scalars[1]
    count = out.shape[0]
    row = lax.broadcasted_iota(jnp.int32, out.shape, 0)
    lane = lax.broadcasted_iota(jnp.int32, out.shape, 1)
    total = jnp.zeros(out.shape, jnp.float32)
    for n, (s, a, b) in enumerate(pairs):
        for k in range(2):
            value = jnp.sum(jnp.sum(sums[2 * n + k], axis=0, keepdims=True), axis=1, keepdims=True)
            i, j = me * group + a, (me - s) * group + b
            here = (row == i) & (lane == j + k * count) | (row == j) & (lane == i + k * count)
            total = total + jnp.where(here & (me >= s), value, 0.0)
    out[...] = total


def finish_kernel(scale, scalars, inner, *refs):
    images, (basis, projected, held, sems) = refs[:-4], refs[-4:]
    group, x, y, z = held.shape
    count = inner.shape[0]
    me = scalars[1]
    row = lax.broadcasted_iota(jnp.int32, inner.shape, 0)
    lane = lax.broadcasted_iota(jnp.int32, inner.shape, 1)
    base = 2 * count
    work = jnp.where(lane == row + base, 1.0, inner[...] * scale)
    for k in range(count):
        column = jnp.broadcast_to(work[:, k : k + 1], inner.shape)
        pivot = jnp.broadcast_to(column[k : k + 1], inner.shape)
        line = jnp.broadcast_to(work[k : k + 1], inner.shape)
        work = work - jnp.where(row > k, column / pivot, 0.0) * line
    pivots = jnp.sum(jnp.where(lane == row, work, 0.0), axis=1, keepdims=True)
    work = work * (1.0 / jnp.sqrt(pivots))

    factors = []
    for a in range(group):
        factors.append([])
        for s in range(len(images)):
            for b in range(group):
                here = (row == me * group + a) & (lane == base + (me - s) * group + b) & (me >= s)
                value = jnp.sum(jnp.where(here, work, 0.0), axis=0, keepdims=True)
                value = jnp.sum(value, axis=1, keepdims=True)
                factors[a].append(jnp.broadcast_to(value, (SUB, LANES)))

    def body(i, carry):
        for c in range(y // SUB):
            for j in range(z // LANES):
                at = (pl.ds(SUB * c, SUB), pl.ds(LANES * j, LANES))
                values = [image[b, i, *at] for image in images for b in range(group)]
                for a in range(group):
                    terms = [factor * value for factor, value in zip(factors[a], values)]
                    while len(terms) > 1:
                        terms = [sum(terms[n : n + 2][1:], terms[n]) for n in range(0, len(terms), 2)]
                    held[a, i, *at] = terms[0]
        return carry

    copies = Copies(sems)
    for start in range(0, x, SUB):
        lax.fori_loop(start, start + SUB, body, None)
        for a in range(group):
            copies.start(held.at[a, pl.ds(start, SUB)], basis.at[a, pl.ds(start, SUB)])

    left = jnp.where((lane >= count) & (lane < base), work, 0.0)
    right = jnp.where((lane >= count) & (lane < base), pltpu.roll(work, LANES - count, 1), 0.0)
    projected[...] = lax.dot_general(
        left,
        right,
        (((1,), (1,)), ((), ())),
        precision=lax.Precision.HIGHEST,
        preferred_element_type=jnp.float32,
    )
    copies.wait()


def all_sum(value):
    for axis in ("sx", "sy", "probe"):
        devices = lax.axis_size(axis)
        if devices & (devices - 1):
            value = lax.psum(value, axis)
            continue
        move = lambda bits: lax.ppermute(value, axis, [(i, i ^ bits) for i in range(devices)])
        bit = 1
        while bit < devices:
            if 4 * bit <= devices:
                value = (value + move(bit)) + (move(2 * bit) + move(3 * bit))
                bit *= 4
            else:
                value = value + move(bit)
                bit *= 2
    return value


def shards(probes, velocity, diffusivity, obs_weight):
    group, x, y, z = probes.shape
    groups = lax.axis_size("probe")
    count = group * groups
    ncells = x * y * z * lax.axis_size("sx") * lax.axis_size("sy")
    both = lax.axis_size("sy") != 2
    side, mine = lax.axis_index("sy"), lax.axis_index("probe")

    where = jnp.stack([side, mine]).astype(jnp.int32)
    wide = (x + 2 * STEPS, y + 2 * STEPS, z)
    tile = f32(group, x, y, z)
    strips2 = strip_shapes(group, x, y, z, both, not both)
    fields = [diffusivity[None], velocity, probes]
    total = 4 + group

    def scratch(copies):
        return [
            pltpu.VMEM((group,) + wide, jnp.float32),
            pltpu.VMEM((group,) + wide, jnp.float32),
            pltpu.SemaphoreType.DMA((copies,)),
        ]

    packs = 2 if both else 1

    def pack(sources):
        number = sum(a.shape[0] for a in sources)
        joined = number == group and not both
        return kernel_call(
            functools.partial(pack_kernel, len(sources)),
            strip_shapes(number, x, y, z, both, joined),
            [pltpu.VMEM((packs, number, x, SUB, z), jnp.float32), pltpu.SemaphoreType.DMA((number * (packs + 2),))],
            [where] + sources,
            3.0,
            12,
            anywhere=range(1, len(sources) + 1),
            space=pl.ANY if joined else pltpu.HBM,
        )

    def right(value, hops):
        return lax.ppermute(value, "probe", [(i, i + hops) for i in range(groups - hops)])

    next_probes = right(probes, 1)
    strips = pack(fields)
    received = exchange(strips)
    coef, halfway, *strips = kernel_call(
        functools.partial(first_kernel, len(received)),
        [f32(7, *wide), tile] + strips2,
        scratch(3 * total),
        [where] + fields + [obs_weight] + received,
        14.0,
        14,
        anywhere=(1, 2, 3, 5, 6),
    )

    def model(field, received, adjoint, last=False):
        ins = [where, coef, field] + ([] if adjoint else [obs_weight])
        return kernel_call(
            functools.partial(next_kernel, len(received), adjoint),
            [tile] + ([] if last else strips2),
            scratch(3 * group),
            ins + received,
            12.0,
            14,
            anywhere=(2, len(ins), len(ins) + 1) if both else (2,),
        )

    images, *strips = model(halfway, exchange(strips), True)
    far = [right(images, hops) for hops in range(3, groups)]

    half_next, *strips_next = model(next_probes, exchange(pack([next_probes])), False)
    strips, half_next = lax.optimization_barrier((strips, half_next))
    (images_next,) = model(half_next, exchange(strips_next), True, True)
    ready, (shifting, far) = images_next, lax.optimization_barrier((images_next, far))
    passed = [images, images_next, right(shifting, 1)] + far

    received, _ = lax.optimization_barrier((exchange(strips), ready))
    halfway, *strips = model(images, received, False)
    (second,) = model(halfway, exchange(strips), True, True)

    (partial,) = kernel_call(
        dots_kernel,
        [f32(count, LANES)],
        [],
        [where, second] + passed,
        4.0,
        14,
    )
    basis, projected = kernel_call(
        functools.partial(finish_kernel, 1.0 / ncells),
        [tile, f32(count, count)],
        [pltpu.VMEM((group, x, y, z), jnp.float32), pltpu.SemaphoreType.DMA((group * (x // SUB),))],
        [where, all_sum(partial)] + passed,
        5.0,
        14,
        outs_anywhere=(0,),
    )
    return (basis, projected)


def solution(mesh):
    return jax.shard_map(
        shards,
        mesh=mesh,
        in_specs=(
            P("probe", "sx", "sy", None),
            P(None, "sx", "sy", None),
            P("sx", "sy", None),
            P("sx", "sy", None),
        ),
        out_specs=(P("probe", "sx", "sy", None), P()),
        check_vma=False,
    )
```

```python
import functools

import jax
import jax.numpy as jnp
from jax import lax
from jax.experimental import pallas as pl
from jax.experimental.pallas import tpu as pltpu
from jax.sharding import PartitionSpec as P

STEPS = 4
SUB = 8
LANES = 128
ROWS = 2
MIB = 1024 * 1024
FLOPS_PER_MICRO = 1.15e9
BYTES_PER_MICRO = 3.6e6


def kernel_call(body, outs, scratch, ins, micros, mib, anywhere=(), outs_anywhere=(), scalars=True):
    spec = lambda n, names: pl.BlockSpec(memory_space=pl.ANY if n in names else pltpu.VMEM)
    specs = [spec(n, anywhere) for n in range(len(ins))]
    if scalars:
        specs[0] = pl.BlockSpec(memory_space=pltpu.SMEM)
    return pl.pallas_call(
        body,
        out_shape=outs,
        in_specs=specs,
        out_specs=[spec(n, outs_anywhere) for n in range(len(outs))],
        scratch_shapes=scratch,
        compiler_params=pltpu.CompilerParams(vmem_limit_bytes=mib * MIB),
        cost_estimate=pl.CostEstimate(
            flops=int(micros * FLOPS_PER_MICRO),
            bytes_accessed=int(micros * BYTES_PER_MICRO),
            transcendentals=0,
        ),
    )(*ins)


def f32(*shape):
    return jax.ShapeDtypeStruct(shape, jnp.float32)


def strip_shapes(fields, x, y, z, both, joined=False):
    packs = [f32(fields, x // 2, SUB, z)] + [f32(fields, 2, SUB, z)] * (0 if joined else 2)
    return [f32(fields, STEPS, y, z)] * 2 + packs * (2 if both else 1)


def pack_starts(packs, y, side):
    if packs == 2:
        return [(0, False), (y - SUB, True)]
    return [(pl.multiple_of(jnp.where(side == 0, y - SUB, 0), SUB), side == 0)]


def packed_pair(row, first, second, last):
    hi = lambda: jnp.where(row < STEPS, pltpu.roll(first, STEPS, 0), second)
    lo = lambda: jnp.where(row < STEPS, first, pltpu.roll(second, STEPS, 0))
    if isinstance(last, bool):
        return hi() if last else lo()
    return jnp.where(last, hi(), lo())


def write_packs(field, n, rows, last, outs):
    pack, *corners = outs[2 + 3 * n : 5 + 3 * n]
    half, z = pack.shape[1], pack.shape[3]
    row = lax.broadcasted_iota(jnp.int32, (SUB, z), 0)

    def step(i, carry):
        pack[field, i] = packed_pair(row, rows(2 * i), rows(2 * i + 1), last)
        return carry

    lax.fori_loop(0, half, step, None, unroll=4)
    for corner, start in zip(corners, (0, half - 2)):
        for i in range(2):
            corner[field, i] = pack[field, start + i]


def write_strips(tile, outs, side):
    fields, x, y, _ = tile.shape
    for p in range(fields):
        for i in range(STEPS):
            outs[0][p, i] = tile[p, i]
            outs[1][p, i] = tile[p, x - STEPS + i]
        for n, (start, last) in enumerate(pack_starts(max((len(outs) - 2) // 3, 1), y, side)):
            write_packs(p, n, lambda i: tile[p, i, pl.ds(start, SUB)], last, outs)


def join_kernel(xlo, xhi, pack, lo, hi):
    fields, steps, y, _ = xlo.shape
    chunks, half = y // SUB, pack.shape[1]
    for f in range(fields):
        for strip, out, start in ((xlo, lo, 0), (xhi, hi, half - 2)):
            for i in range(steps):
                for c in range(chunks):
                    out[f, i * chunks + c] = strip[f, i, SUB * c : SUB * (c + 1)]
            for i in range(2):
                out[f, steps * chunks + i] = pack[f, start + i]


def join(xlo, xhi, pack):
    fields, steps, y, z = xlo.shape
    out = f32(fields, steps * y // SUB + 2, SUB, z)
    return kernel_call(join_kernel, [out, out], [], [xlo, xhi, pack], 1.0, 8, scalars=False)


def exchange(strips, after=None):
    nx, ny = lax.axis_size("sx"), lax.axis_size("sy")
    up = [(i, i + 1) for i in range(nx - 1)]
    down = [(j, i) for i, j in up]

    def moved(value, dx, dys):
        pairs = []
        for i in range(nx):
            for j in range(ny):
                for dy in dys(j):
                    if 0 <= i + dx < nx and 0 <= j + dy < ny:
                        pairs.append((i * ny + j, (i + dx) * ny + j + dy))
        return lax.ppermute(value, ("sx", "sy"), pairs)

    if len(strips) == 3:
        pack = moved(strips[2], 0, lambda j: (1 - 2 * j,))
        if after is not None:
            strips, pack, _ = lax.optimization_barrier((strips, pack, after))
        lo, hi = join(strips[0], strips[1], pack)
        return [lax.ppermute(hi, "sx", up), lax.ppermute(lo, "sx", down), pack]
    below = lax.ppermute(strips[1], "sx", up)
    above = lax.ppermute(strips[0], "sx", down)
    received = [below, above]
    if len(strips) == 5:
        flip = lambda j: (1 - 2 * j,)
        pack, corner_lo, corner_hi = strips[2:]
        received += [moved(pack, 0, flip), moved(corner_hi, 1, flip), moved(corner_lo, -1, flip)]
    else:
        for n, dy in ((0, -1), (1, 1)):
            pack, corner_lo, corner_hi = strips[2 + 3 * n : 5 + 3 * n]
            one = lambda j, dy=dy: (dy,)
            received += [moved(pack, 0, one), moved(corner_hi, 1, one), moved(corner_lo, -1, one)]
    return received


class Copies:
    def __init__(self, sems):
        self.sems, self.open, self.used = sems, [], 0

    def start(self, src, dst):
        copy = pltpu.make_async_copy(src, dst, self.sems.at[self.used])
        self.used += 1
        copy.start()
        self.open.append(copy)
        return copy

    def wait(self):
        for copy in self.open:
            copy.wait()
        self.open = []


def start_widening(copies, dst, tile, field, received):
    x, y = tile.shape[0], tile.shape[1]
    copies.start(tile, dst.at[pl.ds(0, x), pl.ds(0, y)])
    if len(received) == 3:
        return
    copies.start(received[1].at[field], dst.at[pl.ds(x, STEPS), pl.ds(0, y)])
    copies.start(received[0].at[field], dst.at[pl.ds(x + STEPS, STEPS), pl.ds(0, y)])


def widen_rows(dst, field, received, side):
    half, z = received[2].shape[1], received[2].shape[3]
    x, y = 2 * half, dst.shape[1] - SUB
    row = lax.broadcasted_iota(jnp.int32, (SUB, z), 0)
    both = len(received) > 5

    def put(at, packs):
        if both:
            hi, lo = packs
        else:
            hi = jnp.where(side == 0, packs[0], 0.0)
            lo = jnp.where(side == 0, 0.0, packs[0])
        dst[at, y : y + SUB] = jnp.where(row < STEPS, hi, pltpu.roll(lo, STEPS, 0))
        dst[at + 1, y : y + SUB] = jnp.where(row < STEPS, pltpu.roll(hi, STEPS, 0), lo)

    groups = [received[2:5]] + ([received[5:8]] if both else [])
    first = 0
    if len(received) == 3:
        below, above, pack = received
        groups = [[pack, below, above]]
        first = STEPS * y // SUB
        for strip, at in ((above, x), (below, x + STEPS)):
            for i in range(STEPS):
                for c in range(y // SUB):
                    dst[at + i, SUB * c : SUB * (c + 1)] = strip[field, i * (y // SUB) + c]

    def main(i, carry):
        put(2 * i, [g[0][field, i] for g in groups])
        return carry

    lax.fori_loop(0, half, main, None, unroll=4)
    for i in range(2):
        put(x + 2 * i, [g[2][field, first + i] for g in groups])
        put(x + STEPS + 2 * i, [g[1][field, first + i] for g in groups])


def coefficient_rows(coef):
    _, wide, rows, z = coef.shape
    lane = lax.broadcasted_iota(jnp.int32, (SUB, z), 1)

    def row(i, carry):
        for c in range(rows // SUB):
            at = pl.ds(SUB * c, SUB)
            spread = coef[0, i, at]
            values = [1.0 - 6.0 * spread]
            for d in range(3):
                half = 0.5 * coef[1 + 2 * d, i, at]
                plus, minus = spread - half, spread + half
                if d == 2:
                    plus = jnp.where(lane == z - 1, 0.0, plus)
                    minus = jnp.where(lane == 0, 0.0, minus)
                values += [plus, minus]
            for s, value in enumerate(values):
                coef[s, i, at] = value
        return carry

    lax.fori_loop(0, wide, row, None)


def sweep(coef, src, first, stop, adjoint, done, write):
    fields, wide, rows, z = src.shape
    chunks, cols = rows // SUB, z // LANES
    sub = lax.broadcasted_iota(jnp.int32, (SUB, LANES), 0)
    lane = lax.broadcasted_iota(jnp.int32, (SUB, LANES), 1)
    first_row, last_row = sub == 0, sub == SUB - 1
    first_lane, last_lane = lane == 0, lane == LANES - 1

    def piece(ref, lead, xi, c, j):
        return ref[lead, xi, SUB * c : SUB * (c + 1), LANES * j : LANES * (j + 1)]

    def body(pair, carry):
        wrap = lambda a: jnp.where(a < 0, a + wide, a)
        base = first + ROWS * pair
        at = [wrap(base + d) for d in range(-1, ROWS + 1)]
        kept = {}

        def load(ref, lead, r, c, j):
            key = (ref is coef, lead, r, c % chunks, j)
            if key not in kept:
                kept[key] = piece(ref, lead, at[r + 1], c % chunks, j)
            return kept[key]

        def scaled(slot, p, r, c, j):
            u = load(src, p, r, c, j)
            return load(coef, slot, r, c, j) * u if adjoint else u

        def turned(slot, shift, p, r, c, j):
            key = ("turned", slot, p, r, c % chunks, j)
            if key not in kept:
                kept[key] = pltpu.roll(scaled(slot, p, r, c, j), shift, 0)
            return kept[key]

        for c in range(done):
            results = []
            for r in range(ROWS):
                plus, minus = {}, {}
                for j in range(cols):
                    for p in range(fields):
                        plus[p, j] = pltpu.roll(scaled(6, p, r, c, j), LANES - 1, 1)
                        minus[p, j] = pltpu.roll(scaled(5, p, r, c, j), 1, 1)
                for j in range(cols):
                    for p in range(fields):
                        u, xp, xm = (load(src, p, r + d, c, j) for d in (0, 1, -1))
                        yp = jnp.where(last_row, turned(4, SUB - 1, p, r, c + 1, j), turned(4, SUB - 1, p, r, c, j))
                        ym = jnp.where(first_row, turned(3, 1, p, r, c - 1, j), turned(3, 1, p, r, c, j))
                        zp = jnp.where(last_lane, plus[p, (j + 1) % cols], plus[p, j])
                        zm = jnp.where(first_lane, minus[p, (j - 1) % cols], minus[p, j])
                        if adjoint:
                            xs = load(coef, 2, r + 1, c, j) * xp + load(coef, 1, r - 1, c, j) * xm
                            ys, zs = yp + ym, zp + zm
                        else:
                            xs = load(coef, 1, r, c, j) * xp + load(coef, 2, r, c, j) * xm
                            ys = load(coef, 3, r, c, j) * yp + load(coef, 4, r, c, j) * ym
                            zs = load(coef, 5, r, c, j) * zp + load(coef, 6, r, c, j) * zm
                        value = (load(coef, 0, r, c, j) * u + xs) + (ys + zs)
                        results.append((p, at[r + 1], c, j, value))
            for result in results:
                write(*result)
        return carry

    lax.fori_loop(0, (stop - first) // ROWS, body, None)


def run_steps(coef, states, out, adjoint, weight=None):
    x, tile_rows = out.shape[1], out.shape[2]
    for step in range(STEPS):
        src, dst = states[step % 2], states[(step + 1) % 2]
        last = step == STEPS - 1

        def write(p, i, c, j, value):
            at = (pl.ds(SUB * c, SUB), pl.ds(LANES * j, LANES))
            if last:
                out[p, i, *at] = value if weight is None else weight[i, *at] * value
            else:
                dst[p, i, *at] = value

        done = (tile_rows if last else src.shape[2]) // SUB
        reach = STEPS - 1 - step
        sweep(coef, src, -reach, x + reach, adjoint, done, write)


def flat_tiles(sources):
    return [ref.at[n] for ref in sources for n in range(ref.shape[0])]


def pack_y_kernel(fields_in, packs, scalars, *refs):
    sources, outs, (buffers, sems) = refs[:fields_in], refs[fields_in:-2], refs[-2:]
    tiles = flat_tiles(sources)
    starts = pack_starts(packs, tiles[0].shape[1], scalars[0])
    copies = Copies(sems)
    for f, tile in enumerate(tiles):
        for n, (start, _) in enumerate(starts):
            copies.start(tile.at[:, pl.ds(start, SUB)], buffers.at[n, f])
    for f in range(len(tiles)):
        for n, (_, last) in enumerate(starts):
            copies.open[f * len(starts) + n].wait()
            write_packs(f, n, lambda i: buffers[n, f, i], last, (None, None) + outs)


def pack_x_kernel(fields_in, *refs):
    sources, (low, high, sems) = refs[:fields_in], refs[fields_in:]
    copies = Copies(sems)
    for f, tile in enumerate(flat_tiles(sources)):
        copies.start(tile.at[pl.ds(0, STEPS)], low.at[f])
        copies.start(tile.at[pl.ds(tile.shape[0] - STEPS, STEPS)], high.at[f])
    copies.wait()


def first_kernel(count, scalars, diffusivity, velocity, probes, weight, *refs):
    side = scalars[0]
    received, coef, out = refs[:count], refs[count], refs[count + 1]
    strips, (state, other, sems) = refs[count + 2 : -3], refs[-3:]
    copies = Copies(sems)
    tiles = [diffusivity.at[0]] + [velocity.at[d] for d in range(3)]
    slots = [coef.at[s] for s in (0, 1, 3, 5)]
    for p in range(probes.shape[0]):
        tiles.append(probes.at[p])
        slots.append(state.at[p])
    for f, (tile, slot) in enumerate(zip(tiles, slots)):
        start_widening(copies, slot, tile, f, received)
    for f, slot in enumerate(slots):
        widen_rows(slot, f, received, side)
    copies.wait()
    coefficient_rows(coef)
    run_steps(coef, (state, other), out, False, weight)
    write_strips(out, strips, side)


def next_kernel(count, adjoint, scalars, coef, tile, *refs):
    side = scalars[0]
    weight = None if adjoint else refs[0]
    refs = refs if adjoint else refs[1:]
    received, out = refs[:count], refs[count]
    strips, (state, other, sems) = refs[count + 1 : -3], refs[-3:]
    fields = tile.shape[0]
    copies = Copies(sems)
    for p in range(fields):
        start_widening(copies, state.at[p], tile.at[p], p, received)
    for p in range(fields):
        widen_rows(state.at[p], p, received, side)
    copies.wait()
    run_steps(coef, (state, other), out, adjoint, weight)
    if strips:
        write_strips(out, strips, side)


def dots_pairs(group, slots):
    return [(s, a, b) for s in range(slots) for a in range(group) for b in range(group) if s or b <= a]


def dots_kernel(scalars, second, *refs):
    passed, out = refs[:-1], refs[-1]
    group, rows, y, z = second.shape
    chunks, cols = y // SUB, z // LANES
    pairs = dots_pairs(group, len(passed))

    def body(i, sums):
        sums = list(sums)
        for c in range(chunks):
            for j in range(cols):
                at = (pl.ds(SUB * c, SUB), pl.ds(LANES * j, LANES))
                mine = [passed[0][a, i, *at] for a in range(group)]
                then = [second[a, i, *at] for a in range(group)]
                other = {(s, b): passed[s][b, i, *at] for s in range(1, len(passed)) for b in range(group)}
                for n, (s, a, b) in enumerate(pairs):
                    value = other[s, b] if s else mine[b]
                    sums[2 * n] = sums[2 * n] + mine[a] * value
                    sums[2 * n + 1] = sums[2 * n + 1] + then[a] * value
        return tuple(sums)

    zero = jnp.zeros((SUB, LANES), jnp.float32)
    sums = lax.fori_loop(0, rows, body, (zero,) * (2 * len(pairs)))
    me = scalars[1]
    count = out.shape[0]
    row = lax.broadcasted_iota(jnp.int32, out.shape, 0)
    lane = lax.broadcasted_iota(jnp.int32, out.shape, 1)
    total = jnp.zeros(out.shape, jnp.float32)
    for n, (s, a, b) in enumerate(pairs):
        for k in range(2):
            value = jnp.sum(jnp.sum(sums[2 * n + k], axis=0, keepdims=True), axis=1, keepdims=True)
            i, j = me * group + a, (me - s) * group + b
            here = (row == i) & (lane == j + k * count) | (row == j) & (lane == i + k * count)
            total = total + jnp.where(here & (me >= s), value, 0.0)
    out[...] = total


def finish_kernel(scale, scalars, inner, *refs):
    images, (basis, projected, held, sems) = refs[:-4], refs[-4:]
    group, x, y, z = held.shape
    count = inner.shape[0]
    me = scalars[1]
    row = lax.broadcasted_iota(jnp.int32, inner.shape, 0)
    lane = lax.broadcasted_iota(jnp.int32, inner.shape, 1)
    base = 2 * count
    work = jnp.where(lane == row + base, 1.0, inner[...] * scale)
    for k in range(count):
        column = jnp.broadcast_to(work[:, k : k + 1], inner.shape)
        pivot = jnp.broadcast_to(column[k : k + 1], inner.shape)
        line = jnp.broadcast_to(work[k : k + 1], inner.shape)
        work = work - jnp.where(row > k, column / pivot, 0.0) * line
    pivots = jnp.sum(jnp.where(lane == row, work, 0.0), axis=1, keepdims=True)
    work = work * (1.0 / jnp.sqrt(pivots))

    factors = []
    for a in range(group):
        factors.append([])
        for s in range(len(images)):
            for b in range(group):
                here = (row == me * group + a) & (lane == base + (me - s) * group + b) & (me >= s)
                value = jnp.sum(jnp.where(here, work, 0.0), axis=0, keepdims=True)
                value = jnp.sum(value, axis=1, keepdims=True)
                factors[a].append(jnp.broadcast_to(value, (SUB, LANES)))

    def body(i, carry):
        for c in range(y // SUB):
            for j in range(z // LANES):
                at = (pl.ds(SUB * c, SUB), pl.ds(LANES * j, LANES))
                values = [image[b, i, *at] for image in images for b in range(group)]
                for a in range(group):
                    terms = [factor * value for factor, value in zip(factors[a], values)]
                    while len(terms) > 1:
                        terms = [sum(terms[n : n + 2][1:], terms[n]) for n in range(0, len(terms), 2)]
                    held[a, i, *at] = terms[0]
        return carry

    copies = Copies(sems)
    for start in range(0, x, SUB):
        lax.fori_loop(start, start + SUB, body, None)
        for a in range(group):
            copies.start(held.at[a, pl.ds(start, SUB)], basis.at[a, pl.ds(start, SUB)])

    left = jnp.where((lane >= count) & (lane < base), work, 0.0)
    right = jnp.where((lane >= count) & (lane < base), pltpu.roll(work, LANES - count, 1), 0.0)
    projected[...] = lax.dot_general(
        left,
        right,
        (((1,), (1,)), ((), ())),
        precision=lax.Precision.HIGHEST,
        preferred_element_type=jnp.float32,
    )
    copies.wait()


def all_sum(value):
    for axis in ("sx", "sy", "probe"):
        devices = lax.axis_size(axis)
        if devices & (devices - 1):
            value = lax.psum(value, axis)
            continue
        move = lambda bits: lax.ppermute(value, axis, [(i, i ^ bits) for i in range(devices)])
        bit = 1
        while bit < devices:
            if 4 * bit <= devices:
                value = (value + move(bit)) + (move(2 * bit) + move(3 * bit))
                bit *= 4
            else:
                value = value + move(bit)
                bit *= 2
    return value


def shards(probes, velocity, diffusivity, obs_weight):
    group, x, y, z = probes.shape
    groups = lax.axis_size("probe")
    count = group * groups
    ncells = x * y * z * lax.axis_size("sx") * lax.axis_size("sy")
    both = lax.axis_size("sy") != 2
    side, mine = lax.axis_index("sy"), lax.axis_index("probe")

    where = jnp.stack([side, mine]).astype(jnp.int32)
    wide = (x + 2 * STEPS, y + 2 * STEPS, z)
    tile = f32(group, x, y, z)
    strips2 = strip_shapes(group, x, y, z, both, not both)
    fields = [diffusivity[None], velocity, probes]
    total = 4 + group

    def scratch(copies):
        return [
            pltpu.VMEM((group,) + wide, jnp.float32),
            pltpu.VMEM((group,) + wide, jnp.float32),
            pltpu.SemaphoreType.DMA((copies,)),
        ]

    packs = 2 if both else 1

    def pack(sources, joined, mib):
        number = sum(a.shape[0] for a in sources)
        outs = strip_shapes(number, x, y, z, both, joined)
        in_y = kernel_call(
            functools.partial(pack_y_kernel, len(sources), packs),
            outs[2:],
            [pltpu.VMEM((packs, number, x, SUB, z), jnp.float32), pltpu.SemaphoreType.DMA((number * packs,))],
            [where] + sources,
            2.0,
            mib,
            anywhere=range(1, len(sources) + 1),
        )
        in_x = kernel_call(
            functools.partial(pack_x_kernel, len(sources)),
            outs[:2],
            [pltpu.SemaphoreType.DMA((2 * number,))],
            sources,
            2.0,
            mib,
            anywhere=range(len(sources)),
            scalars=False,
        )
        return list(in_x) + list(in_y)

    def right(value, hops):
        return lax.ppermute(value, "probe", [(i, i + hops) for i in range(groups - hops)])

    next_probes = right(probes, 1)
    strips = pack(fields, False, 56)
    received = exchange(strips)
    coef, halfway, *strips = kernel_call(
        functools.partial(first_kernel, len(received)),
        [f32(7, *wide), tile] + strips2,
        scratch(3 * total),
        [where] + fields + [obs_weight] + received,
        4.0,
        14,
        anywhere=(1, 2, 3, 5, 6),
    )

    def model(field, received, adjoint, last=False):
        ins = [where, coef, field] + ([] if adjoint else [obs_weight])
        return kernel_call(
            functools.partial(next_kernel, len(received), adjoint),
            [tile] + ([] if last else strips2),
            scratch(3 * group),
            ins + received,
            12.0,
            14,
            anywhere=(2, len(ins), len(ins) + 1) if both else (2,),
        )

    images, *strips = model(halfway, exchange(strips), True)
    far = [right(images, hops) for hops in range(3, groups)]

    half_next, *strips_next = model(next_probes, exchange(pack([next_probes], not both, 8)), False)
    strips, half_next = lax.optimization_barrier((strips, half_next))
    (images_next,) = model(half_next, exchange(strips_next), True, True)
    shifting, far = lax.optimization_barrier((images_next, far))
    passed = [images, images_next, right(shifting, 1)] + far

    received = exchange(strips, after=images_next)
    halfway, *strips = model(images, received, False)
    (second,) = model(halfway, exchange(strips), True, True)

    (partial,) = kernel_call(
        dots_kernel,
        [f32(count, LANES)],
        [],
        [where, second] + passed,
        4.0,
        14,
    )
    basis, projected = kernel_call(
        functools.partial(finish_kernel, 1.0 / ncells),
        [tile, f32(count, count)],
        [pltpu.VMEM((group, x, y, z), jnp.float32), pltpu.SemaphoreType.DMA((group * (x // SUB),))],
        [where, all_sum(partial)] + passed,
        5.0,
        14,
        outs_anywhere=(0,),
    )
    return (basis, projected)


def solution(mesh):
    return jax.shard_map(
        shards,
        mesh=mesh,
        in_specs=(
            P("probe", "sx", "sy", None),
            P(None, "sx", "sy", None),
            P("sx", "sy", None),
            P("sx", "sy", None),
        ),
        out_specs=(P("probe", "sx", "sy", None), P()),
        check_vma=False,
    )
```

```python
import functools

import jax
import jax.numpy as jnp
from jax import lax
from jax.experimental import pallas as pl
from jax.experimental.pallas import tpu as pltpu
from jax.sharding import PartitionSpec as P

STEPS = 4
SUB = 8
LANES = 128
ROWS = 2
MIB = 1024 * 1024
FLOPS_PER_MICRO = 1.15e9
BYTES_PER_MICRO = 3.6e6


def kernel_call(body, outs, scratch, ins, micros, mib, anywhere=(), outs_anywhere=(), scalars=True):
    spec = lambda n, names: pl.BlockSpec(memory_space=pl.ANY if n in names else pltpu.VMEM)
    specs = [spec(n, anywhere) for n in range(len(ins))]
    if scalars:
        specs[0] = pl.BlockSpec(memory_space=pltpu.SMEM)
    return pl.pallas_call(
        body,
        out_shape=outs,
        in_specs=specs,
        out_specs=[spec(n, outs_anywhere) for n in range(len(outs))],
        scratch_shapes=scratch,
        compiler_params=pltpu.CompilerParams(vmem_limit_bytes=mib * MIB),
        cost_estimate=pl.CostEstimate(
            flops=int(micros * FLOPS_PER_MICRO),
            bytes_accessed=int(micros * BYTES_PER_MICRO),
            transcendentals=0,
        ),
    )(*ins)


def f32(*shape):
    return jax.ShapeDtypeStruct(shape, jnp.float32)


def strip_shapes(fields, x, y, z, both, joined=False):
    packs = [f32(fields, x // 2, SUB, z)] + [f32(fields, 2, SUB, z)] * (0 if joined else 2)
    return [f32(fields, STEPS, y, z)] * 2 + packs * (2 if both else 1)


def pack_starts(packs, y, side):
    if packs == 2:
        return [(0, False), (y - SUB, True)]
    return [(pl.multiple_of(jnp.where(side == 0, y - SUB, 0), SUB), side == 0)]


def packed_pair(row, first, second, last):
    hi = lambda: jnp.where(row < STEPS, pltpu.roll(first, STEPS, 0), second)
    lo = lambda: jnp.where(row < STEPS, first, pltpu.roll(second, STEPS, 0))
    if isinstance(last, bool):
        return hi() if last else lo()
    return jnp.where(last, hi(), lo())


def write_packs(field, n, rows, last, outs):
    pack, *corners = outs[2 + 3 * n : 5 + 3 * n]
    half, z = pack.shape[1], pack.shape[3]
    row = lax.broadcasted_iota(jnp.int32, (SUB, z), 0)

    def step(i, carry):
        pack[field, i] = packed_pair(row, rows(2 * i), rows(2 * i + 1), last)
        return carry

    lax.fori_loop(0, half, step, None, unroll=4)
    for corner, start in zip(corners, (0, half - 2)):
        for i in range(2):
            corner[field, i] = pack[field, start + i]


def write_strips(tile, outs, side):
    fields, x, y, _ = tile.shape
    for p in range(fields):
        for i in range(STEPS):
            outs[0][p, i] = tile[p, i]
            outs[1][p, i] = tile[p, x - STEPS + i]
        for n, (start, last) in enumerate(pack_starts(max((len(outs) - 2) // 3, 1), y, side)):
            write_packs(p, n, lambda i: tile[p, i, pl.ds(start, SUB)], last, outs)


def join_kernel(xlo, xhi, pack, lo, hi):
    fields, steps, y, _ = xlo.shape
    chunks, half = y // SUB, pack.shape[1]
    for f in range(fields):
        for strip, out, start in ((xlo, lo, 0), (xhi, hi, half - 2)):
            for i in range(steps):
                for c in range(chunks):
                    out[f, i * chunks + c] = strip[f, i, SUB * c : SUB * (c + 1)]
            for i in range(2):
                out[f, steps * chunks + i] = pack[f, start + i]


def join(xlo, xhi, pack):
    fields, steps, y, z = xlo.shape
    out = f32(fields, steps * y // SUB + 2, SUB, z)
    return kernel_call(join_kernel, [out, out], [], [xlo, xhi, pack], 1.0, 8, scalars=False)


def exchange(strips, after=None):
    nx, ny = lax.axis_size("sx"), lax.axis_size("sy")
    up = [(i, i + 1) for i in range(nx - 1)]
    down = [(j, i) for i, j in up]

    def moved(value, dx, dys):
        pairs = []
        for i in range(nx):
            for j in range(ny):
                for dy in dys(j):
                    if 0 <= i + dx < nx and 0 <= j + dy < ny:
                        pairs.append((i * ny + j, (i + dx) * ny + j + dy))
        return lax.ppermute(value, ("sx", "sy"), pairs)

    if len(strips) == 3:
        pack = moved(strips[2], 0, lambda j: (1 - 2 * j,))
        if after is not None:
            strips, pack, _ = lax.optimization_barrier((strips, pack, after))
        lo, hi = join(strips[0], strips[1], pack)
        return [lax.ppermute(hi, "sx", up), lax.ppermute(lo, "sx", down), pack]
    below = lax.ppermute(strips[1], "sx", up)
    above = lax.ppermute(strips[0], "sx", down)
    received = [below, above]
    if len(strips) == 5:
        flip = lambda j: (1 - 2 * j,)
        pack, corner_lo, corner_hi = strips[2:]
        received += [moved(pack, 0, flip), moved(corner_hi, 1, flip), moved(corner_lo, -1, flip)]
    else:
        for n, dy in ((0, -1), (1, 1)):
            pack, corner_lo, corner_hi = strips[2 + 3 * n : 5 + 3 * n]
            one = lambda j, dy=dy: (dy,)
            received += [moved(pack, 0, one), moved(corner_hi, 1, one), moved(corner_lo, -1, one)]
    return received


class Copies:
    def __init__(self, sems):
        self.sems, self.open, self.used = sems, [], 0

    def start(self, src, dst):
        copy = pltpu.make_async_copy(src, dst, self.sems.at[self.used])
        self.used += 1
        copy.start()
        self.open.append(copy)
        return copy

    def wait(self):
        for copy in self.open:
            copy.wait()
        self.open = []


def start_widening(copies, dst, tile, field, received):
    x, y = tile.shape[0], tile.shape[1]
    copies.start(tile, dst.at[pl.ds(0, x), pl.ds(0, y)])
    if len(received) == 3:
        return
    copies.start(received[1].at[field], dst.at[pl.ds(x, STEPS), pl.ds(0, y)])
    copies.start(received[0].at[field], dst.at[pl.ds(x + STEPS, STEPS), pl.ds(0, y)])


def widen_rows(dst, field, received, side):
    half, z = received[2].shape[1], received[2].shape[3]
    x, y = 2 * half, dst.shape[1] - SUB
    row = lax.broadcasted_iota(jnp.int32, (SUB, z), 0)
    both = len(received) > 5

    def put(at, packs):
        if both:
            hi, lo = packs
        else:
            hi = jnp.where(side == 0, packs[0], 0.0)
            lo = jnp.where(side == 0, 0.0, packs[0])
        dst[at, y : y + SUB] = jnp.where(row < STEPS, hi, pltpu.roll(lo, STEPS, 0))
        dst[at + 1, y : y + SUB] = jnp.where(row < STEPS, pltpu.roll(hi, STEPS, 0), lo)

    groups = [received[2:5]] + ([received[5:8]] if both else [])
    first = 0
    if len(received) == 3:
        below, above, pack = received
        groups = [[pack, below, above]]
        first = STEPS * y // SUB
        for strip, at in ((above, x), (below, x + STEPS)):
            for i in range(STEPS):
                for c in range(y // SUB):
                    dst[at + i, SUB * c : SUB * (c + 1)] = strip[field, i * (y // SUB) + c]

    def main(i, carry):
        put(2 * i, [g[0][field, i] for g in groups])
        return carry

    lax.fori_loop(0, half, main, None, unroll=4)
    for i in range(2):
        put(x + 2 * i, [g[2][field, first + i] for g in groups])
        put(x + STEPS + 2 * i, [g[1][field, first + i] for g in groups])


def coefficient_rows(coef):
    _, wide, rows, z = coef.shape
    lane = lax.broadcasted_iota(jnp.int32, (SUB, z), 1)

    def row(i, carry):
        for c in range(rows // SUB):
            at = pl.ds(SUB * c, SUB)
            spread = coef[0, i, at]
            values = [1.0 - 6.0 * spread]
            for d in range(3):
                half = 0.5 * coef[1 + 2 * d, i, at]
                plus, minus = spread - half, spread + half
                if d == 2:
                    plus = jnp.where(lane == z - 1, 0.0, plus)
                    minus = jnp.where(lane == 0, 0.0, minus)
                values += [plus, minus]
            for s, value in enumerate(values):
                coef[s, i, at] = value
        return carry

    lax.fori_loop(0, wide, row, None)


def sweep(coef, src, first, stop, adjoint, done, write):
    fields, wide, rows, z = src.shape
    chunks, cols = rows // SUB, z // LANES
    sub = lax.broadcasted_iota(jnp.int32, (SUB, LANES), 0)
    lane = lax.broadcasted_iota(jnp.int32, (SUB, LANES), 1)
    first_row, last_row = sub == 0, sub == SUB - 1
    first_lane, last_lane = lane == 0, lane == LANES - 1

    def piece(ref, lead, xi, c, j):
        return ref[lead, xi, SUB * c : SUB * (c + 1), LANES * j : LANES * (j + 1)]

    def body(pair, carry):
        wrap = lambda a: jnp.where(a < 0, a + wide, a)
        base = first + ROWS * pair
        at = [wrap(base + d) for d in range(-1, ROWS + 1)]
        kept = {}

        def load(ref, lead, r, c, j):
            key = (ref is coef, lead, r, c % chunks, j)
            if key not in kept:
                kept[key] = piece(ref, lead, at[r + 1], c % chunks, j)
            return kept[key]

        def scaled(slot, p, r, c, j):
            u = load(src, p, r, c, j)
            return load(coef, slot, r, c, j) * u if adjoint else u

        def turned(slot, shift, p, r, c, j):
            key = ("turned", slot, p, r, c % chunks, j)
            if key not in kept:
                kept[key] = pltpu.roll(scaled(slot, p, r, c, j), shift, 0)
            return kept[key]

        for c in range(done):
            results = []
            for r in range(ROWS):
                plus, minus = {}, {}
                for j in range(cols):
                    for p in range(fields):
                        plus[p, j] = pltpu.roll(scaled(6, p, r, c, j), LANES - 1, 1)
                        minus[p, j] = pltpu.roll(scaled(5, p, r, c, j), 1, 1)
                for j in range(cols):
                    for p in range(fields):
                        u, xp, xm = (load(src, p, r + d, c, j) for d in (0, 1, -1))
                        yp = jnp.where(last_row, turned(4, SUB - 1, p, r, c + 1, j), turned(4, SUB - 1, p, r, c, j))
                        ym = jnp.where(first_row, turned(3, 1, p, r, c - 1, j), turned(3, 1, p, r, c, j))
                        zp = jnp.where(last_lane, plus[p, (j + 1) % cols], plus[p, j])
                        zm = jnp.where(first_lane, minus[p, (j - 1) % cols], minus[p, j])
                        if adjoint:
                            xs = load(coef, 2, r + 1, c, j) * xp + load(coef, 1, r - 1, c, j) * xm
                            ys, zs = yp + ym, zp + zm
                        else:
                            xs = load(coef, 1, r, c, j) * xp + load(coef, 2, r, c, j) * xm
                            ys = load(coef, 3, r, c, j) * yp + load(coef, 4, r, c, j) * ym
                            zs = load(coef, 5, r, c, j) * zp + load(coef, 6, r, c, j) * zm
                        value = (load(coef, 0, r, c, j) * u + xs) + (ys + zs)
                        results.append((p, at[r + 1], c, j, value))
            for result in results:
                write(*result)
        return carry

    lax.fori_loop(0, (stop - first) // ROWS, body, None)


def run_steps(coef, states, out, adjoint, weight=None):
    x, tile_rows = out.shape[1], out.shape[2]
    for step in range(STEPS):
        src, dst = states[step % 2], states[(step + 1) % 2]
        last = step == STEPS - 1

        def write(p, i, c, j, value):
            at = (pl.ds(SUB * c, SUB), pl.ds(LANES * j, LANES))
            if last:
                out[p, i, *at] = value if weight is None else weight[i, *at] * value
            else:
                dst[p, i, *at] = value

        done = (tile_rows if last else src.shape[2]) // SUB
        reach = STEPS - 1 - step
        sweep(coef, src, -reach, x + reach, adjoint, done, write)


def flat_tiles(sources):
    return [ref.at[n] for ref in sources for n in range(ref.shape[0])]


def pack_y_kernel(fields_in, packs, scalars, *refs):
    sources, outs, (buffers, sems) = refs[:fields_in], refs[fields_in:-2], refs[-2:]
    tiles = flat_tiles(sources)
    starts = pack_starts(packs, tiles[0].shape[1], scalars[0])
    copies = Copies(sems)
    for f, tile in enumerate(tiles):
        for n, (start, _) in enumerate(starts):
            copies.start(tile.at[:, pl.ds(start, SUB)], buffers.at[n, f])
    for f in range(len(tiles)):
        for n, (_, last) in enumerate(starts):
            copies.open[f * len(starts) + n].wait()
            write_packs(f, n, lambda i: buffers[n, f, i], last, (None, None) + outs)


def pack_x_kernel(fields_in, *refs):
    sources, (low, high, sems) = refs[:fields_in], refs[fields_in:]
    copies = Copies(sems)
    for f, tile in enumerate(flat_tiles(sources)):
        copies.start(tile.at[pl.ds(0, STEPS)], low.at[f])
        copies.start(tile.at[pl.ds(tile.shape[0] - STEPS, STEPS)], high.at[f])
    copies.wait()


def first_kernel(count, scalars, diffusivity, velocity, probes, weight, *refs):
    side = scalars[0]
    received, coef, out = refs[:count], refs[count], refs[count + 1]
    strips, (state, other, sems) = refs[count + 2 : -3], refs[-3:]
    copies = Copies(sems)
    tiles = [diffusivity.at[0]] + [velocity.at[d] for d in range(3)]
    slots = [coef.at[s] for s in (0, 1, 3, 5)]
    for p in range(probes.shape[0]):
        tiles.append(probes.at[p])
        slots.append(state.at[p])
    for f, (tile, slot) in enumerate(zip(tiles, slots)):
        start_widening(copies, slot, tile, f, received)
    for f, slot in enumerate(slots):
        widen_rows(slot, f, received, side)
    copies.wait()
    coefficient_rows(coef)
    run_steps(coef, (state, other), out, False, weight)
    write_strips(out, strips, side)


def next_kernel(count, adjoint, scalars, coef, tile, *refs):
    side = scalars[0]
    weight = None if adjoint else refs[0]
    refs = refs if adjoint else refs[1:]
    received, out = refs[:count], refs[count]
    strips, (state, other, sems) = refs[count + 1 : -3], refs[-3:]
    fields = tile.shape[0]
    copies = Copies(sems)
    for p in range(fields):
        start_widening(copies, state.at[p], tile.at[p], p, received)
    for p in range(fields):
        widen_rows(state.at[p], p, received, side)
    copies.wait()
    run_steps(coef, (state, other), out, adjoint, weight)
    if strips:
        write_strips(out, strips, side)


def dots_pairs(group, slots):
    return [(s, a, b) for s in range(slots) for a in range(group) for b in range(group) if s or b <= a]


def dots_kernel(scalars, second, *refs):
    passed, out = refs[:-1], refs[-1]
    group, rows, y, z = second.shape
    chunks, cols = y // SUB, z // LANES
    pairs = dots_pairs(group, len(passed))

    def body(i, sums):
        sums = list(sums)
        for c in range(chunks):
            for j in range(cols):
                at = (pl.ds(SUB * c, SUB), pl.ds(LANES * j, LANES))
                mine = [passed[0][a, i, *at] for a in range(group)]
                then = [second[a, i, *at] for a in range(group)]
                other = {(s, b): passed[s][b, i, *at] for s in range(1, len(passed)) for b in range(group)}
                for n, (s, a, b) in enumerate(pairs):
                    value = other[s, b] if s else mine[b]
                    sums[2 * n] = sums[2 * n] + mine[a] * value
                    sums[2 * n + 1] = sums[2 * n + 1] + then[a] * value
        return tuple(sums)

    zero = jnp.zeros((SUB, LANES), jnp.float32)
    sums = lax.fori_loop(0, rows, body, (zero,) * (2 * len(pairs)))
    me = scalars[1]
    count = out.shape[0]
    row = lax.broadcasted_iota(jnp.int32, out.shape, 0)
    lane = lax.broadcasted_iota(jnp.int32, out.shape, 1)
    total = jnp.zeros(out.shape, jnp.float32)
    for n, (s, a, b) in enumerate(pairs):
        for k in range(2):
            value = jnp.sum(jnp.sum(sums[2 * n + k], axis=0, keepdims=True), axis=1, keepdims=True)
            i, j = me * group + a, (me - s) * group + b
            here = (row == i) & (lane == j + k * count) | (row == j) & (lane == i + k * count)
            total = total + jnp.where(here & (me >= s), value, 0.0)
    out[...] = total


def finish_kernel(scale, scalars, inner, *refs):
    images, (basis, projected, held, sems) = refs[:-4], refs[-4:]
    group, x, y, z = held.shape
    count = inner.shape[0]
    me = scalars[1]
    row = lax.broadcasted_iota(jnp.int32, inner.shape, 0)
    lane = lax.broadcasted_iota(jnp.int32, inner.shape, 1)
    base = 2 * count
    work = jnp.where(lane == row + base, 1.0, inner[...] * scale)
    for k in range(count):
        column = jnp.broadcast_to(work[:, k : k + 1], inner.shape)
        pivot = jnp.broadcast_to(column[k : k + 1], inner.shape)
        line = jnp.broadcast_to(work[k : k + 1], inner.shape)
        work = work - jnp.where(row > k, column / pivot, 0.0) * line
    pivots = jnp.sum(jnp.where(lane == row, work, 0.0), axis=1, keepdims=True)
    work = work * (1.0 / jnp.sqrt(pivots))

    factors = []
    for a in range(group):
        factors.append([])
        for s in range(len(images)):
            for b in range(group):
                here = (row == me * group + a) & (lane == base + (me - s) * group + b) & (me >= s)
                value = jnp.sum(jnp.where(here, work, 0.0), axis=0, keepdims=True)
                value = jnp.sum(value, axis=1, keepdims=True)
                factors[a].append(jnp.broadcast_to(value, (SUB, LANES)))

    def body(i, carry):
        for c in range(y // SUB):
            for j in range(z // LANES):
                at = (pl.ds(SUB * c, SUB), pl.ds(LANES * j, LANES))
                values = [image[b, i, *at] for image in images for b in range(group)]
                for a in range(group):
                    terms = [factor * value for factor, value in zip(factors[a], values)]
                    while len(terms) > 1:
                        terms = [sum(terms[n : n + 2][1:], terms[n]) for n in range(0, len(terms), 2)]
                    held[a, i, *at] = terms[0]
        return carry

    copies = Copies(sems)
    for start in range(0, x, SUB):
        lax.fori_loop(start, start + SUB, body, None)
        for a in range(group):
            copies.start(held.at[a, pl.ds(start, SUB)], basis.at[a, pl.ds(start, SUB)])

    left = jnp.where((lane >= count) & (lane < base), work, 0.0)
    right = jnp.where((lane >= count) & (lane < base), pltpu.roll(work, LANES - count, 1), 0.0)
    projected[...] = lax.dot_general(
        left,
        right,
        (((1,), (1,)), ((), ())),
        precision=lax.Precision.HIGHEST,
        preferred_element_type=jnp.float32,
    )
    copies.wait()


def all_sum(value):
    for axis in ("sx", "sy", "probe"):
        devices = lax.axis_size(axis)
        if devices & (devices - 1):
            value = lax.psum(value, axis)
            continue
        move = lambda bits: lax.ppermute(value, axis, [(i, i ^ bits) for i in range(devices)])
        bit = 1
        while bit < devices:
            if 4 * bit <= devices:
                value = (value + move(bit)) + (move(2 * bit) + move(3 * bit))
                bit *= 4
            else:
                value = value + move(bit)
                bit *= 2
    return value


def shards(probes, velocity, diffusivity, obs_weight):
    group, x, y, z = probes.shape
    groups = lax.axis_size("probe")
    count = group * groups
    ncells = x * y * z * lax.axis_size("sx") * lax.axis_size("sy")
    both = lax.axis_size("sy") != 2
    side, mine = lax.axis_index("sy"), lax.axis_index("probe")

    where = jnp.stack([side, mine]).astype(jnp.int32)
    wide = (x + 2 * STEPS, y + 2 * STEPS, z)
    tile = f32(group, x, y, z)
    strips2 = strip_shapes(group, x, y, z, both, not both)
    fields = [diffusivity[None], velocity, probes]
    total = 4 + group

    def scratch(copies):
        return [
            pltpu.VMEM((group,) + wide, jnp.float32),
            pltpu.VMEM((group,) + wide, jnp.float32),
            pltpu.SemaphoreType.DMA((copies,)),
        ]

    packs = 2 if both else 1

    def pack(sources, joined, mib):
        number = sum(a.shape[0] for a in sources)
        outs = strip_shapes(number, x, y, z, both, joined)
        in_y = kernel_call(
            functools.partial(pack_y_kernel, len(sources), packs),
            outs[2:],
            [pltpu.VMEM((packs, number, x, SUB, z), jnp.float32), pltpu.SemaphoreType.DMA((number * packs,))],
            [where] + sources,
            2.0,
            mib,
            anywhere=range(1, len(sources) + 1),
        )
        in_x = kernel_call(
            functools.partial(pack_x_kernel, len(sources)),
            outs[:2],
            [pltpu.SemaphoreType.DMA((2 * number,))],
            sources,
            2.0,
            mib,
            anywhere=range(len(sources)),
            scalars=False,
        )
        return list(in_x) + list(in_y)

    def right(value, hops):
        return lax.ppermute(value, "probe", [(i, i + hops) for i in range(groups - hops)])

    next_probes = right(probes, 1)
    strips = pack(fields, False, 56)
    received = exchange(strips)
    coef, halfway, *strips = kernel_call(
        functools.partial(first_kernel, len(received)),
        [f32(7, *wide), tile] + strips2,
        scratch(3 * total),
        [where] + fields + [obs_weight] + received,
        4.0,
        14,
        anywhere=(1, 2, 3, 5, 6),
    )

    def model(field, received, adjoint, last=False):
        ins = [where, coef, field] + ([] if adjoint else [obs_weight])
        return kernel_call(
            functools.partial(next_kernel, len(received), adjoint),
            [tile] + ([] if last else strips2),
            scratch(3 * group),
            ins + received,
            5.0,
            14,
            anywhere=(2, len(ins), len(ins) + 1) if both else (2,),
        )

    next_probes, halfway = lax.optimization_barrier((next_probes, halfway))
    strips_next = pack([next_probes], not both, 8)
    images, *strips = model(halfway, exchange(strips), True)
    far = [right(images, hops) for hops in range(3, groups)]

    received, _ = lax.optimization_barrier((exchange(strips_next), images))
    half_next, *strips_next = model(next_probes, received, False)
    strips, half_next = lax.optimization_barrier((strips, half_next))
    (images_next,) = model(half_next, exchange(strips_next), True, True)
    shifting, far = lax.optimization_barrier((images_next, far))
    passed = [images, images_next, right(shifting, 1)] + far

    received = exchange(strips, after=images_next)
    halfway, *strips = model(images, received, False)
    (second,) = model(halfway, exchange(strips), True, True)

    (partial,) = kernel_call(
        dots_kernel,
        [f32(count, LANES)],
        [],
        [where, second] + passed,
        4.0,
        14,
    )
    basis, projected = kernel_call(
        functools.partial(finish_kernel, 1.0 / ncells),
        [tile, f32(count, count)],
        [pltpu.VMEM((group, x, y, z), jnp.float32), pltpu.SemaphoreType.DMA((group * (x // SUB),))],
        [where, all_sum(partial)] + passed,
        5.0,
        14,
        outs_anywhere=(0,),
    )
    return (basis, projected)


def solution(mesh):
    return jax.shard_map(
        shards,
        mesh=mesh,
        in_specs=(
            P("probe", "sx", "sy", None),
            P(None, "sx", "sy", None),
            P("sx", "sy", None),
            P("sx", "sy", None),
        ),
        out_specs=(P("probe", "sx", "sy", None), P()),
        check_vma=False,
    )
```

```python
import functools

import jax
import jax.numpy as jnp
from jax import lax
from jax.experimental import pallas as pl
from jax.experimental.pallas import tpu as pltpu
from jax.sharding import PartitionSpec as P

STEPS = 4
SUB = 8
LANES = 128
ROWS = 2
MIB = 1024 * 1024
FLOPS_PER_MICRO = 1.15e9
BYTES_PER_MICRO = 3.6e6


def kernel_call(body, outs, scratch, ins, micros, mib, anywhere=(), outs_anywhere=(), scalars=True):
    spec = lambda n, names: pl.BlockSpec(memory_space=pl.ANY if n in names else pltpu.VMEM)
    specs = [spec(n, anywhere) for n in range(len(ins))]
    if scalars:
        specs[0] = pl.BlockSpec(memory_space=pltpu.SMEM)
    return pl.pallas_call(
        body,
        out_shape=outs,
        in_specs=specs,
        out_specs=[spec(n, outs_anywhere) for n in range(len(outs))],
        scratch_shapes=scratch,
        compiler_params=pltpu.CompilerParams(vmem_limit_bytes=mib * MIB),
        cost_estimate=pl.CostEstimate(
            flops=int(micros * FLOPS_PER_MICRO),
            bytes_accessed=int(micros * BYTES_PER_MICRO),
            transcendentals=0,
        ),
    )(*ins)


def f32(*shape):
    return jax.ShapeDtypeStruct(shape, jnp.float32)


def strip_shapes(fields, x, y, z, both, joined=False):
    packs = [f32(fields, x // 2, SUB, z)] + [f32(fields, 2, SUB, z)] * (0 if joined else 2)
    return [f32(fields, STEPS, y, z)] * 2 + packs * (2 if both else 1)


def pack_starts(packs, y, side):
    if packs == 2:
        return [(0, False), (y - SUB, True)]
    return [(pl.multiple_of(jnp.where(side == 0, y - SUB, 0), SUB), side == 0)]


def packed_pair(row, first, second, last):
    hi = lambda: jnp.where(row < STEPS, pltpu.roll(first, STEPS, 0), second)
    lo = lambda: jnp.where(row < STEPS, first, pltpu.roll(second, STEPS, 0))
    if isinstance(last, bool):
        return hi() if last else lo()
    return jnp.where(last, hi(), lo())


def write_packs(field, n, rows, last, outs):
    pack, *corners = outs[2 + 3 * n : 5 + 3 * n]
    half, z = pack.shape[1], pack.shape[3]
    row = lax.broadcasted_iota(jnp.int32, (SUB, z), 0)

    def step(i, carry):
        pack[field, i] = packed_pair(row, rows(2 * i), rows(2 * i + 1), last)
        return carry

    lax.fori_loop(0, half, step, None, unroll=4)
    for corner, start in zip(corners, (0, half - 2)):
        for i in range(2):
            corner[field, i] = pack[field, start + i]


def write_strips(tile, outs, side):
    fields, x, y, _ = tile.shape
    for p in range(fields):
        for i in range(STEPS):
            outs[0][p, i] = tile[p, i]
            outs[1][p, i] = tile[p, x - STEPS + i]
        for n, (start, last) in enumerate(pack_starts(max((len(outs) - 2) // 3, 1), y, side)):
            write_packs(p, n, lambda i: tile[p, i, pl.ds(start, SUB)], last, outs)


def join_kernel(xlo, xhi, pack, lo, hi):
    fields, steps, y, _ = xlo.shape
    chunks, half = y // SUB, pack.shape[1]
    for f in range(fields):
        for strip, out, start in ((xlo, lo, 0), (xhi, hi, half - 2)):
            for i in range(steps):
                for c in range(chunks):
                    out[f, i * chunks + c] = strip[f, i, SUB * c : SUB * (c + 1)]
            for i in range(2):
                out[f, steps * chunks + i] = pack[f, start + i]


def join(xlo, xhi, pack):
    fields, steps, y, z = xlo.shape
    out = f32(fields, steps * y // SUB + 2, SUB, z)
    return kernel_call(join_kernel, [out, out], [], [xlo, xhi, pack], 1.0, 8, scalars=False)


def exchange(strips, after=None):
    nx, ny = lax.axis_size("sx"), lax.axis_size("sy")
    up = [(i, i + 1) for i in range(nx - 1)]
    down = [(j, i) for i, j in up]

    def moved(value, dx, dys):
        pairs = []
        for i in range(nx):
            for j in range(ny):
                for dy in dys(j):
                    if 0 <= i + dx < nx and 0 <= j + dy < ny:
                        pairs.append((i * ny + j, (i + dx) * ny + j + dy))
        return lax.ppermute(value, ("sx", "sy"), pairs)

    if len(strips) == 3:
        pack = moved(strips[2], 0, lambda j: (1 - 2 * j,))
        if after is not None:
            strips, pack, _ = lax.optimization_barrier((strips, pack, after))
        lo, hi = join(strips[0], strips[1], pack)
        return [lax.ppermute(hi, "sx", up), lax.ppermute(lo, "sx", down), pack]
    below = lax.ppermute(strips[1], "sx", up)
    above = lax.ppermute(strips[0], "sx", down)
    received = [below, above]
    if len(strips) == 5:
        flip = lambda j: (1 - 2 * j,)
        pack, corner_lo, corner_hi = strips[2:]
        received += [moved(pack, 0, flip), moved(corner_hi, 1, flip), moved(corner_lo, -1, flip)]
    else:
        for n, dy in ((0, -1), (1, 1)):
            pack, corner_lo, corner_hi = strips[2 + 3 * n : 5 + 3 * n]
            one = lambda j, dy=dy: (dy,)
            received += [moved(pack, 0, one), moved(corner_hi, 1, one), moved(corner_lo, -1, one)]
    return received


class Copies:
    def __init__(self, sems):
        self.sems, self.open, self.used = sems, [], 0

    def start(self, src, dst):
        copy = pltpu.make_async_copy(src, dst, self.sems.at[self.used])
        self.used += 1
        copy.start()
        self.open.append(copy)
        return copy

    def wait(self):
        for copy in self.open:
            copy.wait()
        self.open = []


def start_widening(copies, dst, tile, field, received):
    x, y = tile.shape[0], tile.shape[1]
    copies.start(tile, dst.at[pl.ds(0, x), pl.ds(0, y)])
    if len(received) == 3:
        return
    copies.start(received[1].at[field], dst.at[pl.ds(x, STEPS), pl.ds(0, y)])
    copies.start(received[0].at[field], dst.at[pl.ds(x + STEPS, STEPS), pl.ds(0, y)])


def widen_rows(dst, field, received, side):
    half, z = received[2].shape[1], received[2].shape[3]
    x, y = 2 * half, dst.shape[1] - SUB
    row = lax.broadcasted_iota(jnp.int32, (SUB, z), 0)
    both = len(received) > 5

    def put(at, packs):
        if both:
            hi, lo = packs
        else:
            hi = jnp.where(side == 0, packs[0], 0.0)
            lo = jnp.where(side == 0, 0.0, packs[0])
        dst[at, y : y + SUB] = jnp.where(row < STEPS, hi, pltpu.roll(lo, STEPS, 0))
        dst[at + 1, y : y + SUB] = jnp.where(row < STEPS, pltpu.roll(hi, STEPS, 0), lo)

    groups = [received[2:5]] + ([received[5:8]] if both else [])
    first = 0
    if len(received) == 3:
        below, above, pack = received
        groups = [[pack, below, above]]
        first = STEPS * y // SUB
        for strip, at in ((above, x), (below, x + STEPS)):
            for i in range(STEPS):
                for c in range(y // SUB):
                    dst[at + i, SUB * c : SUB * (c + 1)] = strip[field, i * (y // SUB) + c]

    def main(i, carry):
        put(2 * i, [g[0][field, i] for g in groups])
        return carry

    lax.fori_loop(0, half, main, None, unroll=4)
    for i in range(2):
        put(x + 2 * i, [g[2][field, first + i] for g in groups])
        put(x + STEPS + 2 * i, [g[1][field, first + i] for g in groups])


def coefficient_rows(coef):
    _, wide, rows, z = coef.shape
    lane = lax.broadcasted_iota(jnp.int32, (SUB, z), 1)

    def row(i, carry):
        for c in range(rows // SUB):
            at = pl.ds(SUB * c, SUB)
            spread = coef[0, i, at]
            values = [1.0 - 6.0 * spread]
            for d in range(3):
                half = 0.5 * coef[1 + 2 * d, i, at]
                plus, minus = spread - half, spread + half
                if d == 2:
                    plus = jnp.where(lane == z - 1, 0.0, plus)
                    minus = jnp.where(lane == 0, 0.0, minus)
                values += [plus, minus]
            for s, value in enumerate(values):
                coef[s, i, at] = value
        return carry

    lax.fori_loop(0, wide, row, None)


def sweep(coef, src, first, stop, adjoint, done, write):
    fields, wide, rows, z = src.shape
    chunks, cols = rows // SUB, z // LANES
    sub = lax.broadcasted_iota(jnp.int32, (SUB, LANES), 0)
    lane = lax.broadcasted_iota(jnp.int32, (SUB, LANES), 1)
    first_row, last_row = sub == 0, sub == SUB - 1
    first_lane, last_lane = lane == 0, lane == LANES - 1

    def piece(ref, lead, xi, c, j):
        return ref[lead, xi, SUB * c : SUB * (c + 1), LANES * j : LANES * (j + 1)]

    def body(pair, carry):
        wrap = lambda a: jnp.where(a < 0, a + wide, a)
        base = first + ROWS * pair
        at = [wrap(base + d) for d in range(-1, ROWS + 1)]
        kept = {}

        def load(ref, lead, r, c, j):
            key = (ref is coef, lead, r, c % chunks, j)
            if key not in kept:
                kept[key] = piece(ref, lead, at[r + 1], c % chunks, j)
            return kept[key]

        def scaled(slot, p, r, c, j):
            u = load(src, p, r, c, j)
            return load(coef, slot, r, c, j) * u if adjoint else u

        def turned(slot, shift, p, r, c, j):
            key = ("turned", slot, p, r, c % chunks, j)
            if key not in kept:
                kept[key] = pltpu.roll(scaled(slot, p, r, c, j), shift, 0)
            return kept[key]

        for c in range(done):
            results = []
            for r in range(ROWS):
                plus, minus = {}, {}
                for j in range(cols):
                    for p in range(fields):
                        plus[p, j] = pltpu.roll(scaled(6, p, r, c, j), LANES - 1, 1)
                        minus[p, j] = pltpu.roll(scaled(5, p, r, c, j), 1, 1)
                for j in range(cols):
                    for p in range(fields):
                        u, xp, xm = (load(src, p, r + d, c, j) for d in (0, 1, -1))
                        yp = jnp.where(last_row, turned(4, SUB - 1, p, r, c + 1, j), turned(4, SUB - 1, p, r, c, j))
                        ym = jnp.where(first_row, turned(3, 1, p, r, c - 1, j), turned(3, 1, p, r, c, j))
                        zp = jnp.where(last_lane, plus[p, (j + 1) % cols], plus[p, j])
                        zm = jnp.where(first_lane, minus[p, (j - 1) % cols], minus[p, j])
                        if adjoint:
                            xs = load(coef, 2, r + 1, c, j) * xp + load(coef, 1, r - 1, c, j) * xm
                            ys, zs = yp + ym, zp + zm
                        else:
                            xs = load(coef, 1, r, c, j) * xp + load(coef, 2, r, c, j) * xm
                            ys = load(coef, 3, r, c, j) * yp + load(coef, 4, r, c, j) * ym
                            zs = load(coef, 5, r, c, j) * zp + load(coef, 6, r, c, j) * zm
                        value = (load(coef, 0, r, c, j) * u + xs) + (ys + zs)
                        results.append((p, at[r + 1], c, j, value))
            for result in results:
                write(*result)
        return carry

    lax.fori_loop(0, (stop - first) // ROWS, body, None)


def run_steps(coef, states, out, adjoint, weight=None):
    x, tile_rows = out.shape[1], out.shape[2]
    for step in range(STEPS):
        src, dst = states[step % 2], states[(step + 1) % 2]
        last = step == STEPS - 1

        def write(p, i, c, j, value):
            at = (pl.ds(SUB * c, SUB), pl.ds(LANES * j, LANES))
            if last:
                out[p, i, *at] = value if weight is None else weight[i, *at] * value
            else:
                dst[p, i, *at] = value

        done = (tile_rows if last else src.shape[2]) // SUB
        reach = STEPS - 1 - step
        sweep(coef, src, -reach, x + reach, adjoint, done, write)


def flat_tiles(sources):
    return [ref.at[n] for ref in sources for n in range(ref.shape[0])]


def pack_y_kernel(fields_in, packs, scalars, *refs):
    sources, outs, (buffers, sems) = refs[:fields_in], refs[fields_in:-2], refs[-2:]
    tiles = flat_tiles(sources)
    starts = pack_starts(packs, tiles[0].shape[1], scalars[0])
    copies = Copies(sems)
    for f, tile in enumerate(tiles):
        for n, (start, _) in enumerate(starts):
            copies.start(tile.at[:, pl.ds(start, SUB)], buffers.at[n, f])
    for f in range(len(tiles)):
        for n, (_, last) in enumerate(starts):
            copies.open[f * len(starts) + n].wait()
            write_packs(f, n, lambda i: buffers[n, f, i], last, (None, None) + outs)


def pack_x_kernel(fields_in, *refs):
    sources, (low, high, sems) = refs[:fields_in], refs[fields_in:]
    copies = Copies(sems)
    for f, tile in enumerate(flat_tiles(sources)):
        copies.start(tile.at[pl.ds(0, STEPS)], low.at[f])
        copies.start(tile.at[pl.ds(tile.shape[0] - STEPS, STEPS)], high.at[f])
    copies.wait()


def first_kernel(count, scalars, diffusivity, velocity, probes, weight, *refs):
    side = scalars[0]
    received, coef, out = refs[:count], refs[count], refs[count + 1]
    strips, (state, other, sems) = refs[count + 2 : -3], refs[-3:]
    copies = Copies(sems)
    tiles = [diffusivity.at[0]] + [velocity.at[d] for d in range(3)]
    slots = [coef.at[s] for s in (0, 1, 3, 5)]
    for p in range(probes.shape[0]):
        tiles.append(probes.at[p])
        slots.append(state.at[p])
    for f, (tile, slot) in enumerate(zip(tiles, slots)):
        start_widening(copies, slot, tile, f, received)
    for f, slot in enumerate(slots):
        widen_rows(slot, f, received, side)
    copies.wait()
    coefficient_rows(coef)
    run_steps(coef, (state, other), out, False, weight)
    write_strips(out, strips, side)


def next_kernel(count, adjoint, scalars, coef, tile, *refs):
    side = scalars[0]
    weight = None if adjoint else refs[0]
    refs = refs if adjoint else refs[1:]
    received, out = refs[:count], refs[count]
    strips, (state, other, sems) = refs[count + 1 : -3], refs[-3:]
    fields = tile.shape[0]
    copies = Copies(sems)
    for p in range(fields):
        start_widening(copies, state.at[p], tile.at[p], p, received)
    for p in range(fields):
        widen_rows(state.at[p], p, received, side)
    copies.wait()
    run_steps(coef, (state, other), out, adjoint, weight)
    if strips:
        write_strips(out, strips, side)


def dots_pairs(group, slots):
    return [(s, a, b) for s in range(slots) for a in range(group) for b in range(group) if s or b <= a]


def dots_kernel(scalars, second, *refs):
    passed, out = refs[:-1], refs[-1]
    group, rows, y, z = second.shape
    chunks, cols = y // SUB, z // LANES
    pairs = dots_pairs(group, len(passed))

    def body(i, sums):
        sums = list(sums)
        for c in range(chunks):
            for j in range(cols):
                at = (pl.ds(SUB * c, SUB), pl.ds(LANES * j, LANES))
                mine = [passed[0][a, i, *at] for a in range(group)]
                then = [second[a, i, *at] for a in range(group)]
                other = {(s, b): passed[s][b, i, *at] for s in range(1, len(passed)) for b in range(group)}
                for n, (s, a, b) in enumerate(pairs):
                    value = other[s, b] if s else mine[b]
                    sums[2 * n] = sums[2 * n] + mine[a] * value
                    sums[2 * n + 1] = sums[2 * n + 1] + then[a] * value
        return tuple(sums)

    zero = jnp.zeros((SUB, LANES), jnp.float32)
    sums = lax.fori_loop(0, rows, body, (zero,) * (2 * len(pairs)))
    me = scalars[1]
    count = out.shape[0]
    row = lax.broadcasted_iota(jnp.int32, out.shape, 0)
    lane = lax.broadcasted_iota(jnp.int32, out.shape, 1)
    total = jnp.zeros(out.shape, jnp.float32)
    for n, (s, a, b) in enumerate(pairs):
        for k in range(2):
            value = jnp.sum(jnp.sum(sums[2 * n + k], axis=0, keepdims=True), axis=1, keepdims=True)
            i, j = me * group + a, (me - s) * group + b
            here = (row == i) & (lane == j + k * count) | (row == j) & (lane == i + k * count)
            total = total + jnp.where(here & (me >= s), value, 0.0)
    out[...] = total


def finish_kernel(scale, scalars, inner, *refs):
    images, (basis, projected, held, sems) = refs[:-4], refs[-4:]
    group, x, y, z = held.shape
    count = inner.shape[0]
    me = scalars[1]
    row = lax.broadcasted_iota(jnp.int32, inner.shape, 0)
    lane = lax.broadcasted_iota(jnp.int32, inner.shape, 1)
    base = 2 * count
    work = jnp.where(lane == row + base, 1.0, inner[...] * scale)
    for k in range(count):
        column = jnp.broadcast_to(work[:, k : k + 1], inner.shape)
        pivot = jnp.broadcast_to(column[k : k + 1], inner.shape)
        line = jnp.broadcast_to(work[k : k + 1], inner.shape)
        work = work - jnp.where(row > k, column / pivot, 0.0) * line
    pivots = jnp.sum(jnp.where(lane == row, work, 0.0), axis=1, keepdims=True)
    work = work * (1.0 / jnp.sqrt(pivots))

    factors = []
    for a in range(group):
        factors.append([])
        for s in range(len(images)):
            for b in range(group):
                here = (row == me * group + a) & (lane == base + (me - s) * group + b) & (me >= s)
                value = jnp.sum(jnp.where(here, work, 0.0), axis=0, keepdims=True)
                value = jnp.sum(value, axis=1, keepdims=True)
                factors[a].append(jnp.broadcast_to(value, (SUB, LANES)))

    def body(i, carry):
        for c in range(y // SUB):
            for j in range(z // LANES):
                at = (pl.ds(SUB * c, SUB), pl.ds(LANES * j, LANES))
                values = [image[b, i, *at] for image in images for b in range(group)]
                for a in range(group):
                    terms = [factor * value for factor, value in zip(factors[a], values)]
                    while len(terms) > 1:
                        terms = [sum(terms[n : n + 2][1:], terms[n]) for n in range(0, len(terms), 2)]
                    held[a, i, *at] = terms[0]
        return carry

    copies = Copies(sems)
    for start in range(0, x, SUB):
        lax.fori_loop(start, start + SUB, body, None)
        for a in range(group):
            copies.start(held.at[a, pl.ds(start, SUB)], basis.at[a, pl.ds(start, SUB)])

    left = jnp.where((lane >= count) & (lane < base), work, 0.0)
    right = jnp.where((lane >= count) & (lane < base), pltpu.roll(work, LANES - count, 1), 0.0)
    projected[...] = lax.dot_general(
        left,
        right,
        (((1,), (1,)), ((), ())),
        precision=lax.Precision.HIGHEST,
        preferred_element_type=jnp.float32,
    )
    copies.wait()


def all_sum(value):
    for axis in ("sx", "sy", "probe"):
        devices = lax.axis_size(axis)
        if devices & (devices - 1):
            value = lax.psum(value, axis)
            continue
        move = lambda bits: lax.ppermute(value, axis, [(i, i ^ bits) for i in range(devices)])
        bit = 1
        while bit < devices:
            if 4 * bit <= devices:
                value = (value + move(bit)) + (move(2 * bit) + move(3 * bit))
                bit *= 4
            else:
                value = value + move(bit)
                bit *= 2
    return value


def shards(probes, velocity, diffusivity, obs_weight):
    group, x, y, z = probes.shape
    groups = lax.axis_size("probe")
    count = group * groups
    ncells = x * y * z * lax.axis_size("sx") * lax.axis_size("sy")
    both = lax.axis_size("sy") != 2
    side, mine = lax.axis_index("sy"), lax.axis_index("probe")

    where = jnp.stack([side, mine]).astype(jnp.int32)
    wide = (x + 2 * STEPS, y + 2 * STEPS, z)
    tile = f32(group, x, y, z)
    strips2 = strip_shapes(group, x, y, z, both, not both)
    fields = [diffusivity[None], velocity, probes]
    total = 4 + group

    def scratch(copies):
        return [
            pltpu.VMEM((group,) + wide, jnp.float32),
            pltpu.VMEM((group,) + wide, jnp.float32),
            pltpu.SemaphoreType.DMA((copies,)),
        ]

    packs = 2 if both else 1

    def pack(sources, joined, mib):
        number = sum(a.shape[0] for a in sources)
        outs = strip_shapes(number, x, y, z, both, joined)
        in_y = kernel_call(
            functools.partial(pack_y_kernel, len(sources), packs),
            outs[2:],
            [pltpu.VMEM((packs, number, x, SUB, z), jnp.float32), pltpu.SemaphoreType.DMA((number * packs,))],
            [where] + sources,
            2.0,
            mib,
            anywhere=range(1, len(sources) + 1),
        )
        in_x = kernel_call(
            functools.partial(pack_x_kernel, len(sources)),
            outs[:2],
            [pltpu.SemaphoreType.DMA((2 * number,))],
            sources,
            2.0,
            mib,
            anywhere=range(len(sources)),
            scalars=False,
        )
        return list(in_x) + list(in_y)

    def right(value, hops):
        return lax.ppermute(value, "probe", [(i, i + hops) for i in range(groups - hops)])

    strips = pack(fields, False, 56)
    strips[2], leaving = lax.optimization_barrier((strips[2], probes))
    next_probes = right(leaving, 1)
    received = exchange(strips)
    coef, halfway, *strips = kernel_call(
        functools.partial(first_kernel, len(received)),
        [f32(7, *wide), tile] + strips2,
        scratch(3 * total),
        [where] + fields + [obs_weight] + received,
        4.0,
        14,
        anywhere=(1, 2, 3, 5, 6),
    )

    def model(field, received, adjoint, last=False):
        ins = [where, coef, field] + ([] if adjoint else [obs_weight])
        return kernel_call(
            functools.partial(next_kernel, len(received), adjoint),
            [tile] + ([] if last else strips2),
            scratch(3 * group),
            ins + received,
            8.0,
            14,
            anywhere=(2, len(ins), len(ins) + 1) if both else (2,),
        )

    next_probes, halfway = lax.optimization_barrier((next_probes, halfway))
    strips_next = pack([next_probes], not both, 8)
    images, *strips = model(halfway, exchange(strips), True)
    far = [right(images, hops) for hops in range(3, groups)]

    received, _ = lax.optimization_barrier((exchange(strips_next), images))
    half_next, *strips_next = model(next_probes, received, False)
    strips, half_next = lax.optimization_barrier((strips, half_next))
    (images_next,) = model(half_next, exchange(strips_next), True, True)
    shifting, far = lax.optimization_barrier((images_next, far))
    passed = [images, images_next, right(shifting, 1)] + far

    received = exchange(strips, after=images_next)
    halfway, *strips = model(images, received, False)
    (second,) = model(halfway, exchange(strips), True, True)

    (partial,) = kernel_call(
        dots_kernel,
        [f32(count, LANES)],
        [],
        [where, second] + passed,
        4.0,
        14,
    )
    basis, projected = kernel_call(
        functools.partial(finish_kernel, 1.0 / ncells),
        [tile, f32(count, count)],
        [pltpu.VMEM((group, x, y, z), jnp.float32), pltpu.SemaphoreType.DMA((group * (x // SUB),))],
        [where, all_sum(partial)] + passed,
        5.0,
        14,
        outs_anywhere=(0,),
    )
    return (basis, projected)


def solution(mesh):
    return jax.shard_map(
        shards,
        mesh=mesh,
        in_specs=(
            P("probe", "sx", "sy", None),
            P(None, "sx", "sy", None),
            P("sx", "sy", None),
            P("sx", "sy", None),
        ),
        out_specs=(P("probe", "sx", "sy", None), P()),
        check_vma=False,
    )
```

```python
import functools

import jax
import jax.numpy as jnp
from jax import lax
from jax.experimental import pallas as pl
from jax.experimental.pallas import tpu as pltpu
from jax.sharding import PartitionSpec as P

STEPS = 4
SUB = 8
LANES = 128
ROWS = 2
MIB = 1024 * 1024
FLOPS_PER_MICRO = 1.15e9
BYTES_PER_MICRO = 3.6e6


def kernel_call(body, outs, scratch, ins, micros, mib, anywhere=(), outs_anywhere=(), scalars=True):
    spec = lambda n, names: pl.BlockSpec(memory_space=pl.ANY if n in names else pltpu.VMEM)
    specs = [spec(n, anywhere) for n in range(len(ins))]
    if scalars:
        specs[0] = pl.BlockSpec(memory_space=pltpu.SMEM)
    return pl.pallas_call(
        body,
        out_shape=outs,
        in_specs=specs,
        out_specs=[spec(n, outs_anywhere) for n in range(len(outs))],
        scratch_shapes=scratch,
        compiler_params=pltpu.CompilerParams(vmem_limit_bytes=mib * MIB),
        cost_estimate=pl.CostEstimate(
            flops=int(micros * FLOPS_PER_MICRO),
            bytes_accessed=int(micros * BYTES_PER_MICRO),
            transcendentals=0,
        ),
    )(*ins)


def f32(*shape):
    return jax.ShapeDtypeStruct(shape, jnp.float32)


def strip_shapes(fields, x, y, z, both, joined=False):
    packs = [f32(fields, x // 2, SUB, z)] + [f32(fields, 2, SUB, z)] * (0 if joined else 2)
    return [f32(fields, STEPS, y, z)] * 2 + packs * (2 if both else 1)


def pack_starts(packs, y, side):
    if packs == 2:
        return [(0, False), (y - SUB, True)]
    return [(pl.multiple_of(jnp.where(side == 0, y - SUB, 0), SUB), side == 0)]


def packed_pair(row, first, second, last):
    hi = lambda: jnp.where(row < STEPS, pltpu.roll(first, STEPS, 0), second)
    lo = lambda: jnp.where(row < STEPS, first, pltpu.roll(second, STEPS, 0))
    if isinstance(last, bool):
        return hi() if last else lo()
    return jnp.where(last, hi(), lo())


def write_packs(field, n, rows, last, outs):
    pack, *corners = outs[2 + 3 * n : 5 + 3 * n]
    half, z = pack.shape[1], pack.shape[3]
    row = lax.broadcasted_iota(jnp.int32, (SUB, z), 0)

    def step(i, carry):
        pack[field, i] = packed_pair(row, rows(2 * i), rows(2 * i + 1), last)
        return carry

    lax.fori_loop(0, half, step, None, unroll=4)
    for corner, start in zip(corners, (0, half - 2)):
        for i in range(2):
            corner[field, i] = pack[field, start + i]


def write_strips(tile, outs, side):
    fields, x, y, _ = tile.shape
    for p in range(fields):
        for i in range(STEPS):
            outs[0][p, i] = tile[p, i]
            outs[1][p, i] = tile[p, x - STEPS + i]
        for n, (start, last) in enumerate(pack_starts(max((len(outs) - 2) // 3, 1), y, side)):
            write_packs(p, n, lambda i: tile[p, i, pl.ds(start, SUB)], last, outs)


def join_kernel(xlo, xhi, pack, lo, hi):
    fields, steps, y, _ = xlo.shape
    chunks, half = y // SUB, pack.shape[1]
    for f in range(fields):
        for strip, out, start in ((xlo, lo, 0), (xhi, hi, half - 2)):
            for i in range(steps):
                for c in range(chunks):
                    out[f, i * chunks + c] = strip[f, i, SUB * c : SUB * (c + 1)]
            for i in range(2):
                out[f, steps * chunks + i] = pack[f, start + i]


def join(xlo, xhi, pack):
    fields, steps, y, z = xlo.shape
    out = f32(fields, steps * y // SUB + 2, SUB, z)
    return kernel_call(join_kernel, [out, out], [], [xlo, xhi, pack], 1.0, 8, scalars=False)


def exchange(strips, after=None):
    nx, ny = lax.axis_size("sx"), lax.axis_size("sy")
    up = [(i, i + 1) for i in range(nx - 1)]
    down = [(j, i) for i, j in up]

    def moved(value, dx, dys):
        pairs = []
        for i in range(nx):
            for j in range(ny):
                for dy in dys(j):
                    if 0 <= i + dx < nx and 0 <= j + dy < ny:
                        pairs.append((i * ny + j, (i + dx) * ny + j + dy))
        return lax.ppermute(value, ("sx", "sy"), pairs)

    if len(strips) == 3:
        pack = moved(strips[2], 0, lambda j: (1 - 2 * j,))
        if after is not None:
            strips, pack, _ = lax.optimization_barrier((strips, pack, after))
        lo, hi = join(strips[0], strips[1], pack)
        return [lax.ppermute(hi, "sx", up), lax.ppermute(lo, "sx", down), pack]
    below = lax.ppermute(strips[1], "sx", up)
    above = lax.ppermute(strips[0], "sx", down)
    received = [below, above]
    if len(strips) == 5:
        flip = lambda j: (1 - 2 * j,)
        pack, corner_lo, corner_hi = strips[2:]
        received += [moved(pack, 0, flip), moved(corner_hi, 1, flip), moved(corner_lo, -1, flip)]
    else:
        for n, dy in ((0, -1), (1, 1)):
            pack, corner_lo, corner_hi = strips[2 + 3 * n : 5 + 3 * n]
            one = lambda j, dy=dy: (dy,)
            received += [moved(pack, 0, one), moved(corner_hi, 1, one), moved(corner_lo, -1, one)]
    return received


class Copies:
    def __init__(self, sems):
        self.sems, self.open, self.used = sems, [], 0

    def start(self, src, dst):
        copy = pltpu.make_async_copy(src, dst, self.sems.at[self.used])
        self.used += 1
        copy.start()
        self.open.append(copy)
        return copy

    def wait(self):
        for copy in self.open:
            copy.wait()
        self.open = []


def start_widening(copies, dst, tile, field, received):
    x, y = tile.shape[0], tile.shape[1]
    copies.start(tile, dst.at[pl.ds(0, x), pl.ds(0, y)])
    if len(received) == 3:
        return
    copies.start(received[1].at[field], dst.at[pl.ds(x, STEPS), pl.ds(0, y)])
    copies.start(received[0].at[field], dst.at[pl.ds(x + STEPS, STEPS), pl.ds(0, y)])


def widen_rows(dst, field, received, side):
    half, z = received[2].shape[1], received[2].shape[3]
    x, y = 2 * half, dst.shape[1] - SUB
    row = lax.broadcasted_iota(jnp.int32, (SUB, z), 0)
    both = len(received) > 5

    def put(at, packs):
        if both:
            hi, lo = packs
        else:
            hi = jnp.where(side == 0, packs[0], 0.0)
            lo = jnp.where(side == 0, 0.0, packs[0])
        dst[at, y : y + SUB] = jnp.where(row < STEPS, hi, pltpu.roll(lo, STEPS, 0))
        dst[at + 1, y : y + SUB] = jnp.where(row < STEPS, pltpu.roll(hi, STEPS, 0), lo)

    groups = [received[2:5]] + ([received[5:8]] if both else [])
    first = 0
    if len(received) == 3:
        below, above, pack = received
        groups = [[pack, below, above]]
        first = STEPS * y // SUB
        for strip, at in ((above, x), (below, x + STEPS)):
            for i in range(STEPS):
                for c in range(y // SUB):
                    dst[at + i, SUB * c : SUB * (c + 1)] = strip[field, i * (y // SUB) + c]

    def main(i, carry):
        put(2 * i, [g[0][field, i] for g in groups])
        return carry

    lax.fori_loop(0, half, main, None, unroll=4)
    for i in range(2):
        put(x + 2 * i, [g[2][field, first + i] for g in groups])
        put(x + STEPS + 2 * i, [g[1][field, first + i] for g in groups])


def coefficient_rows(coef):
    _, wide, rows, z = coef.shape
    lane = lax.broadcasted_iota(jnp.int32, (SUB, z), 1)

    def row(i, carry):
        for c in range(rows // SUB):
            at = pl.ds(SUB * c, SUB)
            spread = coef[0, i, at]
            values = [1.0 - 6.0 * spread]
            for d in range(3):
                half = 0.5 * coef[1 + 2 * d, i, at]
                plus, minus = spread - half, spread + half
                if d == 2:
                    plus = jnp.where(lane == z - 1, 0.0, plus)
                    minus = jnp.where(lane == 0, 0.0, minus)
                values += [plus, minus]
            for s, value in enumerate(values):
                coef[s, i, at] = value
        return carry

    lax.fori_loop(0, wide, row, None)


def sweep(coef, src, first, stop, adjoint, done, write):
    fields, wide, rows, z = src.shape
    chunks, cols = rows // SUB, z // LANES
    sub = lax.broadcasted_iota(jnp.int32, (SUB, LANES), 0)
    lane = lax.broadcasted_iota(jnp.int32, (SUB, LANES), 1)
    first_row, last_row = sub == 0, sub == SUB - 1
    first_lane, last_lane = lane == 0, lane == LANES - 1

    def piece(ref, lead, xi, c, j):
        return ref[lead, xi, SUB * c : SUB * (c + 1), LANES * j : LANES * (j + 1)]

    def body(pair, carry):
        wrap = lambda a: jnp.where(a < 0, a + wide, a)
        base = first + ROWS * pair
        at = [wrap(base + d) for d in range(-1, ROWS + 1)]
        kept = {}

        def load(ref, lead, r, c, j):
            key = (ref is coef, lead, r, c % chunks, j)
            if key not in kept:
                kept[key] = piece(ref, lead, at[r + 1], c % chunks, j)
            return kept[key]

        def scaled(slot, p, r, c, j):
            u = load(src, p, r, c, j)
            return load(coef, slot, r, c, j) * u if adjoint else u

        def turned(slot, shift, p, r, c, j):
            key = ("turned", slot, p, r, c % chunks, j)
            if key not in kept:
                kept[key] = pltpu.roll(scaled(slot, p, r, c, j), shift, 0)
            return kept[key]

        for c in range(done):
            results = []
            for r in range(ROWS):
                plus, minus = {}, {}
                for j in range(cols):
                    for p in range(fields):
                        plus[p, j] = pltpu.roll(scaled(6, p, r, c, j), LANES - 1, 1)
                        minus[p, j] = pltpu.roll(scaled(5, p, r, c, j), 1, 1)
                for j in range(cols):
                    for p in range(fields):
                        u, xp, xm = (load(src, p, r + d, c, j) for d in (0, 1, -1))
                        yp = jnp.where(last_row, turned(4, SUB - 1, p, r, c + 1, j), turned(4, SUB - 1, p, r, c, j))
                        ym = jnp.where(first_row, turned(3, 1, p, r, c - 1, j), turned(3, 1, p, r, c, j))
                        zp = jnp.where(last_lane, plus[p, (j + 1) % cols], plus[p, j])
                        zm = jnp.where(first_lane, minus[p, (j - 1) % cols], minus[p, j])
                        if adjoint:
                            xs = load(coef, 2, r + 1, c, j) * xp + load(coef, 1, r - 1, c, j) * xm
                            ys, zs = yp + ym, zp + zm
                        else:
                            xs = load(coef, 1, r, c, j) * xp + load(coef, 2, r, c, j) * xm
                            ys = load(coef, 3, r, c, j) * yp + load(coef, 4, r, c, j) * ym
                            zs = load(coef, 5, r, c, j) * zp + load(coef, 6, r, c, j) * zm
                        value = (load(coef, 0, r, c, j) * u + xs) + (ys + zs)
                        results.append((p, at[r + 1], c, j, value))
            for result in results:
                write(*result)
        return carry

    lax.fori_loop(0, (stop - first) // ROWS, body, None)


def run_steps(coef, states, out, adjoint, weight=None):
    x, tile_rows = out.shape[1], out.shape[2]
    for step in range(STEPS):
        src, dst = states[step % 2], states[(step + 1) % 2]
        last = step == STEPS - 1

        def write(p, i, c, j, value):
            at = (pl.ds(SUB * c, SUB), pl.ds(LANES * j, LANES))
            if last:
                out[p, i, *at] = value if weight is None else weight[i, *at] * value
            else:
                dst[p, i, *at] = value

        done = (tile_rows if last else src.shape[2]) // SUB
        reach = STEPS - 1 - step
        sweep(coef, src, -reach, x + reach, adjoint, done, write)


def flat_tiles(sources):
    return [ref.at[n] for ref in sources for n in range(ref.shape[0])]


def pack_y_kernel(fields_in, packs, scalars, *refs):
    sources, outs, (buffers, sems) = refs[:fields_in], refs[fields_in:-2], refs[-2:]
    tiles = flat_tiles(sources)
    starts = pack_starts(packs, tiles[0].shape[1], scalars[0])
    copies = Copies(sems)
    for f, tile in enumerate(tiles):
        for n, (start, _) in enumerate(starts):
            copies.start(tile.at[:, pl.ds(start, SUB)], buffers.at[n, f])
    for f in range(len(tiles)):
        for n, (_, last) in enumerate(starts):
            copies.open[f * len(starts) + n].wait()
            write_packs(f, n, lambda i: buffers[n, f, i], last, (None, None) + outs)


def pack_x_kernel(fields_in, *refs):
    sources, (low, high, sems) = refs[:fields_in], refs[fields_in:]
    copies = Copies(sems)
    for f, tile in enumerate(flat_tiles(sources)):
        copies.start(tile.at[pl.ds(0, STEPS)], low.at[f])
        copies.start(tile.at[pl.ds(tile.shape[0] - STEPS, STEPS)], high.at[f])
    copies.wait()


def first_kernel(count, scalars, diffusivity, velocity, probes, weight, *refs):
    side = scalars[0]
    received, coef, out = refs[:count], refs[count], refs[count + 1]
    strips, (state, other, sems) = refs[count + 2 : -3], refs[-3:]
    copies = Copies(sems)
    tiles = [diffusivity.at[0]] + [velocity.at[d] for d in range(3)]
    slots = [coef.at[s] for s in (0, 1, 3, 5)]
    for p in range(probes.shape[0]):
        tiles.append(probes.at[p])
        slots.append(state.at[p])
    for f, (tile, slot) in enumerate(zip(tiles, slots)):
        start_widening(copies, slot, tile, f, received)
    for f, slot in enumerate(slots):
        widen_rows(slot, f, received, side)
    copies.wait()
    coefficient_rows(coef)
    run_steps(coef, (state, other), out, False, weight)
    write_strips(out, strips, side)


def next_kernel(count, adjoint, scalars, coef, tile, *refs):
    side = scalars[0]
    weight = None if adjoint else refs[0]
    refs = refs if adjoint else refs[1:]
    received, out = refs[:count], refs[count]
    strips, (state, other, sems) = refs[count + 1 : -3], refs[-3:]
    fields = tile.shape[0]
    copies = Copies(sems)
    for p in range(fields):
        start_widening(copies, state.at[p], tile.at[p], p, received)
    for p in range(fields):
        widen_rows(state.at[p], p, received, side)
    copies.wait()
    run_steps(coef, (state, other), out, adjoint, weight)
    if strips:
        write_strips(out, strips, side)


def dots_pairs(group, slots):
    return [(s, a, b) for s in range(slots) for a in range(group) for b in range(group) if s or b <= a]


def dots_kernel(scalars, second, *refs):
    passed, out = refs[:-1], refs[-1]
    group, rows, y, z = second.shape
    chunks, cols = y // SUB, z // LANES
    pairs = dots_pairs(group, len(passed))

    def body(i, sums):
        sums = list(sums)
        for c in range(chunks):
            for j in range(cols):
                at = (pl.ds(SUB * c, SUB), pl.ds(LANES * j, LANES))
                mine = [passed[0][a, i, *at] for a in range(group)]
                then = [second[a, i, *at] for a in range(group)]
                other = {(s, b): passed[s][b, i, *at] for s in range(1, len(passed)) for b in range(group)}
                for n, (s, a, b) in enumerate(pairs):
                    value = other[s, b] if s else mine[b]
                    sums[2 * n] = sums[2 * n] + mine[a] * value
                    sums[2 * n + 1] = sums[2 * n + 1] + then[a] * value
        return tuple(sums)

    zero = jnp.zeros((SUB, LANES), jnp.float32)
    sums = lax.fori_loop(0, rows, body, (zero,) * (2 * len(pairs)))
    me = scalars[1]
    count = out.shape[0]
    row = lax.broadcasted_iota(jnp.int32, out.shape, 0)
    lane = lax.broadcasted_iota(jnp.int32, out.shape, 1)
    total = jnp.zeros(out.shape, jnp.float32)
    for n, (s, a, b) in enumerate(pairs):
        for k in range(2):
            value = jnp.sum(jnp.sum(sums[2 * n + k], axis=0, keepdims=True), axis=1, keepdims=True)
            i, j = me * group + a, (me - s) * group + b
            here = (row == i) & (lane == j + k * count) | (row == j) & (lane == i + k * count)
            total = total + jnp.where(here & (me >= s), value, 0.0)
    out[...] = total


def finish_kernel(scale, scalars, inner, *refs):
    images, (basis, projected, held, sems) = refs[:-4], refs[-4:]
    group, x, y, z = held.shape
    count = inner.shape[0]
    me = scalars[1]
    row = lax.broadcasted_iota(jnp.int32, inner.shape, 0)
    lane = lax.broadcasted_iota(jnp.int32, inner.shape, 1)
    base = 2 * count
    work = jnp.where(lane == row + base, 1.0, inner[...] * scale)
    for k in range(count):
        column = jnp.broadcast_to(work[:, k : k + 1], inner.shape)
        pivot = jnp.broadcast_to(column[k : k + 1], inner.shape)
        line = jnp.broadcast_to(work[k : k + 1], inner.shape)
        work = work - jnp.where(row > k, column / pivot, 0.0) * line
    pivots = jnp.sum(jnp.where(lane == row, work, 0.0), axis=1, keepdims=True)
    work = work * (1.0 / jnp.sqrt(pivots))

    factors = []
    for a in range(group):
        factors.append([])
        for s in range(len(images)):
            for b in range(group):
                here = (row == me * group + a) & (lane == base + (me - s) * group + b) & (me >= s)
                value = jnp.sum(jnp.where(here, work, 0.0), axis=0, keepdims=True)
                value = jnp.sum(value, axis=1, keepdims=True)
                factors[a].append(jnp.broadcast_to(value, (SUB, LANES)))

    def body(i, carry):
        for c in range(y // SUB):
            for j in range(z // LANES):
                at = (pl.ds(SUB * c, SUB), pl.ds(LANES * j, LANES))
                values = [image[b, i, *at] for image in images for b in range(group)]
                for a in range(group):
                    terms = [factor * value for factor, value in zip(factors[a], values)]
                    while len(terms) > 1:
                        terms = [sum(terms[n : n + 2][1:], terms[n]) for n in range(0, len(terms), 2)]
                    held[a, i, *at] = terms[0]
        return carry

    copies = Copies(sems)
    for start in range(0, x, SUB):
        lax.fori_loop(start, start + SUB, body, None)
        for a in range(group):
            copies.start(held.at[a, pl.ds(start, SUB)], basis.at[a, pl.ds(start, SUB)])

    left = jnp.where((lane >= count) & (lane < base), work, 0.0)
    right = jnp.where((lane >= count) & (lane < base), pltpu.roll(work, LANES - count, 1), 0.0)
    projected[...] = lax.dot_general(
        left,
        right,
        (((1,), (1,)), ((), ())),
        precision=lax.Precision.HIGHEST,
        preferred_element_type=jnp.float32,
    )
    copies.wait()


def all_sum(value):
    for axis in ("sx", "sy", "probe"):
        devices = lax.axis_size(axis)
        if devices & (devices - 1):
            value = lax.psum(value, axis)
            continue
        move = lambda bits: lax.ppermute(value, axis, [(i, i ^ bits) for i in range(devices)])
        bit = 1
        while bit < devices:
            if 4 * bit <= devices:
                value = (value + move(bit)) + (move(2 * bit) + move(3 * bit))
                bit *= 4
            else:
                value = value + move(bit)
                bit *= 2
    return value


def shards(probes, velocity, diffusivity, obs_weight):
    group, x, y, z = probes.shape
    groups = lax.axis_size("probe")
    count = group * groups
    ncells = x * y * z * lax.axis_size("sx") * lax.axis_size("sy")
    both = lax.axis_size("sy") != 2
    side, mine = lax.axis_index("sy"), lax.axis_index("probe")

    where = jnp.stack([side, mine]).astype(jnp.int32)
    wide = (x + 2 * STEPS, y + 2 * STEPS, z)
    tile = f32(group, x, y, z)
    strips2 = strip_shapes(group, x, y, z, both, not both)
    fields = [diffusivity[None], velocity, probes]
    total = 4 + group

    def scratch(copies):
        return [
            pltpu.VMEM((group,) + wide, jnp.float32),
            pltpu.VMEM((group,) + wide, jnp.float32),
            pltpu.SemaphoreType.DMA((copies,)),
        ]

    packs = 2 if both else 1

    def pack(sources, joined, mib):
        number = sum(a.shape[0] for a in sources)
        outs = strip_shapes(number, x, y, z, both, joined)
        in_y = kernel_call(
            functools.partial(pack_y_kernel, len(sources), packs),
            outs[2:],
            [pltpu.VMEM((packs, number, x, SUB, z), jnp.float32), pltpu.SemaphoreType.DMA((number * packs,))],
            [where] + sources,
            2.0,
            mib,
            anywhere=range(1, len(sources) + 1),
        )
        in_x = kernel_call(
            functools.partial(pack_x_kernel, len(sources)),
            outs[:2],
            [pltpu.SemaphoreType.DMA((2 * number,))],
            sources,
            2.0,
            min(mib, 12),
            anywhere=range(len(sources)),
            scalars=False,
        )
        return list(in_x) + list(in_y)

    def right(value, hops):
        return lax.ppermute(value, "probe", [(i, i + hops) for i in range(groups - hops)])

    strips = pack(fields, False, 56)
    strips[2], leaving = lax.optimization_barrier((strips[2], probes))
    next_probes = right(leaving, 1)
    received = exchange(strips)
    coef, halfway, *strips = kernel_call(
        functools.partial(first_kernel, len(received)),
        [f32(7, *wide), tile] + strips2,
        scratch(3 * total),
        [where] + fields + [obs_weight] + received,
        4.0,
        14,
        anywhere=(1, 2, 3, 5, 6),
    )

    def model(field, received, adjoint, last=False, micros=8.0):
        ins = [where, coef, field] + ([] if adjoint else [obs_weight])
        return kernel_call(
            functools.partial(next_kernel, len(received), adjoint),
            [tile] + ([] if last else strips2),
            scratch(3 * group),
            ins + received,
            micros,
            14,
            anywhere=(2, len(ins), len(ins) + 1) if both else (2,),
        )

    next_probes, halfway = lax.optimization_barrier((next_probes, halfway))
    strips_next = pack([next_probes], not both, 8)
    images, *strips = model(halfway, exchange(strips), True)
    far = [right(images, hops) for hops in range(3, groups)]

    received, _ = lax.optimization_barrier((exchange(strips_next), images))
    half_next, *strips_next = model(next_probes, received, False)
    strips, half_next = lax.optimization_barrier((strips, half_next))
    (images_next,) = model(half_next, exchange(strips_next), True, True)
    shifting, far = lax.optimization_barrier((images_next, far))
    passed = [images, images_next, right(shifting, 1)] + far

    received = exchange(strips, after=images_next)
    halfway, *strips = model(images, received, False, micros=5.0)
    (second,) = model(halfway, exchange(strips), True, True, micros=5.0)

    (partial,) = kernel_call(
        dots_kernel,
        [f32(count, LANES)],
        [],
        [where, second] + passed,
        4.0,
        14,
    )
    basis, projected = kernel_call(
        functools.partial(finish_kernel, 1.0 / ncells),
        [tile, f32(count, count)],
        [pltpu.VMEM((group, x, y, z), jnp.float32), pltpu.SemaphoreType.DMA((group * (x // SUB),))],
        [where, all_sum(partial)] + passed,
        5.0,
        14,
        outs_anywhere=(0,),
    )
    return (basis, projected)


def solution(mesh):
    return jax.shard_map(
        shards,
        mesh=mesh,
        in_specs=(
            P("probe", "sx", "sy", None),
            P(None, "sx", "sy", None),
            P("sx", "sy", None),
            P("sx", "sy", None),
        ),
        out_specs=(P("probe", "sx", "sy", None), P()),
        check_vma=False,
    )
```

```python
import functools

import jax
import jax.numpy as jnp
from jax import lax
from jax.experimental import pallas as pl
from jax.experimental.pallas import tpu as pltpu
from jax.sharding import PartitionSpec as P

STEPS = 4
SUB = 8
LANES = 128
ROWS = 2
MIB = 1024 * 1024
FLOPS_PER_MICRO = 1.15e9
BYTES_PER_MICRO = 3.6e6


def kernel_call(body, outs, scratch, ins, micros, mib, anywhere=(), outs_anywhere=(), scalars=True):
    spec = lambda n, names: pl.BlockSpec(memory_space=pl.ANY if n in names else pltpu.VMEM)
    specs = [spec(n, anywhere) for n in range(len(ins))]
    if scalars:
        specs[0] = pl.BlockSpec(memory_space=pltpu.SMEM)
    return pl.pallas_call(
        body,
        out_shape=outs,
        in_specs=specs,
        out_specs=[spec(n, outs_anywhere) for n in range(len(outs))],
        scratch_shapes=scratch,
        compiler_params=pltpu.CompilerParams(vmem_limit_bytes=mib * MIB),
        cost_estimate=pl.CostEstimate(
            flops=int(micros * FLOPS_PER_MICRO),
            bytes_accessed=int(micros * BYTES_PER_MICRO),
            transcendentals=0,
        ),
    )(*ins)


def f32(*shape):
    return jax.ShapeDtypeStruct(shape, jnp.float32)


def strip_shapes(fields, x, y, z, both, joined=False):
    packs = [f32(fields, x // 2, SUB, z)] + [f32(fields, 2, SUB, z)] * (0 if joined else 2)
    return [f32(fields, STEPS, y, z)] * 2 + packs * (2 if both else 1)


def pack_starts(packs, y, side):
    if packs == 2:
        return [(0, False), (y - SUB, True)]
    return [(pl.multiple_of(jnp.where(side == 0, y - SUB, 0), SUB), side == 0)]


def packed_pair(row, first, second, last):
    hi = lambda: jnp.where(row < STEPS, pltpu.roll(first, STEPS, 0), second)
    lo = lambda: jnp.where(row < STEPS, first, pltpu.roll(second, STEPS, 0))
    if isinstance(last, bool):
        return hi() if last else lo()
    return jnp.where(last, hi(), lo())


def write_packs(field, n, rows, last, outs):
    pack, *corners = outs[2 + 3 * n : 5 + 3 * n]
    half, z = pack.shape[1], pack.shape[3]
    row = lax.broadcasted_iota(jnp.int32, (SUB, z), 0)

    def step(i, carry):
        pack[field, i] = packed_pair(row, rows(2 * i), rows(2 * i + 1), last)
        return carry

    lax.fori_loop(0, half, step, None, unroll=4)
    for corner, start in zip(corners, (0, half - 2)):
        for i in range(2):
            corner[field, i] = pack[field, start + i]


def write_strips(tile, outs, side):
    fields, x, y, _ = tile.shape
    for p in range(fields):
        for i in range(STEPS):
            outs[0][p, i] = tile[p, i]
            outs[1][p, i] = tile[p, x - STEPS + i]
        for n, (start, last) in enumerate(pack_starts(max((len(outs) - 2) // 3, 1), y, side)):
            write_packs(p, n, lambda i: tile[p, i, pl.ds(start, SUB)], last, outs)


def join_kernel(xlo, xhi, pack, lo, hi):
    fields, steps, y, _ = xlo.shape
    chunks, half = y // SUB, pack.shape[1]
    for f in range(fields):
        for strip, out, start in ((xlo, lo, 0), (xhi, hi, half - 2)):
            for i in range(steps):
                for c in range(chunks):
                    out[f, i * chunks + c] = strip[f, i, SUB * c : SUB * (c + 1)]
            for i in range(2):
                out[f, steps * chunks + i] = pack[f, start + i]


def join(xlo, xhi, pack):
    fields, steps, y, z = xlo.shape
    out = f32(fields, steps * y // SUB + 2, SUB, z)
    return kernel_call(join_kernel, [out, out], [], [xlo, xhi, pack], 1.0, 8, scalars=False)


def exchange(strips, after=None):
    nx, ny = lax.axis_size("sx"), lax.axis_size("sy")
    up = [(i, i + 1) for i in range(nx - 1)]
    down = [(j, i) for i, j in up]

    def moved(value, dx, dys):
        pairs = []
        for i in range(nx):
            for j in range(ny):
                for dy in dys(j):
                    if 0 <= i + dx < nx and 0 <= j + dy < ny:
                        pairs.append((i * ny + j, (i + dx) * ny + j + dy))
        return lax.ppermute(value, ("sx", "sy"), pairs)

    if len(strips) == 3:
        pack = moved(strips[2], 0, lambda j: (1 - 2 * j,))
        if after is not None:
            strips, pack, _ = lax.optimization_barrier((strips, pack, after))
        lo, hi = join(strips[0], strips[1], pack)
        return [lax.ppermute(hi, "sx", up), lax.ppermute(lo, "sx", down), pack]
    below = lax.ppermute(strips[1], "sx", up)
    above = lax.ppermute(strips[0], "sx", down)
    received = [below, above]
    if len(strips) == 5:
        flip = lambda j: (1 - 2 * j,)
        pack, corner_lo, corner_hi = strips[2:]
        received += [moved(pack, 0, flip), moved(corner_hi, 1, flip), moved(corner_lo, -1, flip)]
    else:
        for n, dy in ((0, -1), (1, 1)):
            pack, corner_lo, corner_hi = strips[2 + 3 * n : 5 + 3 * n]
            one = lambda j, dy=dy: (dy,)
            received += [moved(pack, 0, one), moved(corner_hi, 1, one), moved(corner_lo, -1, one)]
    return received


class Copies:
    def __init__(self, sems):
        self.sems, self.open, self.used = sems, [], 0

    def start(self, src, dst):
        copy = pltpu.make_async_copy(src, dst, self.sems.at[self.used])
        self.used += 1
        copy.start()
        self.open.append(copy)
        return copy

    def wait(self):
        for copy in self.open:
            copy.wait()
        self.open = []


def start_widening(copies, dst, tile, field, received):
    x, y = tile.shape[0], tile.shape[1]
    copies.start(tile, dst.at[pl.ds(0, x), pl.ds(0, y)])
    if len(received) == 3:
        return
    copies.start(received[1].at[field], dst.at[pl.ds(x, STEPS), pl.ds(0, y)])
    copies.start(received[0].at[field], dst.at[pl.ds(x + STEPS, STEPS), pl.ds(0, y)])


def widen_rows(dst, field, received, side):
    half, z = received[2].shape[1], received[2].shape[3]
    x, y = 2 * half, dst.shape[1] - SUB
    row = lax.broadcasted_iota(jnp.int32, (SUB, z), 0)
    both = len(received) > 5

    def put(at, packs):
        if both:
            hi, lo = packs
        else:
            hi = jnp.where(side == 0, packs[0], 0.0)
            lo = jnp.where(side == 0, 0.0, packs[0])
        dst[at, y : y + SUB] = jnp.where(row < STEPS, hi, pltpu.roll(lo, STEPS, 0))
        dst[at + 1, y : y + SUB] = jnp.where(row < STEPS, pltpu.roll(hi, STEPS, 0), lo)

    groups = [received[2:5]] + ([received[5:8]] if both else [])
    first = 0
    if len(received) == 3:
        below, above, pack = received
        groups = [[pack, below, above]]
        first = STEPS * y // SUB
        for strip, at in ((above, x), (below, x + STEPS)):
            for i in range(STEPS):
                for c in range(y // SUB):
                    dst[at + i, SUB * c : SUB * (c + 1)] = strip[field, i * (y // SUB) + c]

    def main(i, carry):
        put(2 * i, [g[0][field, i] for g in groups])
        return carry

    lax.fori_loop(0, half, main, None, unroll=4)
    for i in range(2):
        put(x + 2 * i, [g[2][field, first + i] for g in groups])
        put(x + STEPS + 2 * i, [g[1][field, first + i] for g in groups])


def coefficient_rows(coef):
    _, wide, rows, z = coef.shape
    lane = lax.broadcasted_iota(jnp.int32, (SUB, z), 1)

    def row(i, carry):
        for c in range(rows // SUB):
            at = pl.ds(SUB * c, SUB)
            spread = coef[0, i, at]
            values = [1.0 - 6.0 * spread]
            for d in range(3):
                half = 0.5 * coef[1 + 2 * d, i, at]
                plus, minus = spread - half, spread + half
                if d == 2:
                    plus = jnp.where(lane == z - 1, 0.0, plus)
                    minus = jnp.where(lane == 0, 0.0, minus)
                values += [plus, minus]
            for s, value in enumerate(values):
                coef[s, i, at] = value
        return carry

    lax.fori_loop(0, wide, row, None)


def sweep(coef, src, first, stop, adjoint, done, write):
    fields, wide, rows, z = src.shape
    chunks, cols = rows // SUB, z // LANES
    sub = lax.broadcasted_iota(jnp.int32, (SUB, LANES), 0)
    lane = lax.broadcasted_iota(jnp.int32, (SUB, LANES), 1)
    first_row, last_row = sub == 0, sub == SUB - 1
    first_lane, last_lane = lane == 0, lane == LANES - 1

    def piece(ref, lead, xi, c, j):
        return ref[lead, xi, SUB * c : SUB * (c + 1), LANES * j : LANES * (j + 1)]

    def body(pair, carry):
        wrap = lambda a: jnp.where(a < 0, a + wide, a)
        base = first + ROWS * pair
        at = [wrap(base + d) for d in range(-1, ROWS + 1)]
        kept = {}

        def load(ref, lead, r, c, j):
            key = (ref is coef, lead, r, c % chunks, j)
            if key not in kept:
                kept[key] = piece(ref, lead, at[r + 1], c % chunks, j)
            return kept[key]

        def scaled(slot, p, r, c, j):
            u = load(src, p, r, c, j)
            return load(coef, slot, r, c, j) * u if adjoint else u

        def turned(slot, shift, p, r, c, j):
            key = ("turned", slot, p, r, c % chunks, j)
            if key not in kept:
                kept[key] = pltpu.roll(scaled(slot, p, r, c, j), shift, 0)
            return kept[key]

        for c in range(done):
            results = []
            for r in range(ROWS):
                plus, minus = {}, {}
                for j in range(cols):
                    for p in range(fields):
                        plus[p, j] = pltpu.roll(scaled(6, p, r, c, j), LANES - 1, 1)
                        minus[p, j] = pltpu.roll(scaled(5, p, r, c, j), 1, 1)
                for j in range(cols):
                    for p in range(fields):
                        u, xp, xm = (load(src, p, r + d, c, j) for d in (0, 1, -1))
                        yp = jnp.where(last_row, turned(4, SUB - 1, p, r, c + 1, j), turned(4, SUB - 1, p, r, c, j))
                        ym = jnp.where(first_row, turned(3, 1, p, r, c - 1, j), turned(3, 1, p, r, c, j))
                        zp = jnp.where(last_lane, plus[p, (j + 1) % cols], plus[p, j])
                        zm = jnp.where(first_lane, minus[p, (j - 1) % cols], minus[p, j])
                        if adjoint:
                            xs = load(coef, 2, r + 1, c, j) * xp + load(coef, 1, r - 1, c, j) * xm
                            ys, zs = yp + ym, zp + zm
                        else:
                            xs = load(coef, 1, r, c, j) * xp + load(coef, 2, r, c, j) * xm
                            ys = load(coef, 3, r, c, j) * yp + load(coef, 4, r, c, j) * ym
                            zs = load(coef, 5, r, c, j) * zp + load(coef, 6, r, c, j) * zm
                        value = (load(coef, 0, r, c, j) * u + xs) + (ys + zs)
                        results.append((p, at[r + 1], c, j, value))
            for result in results:
                write(*result)
        return carry

    lax.fori_loop(0, (stop - first) // ROWS, body, None)


def run_steps(coef, states, out, adjoint, weight=None):
    x, tile_rows = out.shape[1], out.shape[2]
    for step in range(STEPS):
        src, dst = states[step % 2], states[(step + 1) % 2]
        last = step == STEPS - 1

        def write(p, i, c, j, value):
            at = (pl.ds(SUB * c, SUB), pl.ds(LANES * j, LANES))
            if last:
                out[p, i, *at] = value if weight is None else weight[i, *at] * value
            else:
                dst[p, i, *at] = value

        done = (tile_rows if last else src.shape[2]) // SUB
        reach = STEPS - 1 - step
        sweep(coef, src, -reach, x + reach, adjoint, done, write)


def flat_tiles(sources):
    return [ref.at[n] for ref in sources for n in range(ref.shape[0])]


def pack_y_kernel(fields_in, packs, scalars, *refs):
    sources, outs, (buffers, sems) = refs[:fields_in], refs[fields_in:-2], refs[-2:]
    tiles = flat_tiles(sources)
    starts = pack_starts(packs, tiles[0].shape[1], scalars[0])
    copies = Copies(sems)
    for f, tile in enumerate(tiles):
        for n, (start, _) in enumerate(starts):
            copies.start(tile.at[:, pl.ds(start, SUB)], buffers.at[n, f])
    for f in range(len(tiles)):
        for n, (_, last) in enumerate(starts):
            copies.open[f * len(starts) + n].wait()
            write_packs(f, n, lambda i: buffers[n, f, i], last, (None, None) + outs)


def pack_x_kernel(fields_in, *refs):
    sources, (low, high, sems) = refs[:fields_in], refs[fields_in:]
    copies = Copies(sems)
    for f, tile in enumerate(flat_tiles(sources)):
        copies.start(tile.at[pl.ds(0, STEPS)], low.at[f])
        copies.start(tile.at[pl.ds(tile.shape[0] - STEPS, STEPS)], high.at[f])
    copies.wait()


def first_kernel(count, scalars, diffusivity, velocity, probes, weight, *refs):
    side = scalars[0]
    received, coef, out = refs[:count], refs[count], refs[count + 1]
    strips, (state, other, sems) = refs[count + 2 : -3], refs[-3:]
    copies = Copies(sems)
    tiles = [diffusivity.at[0]] + [velocity.at[d] for d in range(3)]
    slots = [coef.at[s] for s in (0, 1, 3, 5)]
    for p in range(probes.shape[0]):
        tiles.append(probes.at[p])
        slots.append(state.at[p])
    for f, (tile, slot) in enumerate(zip(tiles, slots)):
        start_widening(copies, slot, tile, f, received)
    for f, slot in enumerate(slots):
        widen_rows(slot, f, received, side)
    copies.wait()
    coefficient_rows(coef)
    run_steps(coef, (state, other), out, False, weight)
    write_strips(out, strips, side)


def next_kernel(count, adjoint, scalars, coef, tile, *refs):
    side = scalars[0]
    weight = None if adjoint else refs[0]
    refs = refs if adjoint else refs[1:]
    received, out = refs[:count], refs[count]
    strips, (state, other, sems) = refs[count + 1 : -3], refs[-3:]
    fields = tile.shape[0]
    copies = Copies(sems)
    for p in range(fields):
        start_widening(copies, state.at[p], tile.at[p], p, received)
    for p in range(fields):
        widen_rows(state.at[p], p, received, side)
    copies.wait()
    run_steps(coef, (state, other), out, adjoint, weight)
    if strips:
        write_strips(out, strips, side)


def dots_pairs(group, slots):
    return [(s, a, b) for s in range(slots) for a in range(group) for b in range(group) if s or b <= a]


def dots_kernel(scalars, second, *refs):
    passed, out = refs[:-1], refs[-1]
    group, rows, y, z = second.shape
    chunks, cols = y // SUB, z // LANES
    pairs = dots_pairs(group, len(passed))

    def body(i, sums):
        sums = list(sums)
        for c in range(chunks):
            for j in range(cols):
                at = (pl.ds(SUB * c, SUB), pl.ds(LANES * j, LANES))
                mine = [passed[0][a, i, *at] for a in range(group)]
                then = [second[a, i, *at] for a in range(group)]
                other = {(s, b): passed[s][b, i, *at] for s in range(1, len(passed)) for b in range(group)}
                for n, (s, a, b) in enumerate(pairs):
                    value = other[s, b] if s else mine[b]
                    sums[2 * n] = sums[2 * n] + mine[a] * value
                    sums[2 * n + 1] = sums[2 * n + 1] + then[a] * value
        return tuple(sums)

    zero = jnp.zeros((SUB, LANES), jnp.float32)
    sums = lax.fori_loop(0, rows, body, (zero,) * (2 * len(pairs)))
    me = scalars[1]
    count = out.shape[0]
    row = lax.broadcasted_iota(jnp.int32, out.shape, 0)
    lane = lax.broadcasted_iota(jnp.int32, out.shape, 1)
    total = jnp.zeros(out.shape, jnp.float32)
    for n, (s, a, b) in enumerate(pairs):
        for k in range(2):
            value = jnp.sum(jnp.sum(sums[2 * n + k], axis=0, keepdims=True), axis=1, keepdims=True)
            i, j = me * group + a, (me - s) * group + b
            here = (row == i) & (lane == j + k * count) | (row == j) & (lane == i + k * count)
            total = total + jnp.where(here & (me >= s), value, 0.0)
    out[...] = total


def finish_kernel(scale, scalars, inner, *refs):
    images, (basis, projected, held, sems) = refs[:-4], refs[-4:]
    group, x, y, z = held.shape
    count = inner.shape[0]
    me = scalars[1]
    row = lax.broadcasted_iota(jnp.int32, inner.shape, 0)
    lane = lax.broadcasted_iota(jnp.int32, inner.shape, 1)
    base = 2 * count
    work = jnp.where(lane == row + base, 1.0, inner[...] * scale)
    for k in range(count):
        column = jnp.broadcast_to(work[:, k : k + 1], inner.shape)
        pivot = jnp.broadcast_to(column[k : k + 1], inner.shape)
        line = jnp.broadcast_to(work[k : k + 1], inner.shape)
        work = work - jnp.where(row > k, column / pivot, 0.0) * line
    pivots = jnp.sum(jnp.where(lane == row, work, 0.0), axis=1, keepdims=True)
    work = work * (1.0 / jnp.sqrt(pivots))

    factors = []
    for a in range(group):
        factors.append([])
        for s in range(len(images)):
            for b in range(group):
                here = (row == me * group + a) & (lane == base + (me - s) * group + b) & (me >= s)
                value = jnp.sum(jnp.where(here, work, 0.0), axis=0, keepdims=True)
                value = jnp.sum(value, axis=1, keepdims=True)
                factors[a].append(jnp.broadcast_to(value, (SUB, LANES)))

    def body(i, carry):
        for c in range(y // SUB):
            for j in range(z // LANES):
                at = (pl.ds(SUB * c, SUB), pl.ds(LANES * j, LANES))
                values = [image[b, i, *at] for image in images for b in range(group)]
                for a in range(group):
                    terms = [factor * value for factor, value in zip(factors[a], values)]
                    while len(terms) > 1:
                        terms = [sum(terms[n : n + 2][1:], terms[n]) for n in range(0, len(terms), 2)]
                    held[a, i, *at] = terms[0]
        return carry

    copies = Copies(sems)
    for start in range(0, x, SUB):
        lax.fori_loop(start, start + SUB, body, None)
        for a in range(group):
            copies.start(held.at[a, pl.ds(start, SUB)], basis.at[a, pl.ds(start, SUB)])

    left = jnp.where((lane >= count) & (lane < base), work, 0.0)
    right = jnp.where((lane >= count) & (lane < base), pltpu.roll(work, LANES - count, 1), 0.0)
    projected[...] = lax.dot_general(
        left,
        right,
        (((1,), (1,)), ((), ())),
        precision=lax.Precision.HIGHEST,
        preferred_element_type=jnp.float32,
    )
    copies.wait()


def all_sum(value):
    for axis in ("sx", "sy", "probe"):
        devices = lax.axis_size(axis)
        if devices & (devices - 1):
            value = lax.psum(value, axis)
            continue
        move = lambda bits: lax.ppermute(value, axis, [(i, i ^ bits) for i in range(devices)])
        bit = 1
        while bit < devices:
            if 4 * bit <= devices:
                value = (value + move(bit)) + (move(2 * bit) + move(3 * bit))
                bit *= 4
            else:
                value = value + move(bit)
                bit *= 2
    return value


def shards(probes, velocity, diffusivity, obs_weight):
    group, x, y, z = probes.shape
    groups = lax.axis_size("probe")
    count = group * groups
    ncells = x * y * z * lax.axis_size("sx") * lax.axis_size("sy")
    both = lax.axis_size("sy") != 2
    side, mine = lax.axis_index("sy"), lax.axis_index("probe")

    where = jnp.stack([side, mine]).astype(jnp.int32)
    wide = (x + 2 * STEPS, y + 2 * STEPS, z)
    tile = f32(group, x, y, z)
    strips2 = strip_shapes(group, x, y, z, both, not both)
    fields = [diffusivity[None], velocity, probes]
    total = 4 + group

    def scratch(copies):
        return [
            pltpu.VMEM((group,) + wide, jnp.float32),
            pltpu.VMEM((group,) + wide, jnp.float32),
            pltpu.SemaphoreType.DMA((copies,)),
        ]

    packs = 2 if both else 1

    def pack(sources, joined, mib):
        number = sum(a.shape[0] for a in sources)
        outs = strip_shapes(number, x, y, z, both, joined)
        in_y = kernel_call(
            functools.partial(pack_y_kernel, len(sources), packs),
            outs[2:],
            [pltpu.VMEM((packs, number, x, SUB, z), jnp.float32), pltpu.SemaphoreType.DMA((number * packs,))],
            [where] + sources,
            2.0,
            mib,
            anywhere=range(1, len(sources) + 1),
        )
        in_x = kernel_call(
            functools.partial(pack_x_kernel, len(sources)),
            outs[:2],
            [pltpu.SemaphoreType.DMA((2 * number,))],
            sources,
            2.0,
            min(mib, 12),
            anywhere=range(len(sources)),
            scalars=False,
        )
        return list(in_x) + list(in_y)

    def right(value, hops):
        return lax.ppermute(value, "probe", [(i, i + hops) for i in range(groups - hops)])

    strips = pack(fields, False, 56)
    strips[2], leaving = lax.optimization_barrier((strips[2], probes))
    next_probes = right(leaving, 1)
    received = exchange(strips)
    coef, halfway, *strips = kernel_call(
        functools.partial(first_kernel, len(received)),
        [f32(7, *wide), tile] + strips2,
        scratch(3 * total),
        [where] + fields + [obs_weight] + received,
        4.0,
        14,
        anywhere=(1, 2, 3, 5, 6),
    )

    def model(field, received, adjoint, last=False, micros=8.0):
        ins = [where, coef, field] + ([] if adjoint else [obs_weight])
        return kernel_call(
            functools.partial(next_kernel, len(received), adjoint),
            [tile] + ([] if last else strips2),
            scratch(3 * group),
            ins + received,
            micros,
            14,
            anywhere=(2, len(ins), len(ins) + 1) if both else (2,),
        )

    next_probes, halfway = lax.optimization_barrier((next_probes, halfway))
    strips_next = pack([next_probes], not both, 8)
    images, *strips = model(halfway, exchange(strips), True)
    far = [right(images, hops) for hops in range(3, groups)]

    received, _ = lax.optimization_barrier((exchange(strips_next), images))
    half_next, *strips_next = model(next_probes, received, False)
    strips, half_next = lax.optimization_barrier((strips, half_next))
    (images_next,) = model(half_next, exchange(strips_next), True, True)
    shifting, far = lax.optimization_barrier((images_next, far))
    passed = [images, images_next, right(shifting, 1)] + far

    received = exchange(strips, after=images_next)
    halfway, *strips = model(images, received, False, micros=8.0)
    (second,) = model(halfway, exchange(strips), True, True, micros=8.0)

    (partial,) = kernel_call(
        dots_kernel,
        [f32(count, LANES)],
        [],
        [where, second] + passed,
        4.0,
        14,
    )
    basis, projected = kernel_call(
        functools.partial(finish_kernel, 1.0 / ncells),
        [tile, f32(count, count)],
        [pltpu.VMEM((group, x, y, z), jnp.float32), pltpu.SemaphoreType.DMA((group * (x // SUB),))],
        [where, all_sum(partial)] + passed,
        5.0,
        14,
        outs_anywhere=(0,),
    )
    return (basis, projected)


def solution(mesh):
    return jax.shard_map(
        shards,
        mesh=mesh,
        in_specs=(
            P("probe", "sx", "sy", None),
            P(None, "sx", "sy", None),
            P("sx", "sy", None),
            P("sx", "sy", None),
        ),
        out_specs=(P("probe", "sx", "sy", None), P()),
        check_vma=False,
    )
```
